32 devices in a mesh: gx: 8 (over z, y), gy: 4 (over x, core).
Axes of the slice: x: 2, y: 2, z: 4, core: 2. Of those that a mesh axis runs over, the one named last changes fastest.
Arguments:
- phase: float32 [128, 128, 256], P('gx', 'gy'), may hold values from -1 to 1
- solute: float32 [128, 128, 256], P('gx', 'gy'), may hold values from -1 to 1
- macro_temp: float32 [32, 32, 64], P('gx', None, 'gy'), may hold values from -1 to 1
Outputs:
- phase_out: float32 [128, 128, 256], P('gx', 'gy')
- solute_out: float32 [128, 128, 256], P('gx', 'gy')
- latent_heat: float32 [32, 32, 64], P('gx', None, 'gy')
The draws below stay inside these ranges and needn't reach their ends.
All inputs are finite; a program needn't handle non-finite values.
Results may differ from the reference program's by a relative error of at most 0.0001.
Values sent between devices are 32-bit elements; how exact they have to be, the bound alone decides.
No kernel may reach another device: no remote copies, remote signals or barrier semaphores. Data moves between devices by JAX's collectives and lax.ppermute only.
A program may use at most 64 MiB of HBM per device.

```python
import jax
import jax.numpy as jnp

NZ = 256
SUBSTEPS = 2
NX = 128
NY = 128
MX = 32
MY = 32
MZ = 64


def block_levels(stream_key, extent, shards, smallest, high):
    loudness, own = 1.0, jax.random.fold_in(stream_key, 6)
    for axis_at, parts in shards:
        draws = jnp.exp(jax.random.uniform(jax.random.fold_in(own, axis_at), (parts,), jnp.float32, smallest / len(shards), high / len(shards)))
        loudness = loudness * jnp.repeat(draws, extent[axis_at] // parts).reshape([-1 if axis == axis_at else 1 for axis in range(len(extent))])
    return loudness


def setup_inputs(seed: int = 0) -> dict:
    keys = jax.random.split(jax.random.key(seed), 4)
    phase = jnp.clip(jax.random.uniform(keys[0], (NX, NY, NZ), jnp.float32, -1.0, 1.0) * block_levels(keys[0], (NX, NY, NZ), ((0, 8), (1, 4)), -0.4, 0.0), -1.0, 1.0)
    solute = jnp.clip(jax.random.uniform(keys[1], (NX, NY, NZ), jnp.float32, -1.0, 1.0) * block_levels(keys[1], (NX, NY, NZ), ((0, 8), (1, 4)), -0.4, 0.0), -1.0, 1.0)
    macro_temp = jnp.clip(jax.random.uniform(keys[2], (MX, MY, MZ), jnp.float32, -1.0, 1.0) * block_levels(keys[2], (MX, MY, MZ), ((0, 8), (2, 4)), -0.4, 0.0), -1.0, 1.0)
    return dict(phase=phase, solute=solute, macro_temp=macro_temp)


time_step = 0.1
anisotropy = 0.3
coupling = 2.0
rejection = 0.5


def stretch(coarse, axis, count, periodic):
    size = coarse.shape[axis]
    fine = jnp.arange(count, dtype=jnp.int32)
    lower = jnp.floor_divide(2 * fine - 3, 8).astype(jnp.int32)
    frac = ((2 * fine - 3) - 8 * lower).astype(jnp.float32) / 8.0
    if periodic:
        first = (lower % size).astype(jnp.int32)
        second = ((lower + 1) % size).astype(jnp.int32)
    else:
        first = jnp.clip(lower, 0, size - 1).astype(jnp.int32)
        second = jnp.clip(lower + 1, 0, size - 1).astype(jnp.int32)
    shape = [1, 1, 1]
    shape[axis] = count
    frac = frac.reshape(shape)
    return (1.0 - frac) * jnp.take(coarse, first, axis=axis) + frac * jnp.take(coarse, second, axis=axis)


def divergence(pad_field, with_aniso):
    grid = jnp.pad(pad_field, ((0, 0), (0, 0), (2, 2)), mode="edge")
    grad_x = 0.5 * (grid[2:, 1:-1, 1:-1] - grid[:-2, 1:-1, 1:-1])
    grad_y = 0.5 * (grid[1:-1, 2:, 1:-1] - grid[1:-1, :-2, 1:-1])
    grad_z = 0.5 * (grid[1:-1, 1:-1, 2:] - grid[1:-1, 1:-1, :-2])
    if with_aniso:
        sq_x = grad_x * grad_x
        sq_y = grad_y * grad_y
        planar = sq_x + sq_y + 1.0
        factor = 1.0 + anisotropy * (sq_x * sq_x - 6.0 * sq_x * sq_y + sq_y * sq_y) / (planar * planar)
        stiff = factor * factor
        grad_x = stiff * grad_x
        grad_y = stiff * grad_y
        grad_z = stiff * grad_z
    total = 0.5 * (grad_x[2:, 1:-1, 1:-1] - grad_x[:-2, 1:-1, 1:-1])
    total = total + 0.5 * (grad_y[1:-1, 2:, 1:-1] - grad_y[1:-1, :-2, 1:-1])
    total = total + 0.5 * (grad_z[1:-1, 1:-1, 2:] - grad_z[1:-1, 1:-1, :-2])
    return total


def substep(phase_pad, solute_pad, theta):
    old = phase_pad[2:-2, 2:-2, :]
    conc = solute_pad[2:-2, 2:-2, :]
    square = 1.0 - old * old
    drive = divergence(phase_pad, True) + old - old * old * old - coupling * square * square * (theta + conc)
    new_phase = old + time_step * drive
    new_solute = conc + time_step * divergence(solute_pad, False) + rejection * (new_phase - old)
    return new_phase, new_solute


def reference(phase, solute, macro_temp):
    theta = stretch(macro_temp, 0, NX, True)
    theta = stretch(theta, 1, NY, True)
    theta = stretch(theta, 2, NZ, False)
    current_phase, current_solute = phase, solute
    for step in range(SUBSTEPS):
        phase_pad = jnp.pad(current_phase, ((2, 2), (2, 2), (0, 0)), mode="wrap")
        solute_pad = jnp.pad(current_solute, ((2, 2), (2, 2), (0, 0)), mode="wrap")
        current_phase, current_solute = substep(phase_pad, solute_pad, theta)
    change = 0.5 * (current_phase - phase)
    latent = change.reshape(MX, 4, MY, 4, MZ, 4).mean(axis=(1, 3, 5))
    return current_phase, current_solute, latent
```

```python
import functools

import jax
import jax.numpy as jnp
from jax import lax
from jax.experimental import pallas as pl
from jax.experimental.pallas import tpu as pltpu
from jax.sharding import PartitionSpec as P

time_step = 0.1
anisotropy = 0.3
coupling = 2.0
rejection = 0.5

F32 = jnp.float32
HIGHEST = lax.Precision.HIGHEST
HALO = 4
ROWS = 8
LANES = 128
VMEM_LIMIT = 40 * 1024 * 1024


def vmem():
    return pl.BlockSpec(memory_space=pltpu.VMEM)


def hbm():
    return pl.BlockSpec(memory_space=pl.ANY)


def pairs(count, first):
    forward = [((first + k) % count, (first + k + 1) % count) for k in range(0, count, 2)]
    return forward + [(b, a) for a, b in forward]


def flips(me):
    odd = lax.rem(me, 2)
    return me, me + 1 - 2 * odd, lax.rem(me + 2, 4), 3 - me


def row_ids(shape):
    return lax.broadcasted_iota(jnp.int32, shape, len(shape) - 2)


def lane_ids(shape):
    return lax.broadcasted_iota(jnp.int32, shape, len(shape) - 1)


def pack_kernel(phase, solute, macro, face_a, face_b, side_a, side_b, table, low, high, sems):
    size_x, size_y, _ = phase.shape
    odd_x = lax.rem(lax.axis_index("gx"), 2)
    odd_y = lax.rem(lax.axis_index("gy"), 2)
    start_a = (1 - odd_x) * (size_x - HALO)
    start_b = odd_x * (size_x - HALO)
    copies = []
    for field, ref in enumerate((phase, solute)):
        copies.append((ref.at[:, pl.ds(0, ROWS), :], low.at[field]))
        copies.append((ref.at[:, pl.ds(size_y - ROWS, ROWS), :], high.at[field]))
        copies.append((ref.at[pl.ds(start_a, HALO)], face_a.at[field]))
        copies.append((ref.at[pl.ds(start_b, HALO)], face_b.at[field]))
    copies = [pltpu.make_async_copy(s, d, sems.at[n]) for n, (s, d) in enumerate(copies)]
    for copy in copies:
        copy.start()
    coarse_x, coarse_y, coarse_z = macro.shape
    wide = jnp.concatenate([macro[k] for k in range(coarse_x)], axis=1)
    wide = jnp.pad(wide, ((0, 0), (0, LANES - coarse_x * coarse_z)))
    table[...] = wide.reshape(table.shape)
    for copy in copies:
        copy.wait()
    shape = (size_x, ROWS, phase.shape[2])
    top = row_ids(shape) < HALO
    low_side = jnp.where(top, low[0], pltpu.roll(low[1], HALO, 1))
    high_side = jnp.where(top, pltpu.roll(high[1], HALO, 1), high[0])
    even = odd_y == 0
    side_a[...] = jnp.where(even, high_side, low_side)
    side_b[...] = jnp.where(even, low_side, high_side)


def pack(phase, solute, macro):
    size_x, size_y, size_z = phase.shape
    coarse_x, coarse_y, coarse_z = macro.shape
    face = jax.ShapeDtypeStruct((2, HALO, size_y, size_z), F32)
    side = jax.ShapeDtypeStruct((size_x, ROWS, size_z), F32)
    table = jax.ShapeDtypeStruct((coarse_y // ROWS, ROWS, LANES), F32)
    return pl.pallas_call(
        pack_kernel,
        out_shape=(face, face, side, side, table),
        in_specs=[hbm(), hbm(), vmem()],
        out_specs=[vmem()] * 5,
        scratch_shapes=[
            pltpu.VMEM((2, size_x, ROWS, size_z), F32),
            pltpu.VMEM((2, size_x, ROWS, size_z), F32),
            pltpu.SemaphoreType.DMA((8,)),
        ],
        compiler_params=pltpu.CompilerParams(vmem_limit_bytes=VMEM_LIMIT),
        cost_estimate=pl.CostEstimate(flops=10**5, bytes_accessed=2 * 10**6, transcendentals=0),
        name="pack",
    )(phase, solute, macro)


def corner_kernel(count, coarse_x, coarse_z, side_a, side_b, *rest):
    tables, (corner_a, corner_b, coarse) = rest[:count], rest[count:]
    size_x = side_a.shape[0]
    me = lax.axis_index("gy")
    even_x = lax.rem(lax.axis_index("gx"), 2) == 0
    even_y = lax.rem(me, 2) == 0
    groups = tables[0].shape[0]
    ranks = lax.axis_size("gy")
    if count == 4:
        owners = flips(me)
        pick = lambda s, g: tables[s][g]
    else:
        owners = tuple(range(ranks))
        groups = tables[0].shape[1]
        pick = lambda s, g: tables[0][s, g]
    lane = lane_ids((ROWS, LANES))
    parts = []
    for k in range(coarse_x):
        for g in range(3):
            group = lax.rem(me + g - 1 + groups, groups)
            total = jnp.zeros((ROWS, LANES), F32)
            for s, owner in enumerate(owners):
                at = owner * coarse_z
                shift = lax.rem(at - k * coarse_z + LANES, LANES)
                moved = pltpu.roll(pick(s, group), shift, 1)
                total = total + jnp.where((lane >= at) & (lane < at + coarse_z), moved, 0.0)
            coarse[k, pl.ds(g * ROWS, ROWS), :] = total
            parts.append(total)
    for corner, top_side in ((corner_a, even_x), (corner_b, jnp.logical_not(even_x))):
        layer = lambda ref, d: ref[jnp.where(top_side, size_x - d, d - 1)]
        row = row_ids(side_a.shape[1:])
        for n, keep in ((0, 5), (1, 2)):
            def one(d, n=n):
                first, second = layer(side_a, d), layer(side_b, d)
                return jnp.where(even_y, second, first) if n == 0 else jnp.where(even_y, first, second)

            third = pltpu.roll(one(3), 6 if n == 0 else 2, 0)
            corner[2 * n] = one(1)
            corner[2 * n + 1] = jnp.where(row == keep, third, one(2))
        edge = [jnp.where(top_side, parts[3 * (coarse_x - 1) + g], parts[g]) for g in range(3)]
        corner[4] = jnp.concatenate([edge[0] + pltpu.roll(edge[1], LANES // 2, 1), edge[2]], axis=1)


def corners(side_a, side_b, tables, coarse_x, coarse_z):
    size_x, _, size_z = side_a.shape
    corner = jax.ShapeDtypeStruct((5, ROWS, size_z), F32)
    coarse = jax.ShapeDtypeStruct((coarse_x, 3 * ROWS, LANES), F32)
    return pl.pallas_call(
        functools.partial(corner_kernel, len(tables), coarse_x, coarse_z),
        out_shape=(corner, corner, coarse),
        in_specs=[vmem()] * (2 + len(tables)),
        out_specs=[vmem()] * 3,
        compiler_params=pltpu.CompilerParams(vmem_limit_bytes=VMEM_LIMIT),
        cost_estimate=pl.CostEstimate(flops=10**5, bytes_accessed=4 * 10**5, transcendentals=0),
        name="corners",
    )(side_a, side_b, *tables)


def interpolation(fine, count, offset):
    lower = (2 * fine - 3 + 8 * 8) // 8 - 8
    frac = (2 * fine - 3 - 8 * lower).astype(F32) / 8.0
    tick = lane_ids(fine.shape)
    first = jnp.clip(lower + offset, 0, count - 1)
    second = jnp.clip(lower + 1 + offset, 0, count - 1)
    return jnp.where(tick == first, 1.0 - frac, 0.0) + jnp.where(tick == second, frac, 0.0)


def step_kernel(
    phase, solute, face_a, face_b, side_a, side_b, corner_a, corner_b, coarse,
    phase_out, solute_out, latent,
    p0, c0, p1, c1, gx, div, theta, weights, fan, sems,
):
    size_x, size_y, size_z = phase.shape
    coarse_x = coarse.shape[0]
    rows = size_y + 2 * HALO
    even_x = lax.rem(lax.axis_index("gx"), 2) == 0
    even_y = lax.rem(lax.axis_index("gy"), 2) == 0
    spot_a = jnp.where(even_x, size_x + HALO, 0)
    spot_b = jnp.where(even_x, 0, size_x + HALO)
    copies = []
    for n, (source, face) in enumerate(((phase, 0), (solute, 1))):
        field = (p0, c0)[n]
        own = field.at[pl.ds(HALO, size_x), pl.ds(0, size_y), :]
        copies.append((source, own))
        copies.append((face_a.at[face], field.at[pl.ds(spot_a, HALO), pl.ds(0, size_y), :]))
        copies.append((face_b.at[face], field.at[pl.ds(spot_b, HALO), pl.ds(0, size_y), :]))
    copies = [pltpu.make_async_copy(s, d, sems.at[n]) for n, (s, d) in enumerate(copies)]
    for copy in copies:
        copy.start()

    row = row_ids((ROWS, size_z))
    top = row < HALO

    def put(at, low, high):
        p0[at, pl.ds(size_y, ROWS), :] = jnp.where(top, high, low)
        c0[at, pl.ds(size_y, ROWS), :] = pltpu.roll(jnp.where(top, low, high), HALO, 0)

    for k in range(size_x):
        first, second = side_a[k], side_b[k]
        put(k + HALO, jnp.where(even_y, second, first), jnp.where(even_y, first, second))
    for above in (False, True):
        use_a = even_x if above else jnp.logical_not(even_x)
        tile = [jnp.where(use_a, corner_a[k], corner_b[k]) for k in range(5)]
        place = lambda d: size_x + HALO - 1 + d if above else HALO - d
        put(place(1), tile[0], tile[2])
        put(place(2), tile[1], tile[3])
        put(place(3), pltpu.roll(tile[1], 2, 0), pltpu.roll(tile[3], 6, 0))
        put(place(4), jnp.zeros_like(tile[0]), jnp.zeros_like(tile[0]))
        edge = coarse_x + 1 if above else 0
        weights[edge, pl.ds(0, ROWS), :] = tile[4][:, :LANES]
        weights[edge, pl.ds(ROWS, ROWS), :] = pltpu.roll(tile[4][:, :LANES], LANES // 2, 1)
        weights[edge, pl.ds(2 * ROWS, ROWS), :] = tile[4][:, LANES:]
    weights[pl.ds(1, coarse_x)] = coarse[...]

    half = LANES // 2
    fine_z = lax.broadcasted_iota(jnp.int32, (size_z, half), 0)
    along_z = interpolation(fine_z, size_z // 4, 0)
    fine_y = lax.broadcasted_iota(jnp.int32, (rows, 3 * ROWS), 0)
    fine_y = jnp.where(fine_y >= size_y + HALO, fine_y - rows, fine_y)
    along_y = interpolation(fine_y, 3 * ROWS, ROWS)
    block = weights[...].reshape((coarse_x + 2) * 3 * ROWS, LANES)[:, :half]
    deep = lax.dot_general(block, along_z, (((1,), (1,)), ((), ())), precision=HIGHEST, preferred_element_type=F32)
    for k in range(coarse_x + 2):
        fan[k] = lax.dot_general(
            along_y, deep[k * 3 * ROWS : (k + 1) * 3 * ROWS], (((1,), (0,)), ((), ())), precision=HIGHEST,
            preferred_element_type=F32,
        )
    for x in range(-2, size_x + 2):
        lower = (2 * x - 3) // 8
        frac = (2 * x - 3 - 8 * lower) / 8.0
        theta[x + 2] = (1.0 - frac) * fan[lower + 1] + frac * fan[lower + 2]

    for copy in copies:
        copy.wait()

    lane = lane_ids((rows, size_z))

    def turn(value, by, axis):
        return pltpu.roll(value, by % value.shape[axis], axis)

    def stiff_flux(old, shift, at):
        here = old[at + shift]
        along_x = old[at + shift + 1] - old[at + shift - 1]
        along_y = turn(here, -1, 0) - turn(here, 1, 0)
        after = jnp.where(lane == size_z - 1, here, turn(here, -1, 1))
        before = jnp.where(lane == 0, here, turn(here, 1, 1))
        along_z = after - before
        sq_x = along_x * along_x
        sq_y = along_y * along_y
        both = sq_x + sq_y
        inverse = 1.0 / (both + 4.0)
        factor = 1.0 + anisotropy * (both * both - 8.0 * (sq_x * sq_y)) * (inverse * inverse)
        stiff = (0.25 * time_step) * (factor * factor)
        return stiff * along_x, stiff * along_y, stiff * along_z

    def flux_step(old, shift, first, last):
        def run(n, _):
            flux_x, flux_y, flux_z = stiff_flux(old, shift + first, n)
            gx[n] = flux_x
            after = jnp.where(lane == size_z - 1, 0.0, turn(flux_z, -1, 1))
            before = jnp.where(lane == 0, 0.0, turn(flux_z, 1, 1))
            div[n] = (turn(flux_y, -1, 0) - turn(flux_y, 1, 0)) + (after - before)
            return 0

        lax.fori_loop(0, last - first, run, 0)

    def update(old, conc, n, drop):
        here = old[n + 2]
        centre = conc[n + 2]
        total = (gx[n + 2] - gx[n]) + div[n + 1]
        square = 1.0 - here * here
        drive = square * (here - (coupling * square) * (theta[n + drop] + centre))
        delta = total + time_step * drive
        laplace = conc[n + 4] + conc[n] + turn(centre, -2, 0) + turn(centre, 2, 0)
        ahead = jnp.where(lane >= size_z - 2, jnp.broadcast_to(centre[:, size_z - 1 :], centre.shape), turn(centre, -2, 1))
        behind = jnp.where(lane < 2, jnp.broadcast_to(centre[:, :1], centre.shape), turn(centre, 2, 1))
        laplace = laplace + ahead + behind - 6.0 * centre
        new_conc = centre + (0.25 * time_step) * laplace + rejection * delta
        return here + delta, new_conc

    flux_step(p0, HALO, -3, size_x + 3)

    def first_update(n, _):
        p1[n], c1[n] = update(p0, c0, n, 0)
        return 0

    lax.fori_loop(0, size_x + 4, first_update, 0)
    flux_step(p1, 2, -1, size_x + 1)

    def second_update(x, _):
        new_phase, new_conc = update(p1, c1, x, 2)
        phase_out[x] = new_phase[:size_y]
        solute_out[x] = new_conc[:size_y]
        return 0

    lax.fori_loop(0, size_x, second_update, 0)

    per = size_y // 4
    pool_y = (row_ids((per, size_y)) == lane_ids((per, size_y)) // 4).astype(F32)
    pool_z = (row_ids((size_z, LANES)) // 4 == lane_ids((size_z, LANES))).astype(F32)
    for k in range(coarse_x):
        change = jnp.zeros((size_y, size_z), F32)
        for x in range(4 * k, 4 * k + 4):
            change = change + (phase_out[x] - p0[x + HALO, pl.ds(0, size_y), :])
        change = jnp.dot(change, pool_z, precision=HIGHEST, preferred_element_type=F32)
        latent[k] = (0.5 / 64.0) * jnp.dot(pool_y, change, precision=HIGHEST, preferred_element_type=F32)


def steps(phase, solute, face_a, face_b, side_a, side_b, corner_a, corner_b, coarse):
    size_x, size_y, size_z = phase.shape
    coarse_x = coarse.shape[0]
    rows = size_y + 2 * HALO
    out = jax.ShapeDtypeStruct(phase.shape, F32)
    slabs = lambda count: pltpu.VMEM((count, rows, size_z), F32)
    return pl.pallas_call(
        step_kernel,
        out_shape=(out, out, jax.ShapeDtypeStruct((coarse_x, size_y // 4, LANES), F32)),
        in_specs=[hbm(), hbm()] + [vmem()] * 7,
        out_specs=[vmem()] * 3,
        scratch_shapes=[
            slabs(size_x + 8), slabs(size_x + 8), slabs(size_x + 4), slabs(size_x + 4),
            slabs(size_x + 6), slabs(size_x + 6), slabs(size_x + 4),
            pltpu.VMEM((coarse_x + 2, 3 * ROWS, LANES), F32),
            slabs(coarse_x + 2),
            pltpu.SemaphoreType.DMA((6,)),
        ],
        compiler_params=pltpu.CompilerParams(vmem_limit_bytes=VMEM_LIMIT),
        cost_estimate=pl.CostEstimate(flops=4 * 10**7, bytes_accessed=3 * 10**6, transcendentals=0),
        name="substeps",
    )(phase, solute, face_a, face_b, side_a, side_b, corner_a, corner_b, coarse)


def owner_kernel(coarse_z, mine, core, chip, far, out):
    me = lax.axis_index("gy")
    per = mine.shape[1]
    for source, ref in zip(flips(me), (mine, core, chip, far)):
        for k in range(mine.shape[0]):
            moved = pltpu.roll(ref[k], lax.rem(LANES - me * coarse_z, LANES), 1)
            out[k, pl.ds(pl.multiple_of(source * per, per), per), :] = moved[:, :coarse_z]


def owner(parts, coarse_y, coarse_z):
    coarse_x = parts[0].shape[0]
    return pl.pallas_call(
        functools.partial(owner_kernel, coarse_z),
        out_shape=jax.ShapeDtypeStruct((coarse_x, coarse_y, coarse_z), F32),
        in_specs=[vmem()] * 4,
        out_specs=vmem(),
        name="owner",
    )(*parts)


def body(phase, solute, macro_temp):
    count_x, count_y = lax.axis_size("gx"), lax.axis_size("gy")
    coarse_x, coarse_y, coarse_z = macro_temp.shape
    swap = lambda value, axis, table: lax.ppermute(value, axis, table)
    near_x, far_x = pairs(count_x, 0), pairs(count_x, 1)
    near_y, far_y = pairs(count_y, 0), pairs(count_y, 1)
    across = [(k, k ^ 2) for k in range(count_y)]
    face_a, face_b, side_a, side_b, table = pack(phase, solute, macro_temp)
    face_a = swap(face_a, "gx", near_x)
    face_b = swap(face_b, "gx", far_x)
    side_a = swap(side_a, "gy", near_y)
    side_b = swap(side_b, "gy", far_y)
    if count_y == 4:
        opposite = swap(table, "gy", across)
        core = swap(table, "gy", near_y)
        tables = (table, core, opposite, swap(opposite, "gy", near_y))
    else:
        tables = (lax.all_gather(table, "gy"),)
    corner_a, corner_b, coarse = corners(side_a, side_b, tables, coarse_x, coarse_z)
    corner_a = swap(corner_a, "gx", near_x)
    corner_b = swap(corner_b, "gx", far_x)
    phase_out, solute_out, latent = steps(
        phase, solute, face_a, face_b, side_a, side_b, corner_a, corner_b, coarse
    )
    if count_y == 4:
        opposite = swap(latent, "gy", across)
        core = swap(latent, "gy", near_y)
        latent = owner((latent, core, opposite, swap(opposite, "gy", near_y)), coarse_y, coarse_z)
    else:
        split = latent[:, :, : coarse_z * count_y].reshape(coarse_x, latent.shape[1], count_y, coarse_z)
        latent = lax.all_to_all(split, "gy", split_axis=2, concat_axis=1, tiled=True)
        latent = latent.reshape(coarse_x, coarse_y, coarse_z)
    return phase_out, solute_out, latent


def solution(mesh):
    in_specs = (P("gx", "gy", None), P("gx", "gy", None), P("gx", None, "gy"))
    out_specs = (P("gx", "gy", None), P("gx", "gy", None), P("gx", None, "gy"))
    return jax.shard_map(body, mesh=mesh, in_specs=in_specs, out_specs=out_specs, check_vma=False)
```

```python
import functools

import jax
import jax.numpy as jnp
from jax import lax
from jax.experimental import pallas as pl
from jax.experimental.pallas import tpu as pltpu
from jax.sharding import PartitionSpec as P

time_step = 0.1
anisotropy = 0.3
coupling = 2.0
rejection = 0.5

F32 = jnp.float32
HIGHEST = lax.Precision.HIGHEST
HALO = 4
ROWS = 8
LANES = 128
VMEM_LIMIT = 24 * 1024 * 1024


def vmem():
    return pl.BlockSpec(memory_space=pltpu.VMEM)


def anywhere():
    return pl.BlockSpec(memory_space=pl.ANY)


def hbm():
    return pl.BlockSpec(memory_space=pltpu.HBM)


def pairs(count, first):
    forward = [((first + k) % count, (first + k + 1) % count) for k in range(0, count, 2)]
    return forward + [(b, a) for a, b in forward]


def flips(me):
    odd = lax.rem(me, 2)
    return me, me + 1 - 2 * odd, lax.rem(me + 2, 4), 3 - me


def row_ids(shape):
    return lax.broadcasted_iota(jnp.int32, shape, len(shape) - 2)


def lane_ids(shape):
    return lax.broadcasted_iota(jnp.int32, shape, len(shape) - 1)


def start_all(copies, sems):
    copies = [pltpu.make_async_copy(source, target, sems.at[n]) for n, (source, target) in enumerate(copies)]
    for copy in copies:
        copy.start()
    return copies


def wait_all(copies):
    for copy in copies:
        copy.wait()


def fold(table):
    half = table.shape[0] // 2
    return jnp.concatenate([table[:half], table[half:]], axis=1)


def unfold(tile):
    return jnp.concatenate([tile[:, :LANES], tile[:, LANES:]], axis=0)


def pack_kernel(phase, solute, macro, face_a, face_b, side_a, side_b, table, low, high, sems):
    size_x, size_y, size_z = phase.shape
    odd_x = lax.rem(lax.axis_index("gx"), 2)
    even_y = lax.rem(lax.axis_index("gy"), 2) == 0
    start_a = (1 - odd_x) * (size_x - HALO)
    start_b = odd_x * (size_x - HALO)
    copies = []
    for field, ref in enumerate((phase, solute)):
        copies.append((ref.at[pl.ds(start_a, HALO)], face_a.at[field]))
        copies.append((ref.at[pl.ds(start_b, HALO)], face_b.at[field]))
        copies.append((ref.at[:, pl.ds(0, ROWS), :], low.at[field]))
        copies.append((ref.at[:, pl.ds(size_y - ROWS, ROWS), :], high.at[field]))
    copies = start_all(copies, sems)
    wide = jnp.concatenate([macro[k] for k in range(macro.shape[0])], axis=1)
    table[...] = wide
    wait_all(copies)
    top = row_ids((size_x, ROWS, size_z)) < HALO
    low_side = jnp.where(top, low[0], pltpu.roll(low[1], HALO, 1))
    high_side = jnp.where(top, pltpu.roll(high[1], HALO, 1), high[0])
    side_a[pl.ds(0, size_x)] = jnp.where(even_y, high_side, low_side)
    side_b[pl.ds(0, size_x)] = jnp.where(even_y, low_side, high_side)
    if side_a.shape[0] > size_x:
        side_a[size_x] = fold(wide)
        side_b[size_x] = fold(wide)


def pack(phase, solute, macro, ride):
    size_x, size_y, size_z = phase.shape
    coarse_x, coarse_z, coarse_y = macro.shape
    face = jax.ShapeDtypeStruct((2, HALO, size_y, size_z), F32)
    side = jax.ShapeDtypeStruct((size_x + (1 if ride else 0), ROWS, size_z), F32)
    table = jax.ShapeDtypeStruct((coarse_z, coarse_x * coarse_y), F32)
    return pl.pallas_call(
        pack_kernel,
        out_shape=(face, face, side, side, table),
        in_specs=[hbm(), hbm(), vmem()],
        out_specs=[vmem()] * 5,
        scratch_shapes=[
            pltpu.VMEM((2, size_x, ROWS, size_z), F32),
            pltpu.VMEM((2, size_x, ROWS, size_z), F32),
            pltpu.SemaphoreType.DMA((8,)),
        ],
        compiler_params=pltpu.CompilerParams(vmem_limit_bytes=VMEM_LIMIT),
        cost_estimate=pl.CostEstimate(flops=10**5, bytes_accessed=2 * 10**6, transcendentals=0),
        name="pack",
    )(phase, solute, macro)


def corner_kernel(coarse_y, gathered, side_a, side_b, *rest):
    size_x = side_a.shape[0] - (0 if gathered else 1)
    me = lax.axis_index("gy")
    even_x = lax.rem(lax.axis_index("gx"), 2) == 0
    even_y = lax.rem(me, 2) == 0
    if gathered:
        coarse, corner_a, corner_b = rest
    else:
        mine, across, coarse, corner_a, corner_b = rest
        depth = mine.shape[0]
        near, opposite, far = flips(me)[1:]
        for source, tile in (
            (me, mine[...]),
            (opposite, across[...]),
            (near, unfold(side_a[size_x])),
            (far, unfold(side_b[size_x])),
        ):
            coarse[pl.ds(pl.multiple_of(source * depth, depth), depth), :] = tile
    block = coarse[...]
    depth, width = block.shape
    stack = LANES // coarse_y
    height = depth // stack
    row = row_ids(side_a.shape[1:])
    for corner, top_side in ((corner_a, even_x), (corner_b, jnp.logical_not(even_x))):
        for n, keep in ((0, 5), (1, 2)):
            def layer(d, n=n):
                at = jnp.where(top_side, size_x - d, d - 1)
                first, second = side_a[at], side_b[at]
                return jnp.where(even_y, second, first) if n == 0 else jnp.where(even_y, first, second)

            corner[2 * n] = layer(1)
            corner[2 * n + 1] = jnp.where(row == keep, pltpu.roll(layer(3), 6 if n == 0 else 2, 0), layer(2))
        edge = jnp.where(top_side, block[:, width - coarse_y :], block[:, :coarse_y])
        edge = jnp.concatenate([edge[q * height : (q + 1) * height] for q in range(stack)], axis=1)
        corner[pl.ds(4, height // 16)] = fold(edge).reshape(height // 16, ROWS, 2 * LANES)


def corners(side_a, side_b, tables, coarse_y, coarse_shape):
    size_z = side_a.shape[2]
    gathered = len(tables) == 1
    height = coarse_shape[0] * coarse_y // LANES
    corner = jax.ShapeDtypeStruct((4 + height // 16, ROWS, size_z), F32)
    coarse = jax.ShapeDtypeStruct(coarse_shape, F32)
    out = pl.pallas_call(
        functools.partial(corner_kernel, coarse_y, gathered),
        out_shape=(corner, corner) if gathered else (coarse, corner, corner),
        in_specs=[vmem()] * (2 + len(tables)),
        out_specs=[vmem()] * (2 if gathered else 3),
        compiler_params=pltpu.CompilerParams(vmem_limit_bytes=VMEM_LIMIT),
        cost_estimate=pl.CostEstimate(flops=10**5, bytes_accessed=4 * 10**5, transcendentals=0),
        name="corners",
    )(side_a, side_b, *tables)
    return (*tables, *out) if gathered else out


def weights(lower, frac, shape, tick):
    first, second = lower
    return jnp.where(tick == first, 1.0 - frac, 0.0) + jnp.where(tick == second, frac, 0.0)


def interpolate(block, coarse_y, size_y, size_z):
    depth, width = block.shape
    rows = size_y + 2 * HALO
    shape = (depth, size_z)
    fine = lane_ids(shape)
    lower = (2 * fine + 5) // 8 - 1
    frac = (2 * fine - 3 - 8 * lower).astype(F32) / 8.0
    ends = jnp.clip(lower, 0, depth - 1), jnp.clip(lower + 1, 0, depth - 1)
    along_z = weights(ends, frac, shape, row_ids(shape))
    deep = lax.dot_general(block, along_z, (((0,), (0,)), ((), ())), precision=HIGHEST, preferred_element_type=F32)
    shape = (rows, coarse_y)
    fine = row_ids(shape)
    fine = jnp.where(fine >= size_y + HALO, fine - rows, fine)
    local = (2 * fine + 13) // 8 - 2
    frac = (2 * fine - 3 - 8 * local).astype(F32) / 8.0
    lower = local + lax.axis_index("gy") * (size_y // 4) + coarse_y
    ends = lax.rem(lower, coarse_y), lax.rem(lower + 1, coarse_y)
    along_y = weights(ends, frac, shape, lane_ids(shape))
    return [
        jnp.dot(along_y, deep[k * coarse_y : (k + 1) * coarse_y], precision=HIGHEST, preferred_element_type=F32)
        for k in range(width // coarse_y)
    ]


def blend(x, fans):
    lower = (2 * x - 3) // 8
    frac = (2 * x - 3 - 8 * lower) / 8.0
    return (1.0 - frac) * fans[lower] + frac * fans[lower + 1]


def turn(value, by, axis):
    return pltpu.roll(value, by % value.shape[axis], axis)


def z_matrices(size_z):
    shape = (size_z, size_z)
    source, target = row_ids(shape), lane_ids(shape)
    hit = lambda at: (source == at).astype(F32)
    end = size_z - 1
    gradient = hit(jnp.minimum(target + 1, end)) - hit(jnp.maximum(target - 1, 0))
    difference = hit(target + 1) - hit(target - 1)
    laplace = hit(jnp.minimum(target + 2, end)) + hit(jnp.maximum(target - 2, 0)) - 6.0 * hit(target)
    return tuple(m.astype(jnp.bfloat16) for m in (gradient, difference, laplace))


def along(slabs, matrix):
    value = slabs.reshape(-1, slabs.shape[-1])
    coarse = value.astype(jnp.bfloat16)
    rest = (value - coarse.astype(F32)).astype(jnp.bfloat16)
    product = jnp.dot(coarse, matrix, preferred_element_type=F32) + jnp.dot(rest, matrix, preferred_element_type=F32)
    return product.reshape(slabs.shape)


def flux(before, here, after, along_z):
    along_x = after - before
    along_y = turn(here, -1, 0) - turn(here, 1, 0)
    sq_x = along_x * along_x
    sq_y = along_y * along_y
    both = sq_x + sq_y
    inverse = 1.0 / (both + 4.0)
    factor = 1.0 + anisotropy * (both * both - 8.0 * (sq_x * sq_y)) * (inverse * inverse)
    stiff = (0.25 * time_step) * (factor * factor)
    return stiff * along_x, stiff * along_y, stiff * along_z


def spread(flux_y):
    return turn(flux_y, -1, 0) - turn(flux_y, 1, 0)


def phase_change(here, conc, theta, divergence):
    square = 1.0 - here * here
    drive = square * (here - (coupling * square) * (theta + conc))
    return divergence + time_step * drive


def solute_step(conc, beyond_x, beyond_y, along_z, change):
    return conc + (0.25 * time_step) * (beyond_x + beyond_y + along_z) + rejection * change


def next_row(conc):
    return turn(conc, -2, 0) + turn(conc, 2, 0)


def pools(size_y, size_z):
    pool_y = (row_ids((size_y // 4, size_y)) == lane_ids((size_y // 4, size_y)) // 4).astype(F32)
    pool_z = (row_ids((size_z, LANES)) // 4 == lane_ids((size_z, LANES))).astype(F32)
    return pool_y, pool_z


def restrict(change, pool):
    pool_y, pool_z = pool
    change = jnp.dot(change, pool_z, precision=HIGHEST, preferred_element_type=F32)
    return (0.5 / 64.0) * jnp.dot(pool_y, change, precision=HIGHEST, preferred_element_type=F32)


KEPT = ("p0", "c0", "dz0", "cz0", "gx0", "dv0", "p1", "c1", "dz1", "cz1", "gx1", "dv1", "th")


def spans(size_x):
    ranges = dict(
        p0=(0, size_x), c0=(0, size_x), dz0=(0, size_x), cz0=(0, size_x), gx0=(1, size_x - 1), dv0=(1, size_x - 1),
        p1=(2, size_x - 2), c1=(2, size_x - 2), dz1=(2, size_x - 2), cz1=(2, size_x - 2),
        gx1=(3, size_x - 3), dv1=(3, size_x - 3), th=(2, size_x - 2),
    )
    return {name: ranges[name] for name in KEPT}


def inner_kernel(coarse_y, phase, solute, side_a, side_b, coarse, phase_out, solute_out, latent, *rest):
    kept = dict(zip(KEPT, rest[: len(KEPT)]))
    fz, phase_new, solute_new, sems, out_sems = rest[len(KEPT) :]
    size_x, size_y, size_z = phase.shape
    span = spans(size_x)
    even_y = lax.rem(lax.axis_index("gy"), 2) == 0
    at = lambda name, x: kept[name].at[x - span[name][0]]
    get = lambda name, x: kept[name][x - span[name][0]]
    copies = start_all(
        [(ref, kept[name].at[:, pl.ds(0, size_y), :]) for name, ref in (("p0", phase), ("c0", solute))], sems
    )
    top = row_ids((size_x, ROWS, size_z)) < HALO
    first, second = side_a[pl.ds(0, size_x)], side_b[pl.ds(0, size_x)]
    low, high = jnp.where(even_y, second, first), jnp.where(even_y, first, second)
    kept["p0"][:, pl.ds(size_y, ROWS), :] = jnp.where(top, high, low)
    kept["c0"][:, pl.ds(size_y, ROWS), :] = pltpu.roll(jnp.where(top, low, high), HALO, 1)
    fans = dict(enumerate(interpolate(coarse[...], coarse_y, size_y, size_z)))
    for x in range(*span["th"]):
        at("th", x)[...] = blend(x, fans)
    gradient, difference, laplace = z_matrices(size_z)
    wait_all(copies)

    for step in "01":
        p, c, dz, cz, gx, dv = (name + step for name in ("p", "c", "dz", "cz", "gx", "dv"))
        kept[dz][...] = along(kept[p][...], gradient)
        kept[cz][...] = along(kept[c][...], laplace)
        begin, end = span[gx]
        for x in range(begin, end):
            flux_x, flux_y, flux_z = flux(get(p, x - 1), get(p, x), get(p, x + 1), get(dz, x))
            at(gx, x)[...] = flux_x
            at(dv, x)[...] = spread(flux_y)
            fz[x - begin] = flux_z
        kept[dv][...] += along(fz[pl.ds(0, end - begin)], difference)
        take = (lambda v: v) if step == "0" else (lambda v: v[:size_y])
        for x in range(begin + 1, end - 1):
            here, conc = take(get(p, x)), get(c, x)
            divergence = take(get(gx, x + 1)) - take(get(gx, x - 1)) + take(get(dv, x))
            change = phase_change(here, take(conc), take(get("th", x)), divergence)
            beyond = take(get(c, x + 2)) + take(get(c, x - 2))
            new_conc = solute_step(take(conc), beyond, take(next_row(conc)), take(get(cz, x)), change)
            if step == "0":
                at("p1", x)[...] = here + change
                at("c1", x)[...] = new_conc
            else:
                phase_new[x - begin - 1] = here + change
                solute_new[x - begin - 1] = new_conc
    count = size_x - 8
    copies = start_all(
        [(phase_new, phase_out.at[pl.ds(4, count)]), (solute_new, solute_out.at[pl.ds(4, count)])], out_sems
    )
    pool = pools(size_y, size_z)
    for k in range(1, size_x // 4 - 1):
        change = jnp.zeros((size_y, size_z), F32)
        for x in range(4 * k, 4 * k + 4):
            change = change + (phase_new[x - 4] - get("p0", x)[:size_y])
        latent[k - 1] = restrict(change, pool)
    wait_all(copies)


def inner(phase, solute, side_a, side_b, coarse, coarse_y):
    size_x, size_y, size_z = phase.shape
    rows = size_y + 2 * HALO
    out = jax.ShapeDtypeStruct(phase.shape, F32)
    kept = [jax.ShapeDtypeStruct((end - begin, rows, size_z), F32) for begin, end in spans(size_x).values()]
    latent = jax.ShapeDtypeStruct((size_x // 4 - 2, size_y // 4, LANES), F32)
    part = pltpu.VMEM((size_x - 8, size_y, size_z), F32)
    return pl.pallas_call(
        functools.partial(inner_kernel, coarse_y),
        out_shape=(out, out, latent, *kept),
        in_specs=[anywhere(), anywhere()] + [vmem()] * 3,
        out_specs=[hbm(), hbm()] + [vmem()] * (1 + len(kept)),
        scratch_shapes=[
            pltpu.VMEM((size_x - 2, rows, size_z), F32), part, part,
            pltpu.SemaphoreType.DMA((2,)), pltpu.SemaphoreType.DMA((2,)),
        ],
        compiler_params=pltpu.CompilerParams(vmem_limit_bytes=VMEM_LIMIT),
        cost_estimate=pl.CostEstimate(flops=2 * 10**7, bytes_accessed=3 * 10**6, transcendentals=0),
        name="inner",
    )(phase, solute, side_a, side_b, coarse)


def rim_kernel(coarse_y, phase_in, solute_in, face_a, face_b, corner_a, corner_b, coarse, inner_latent, *rest):
    kept = dict(zip(KEPT, rest[: len(KEPT)]))
    phase_out, solute_out, latent = rest[len(KEPT) : len(KEPT) + 3]
    hp0, hc0, p1, c1, gx, dv, dz, cz, fz, th, phase_new, solute_new, sems, out_sems = rest[len(KEPT) + 3 :]
    size_x = latent.shape[0] * 4
    size_y, size_z = phase_out.shape[1:]
    span = spans(size_x)
    even_x = lax.rem(lax.axis_index("gx"), 2) == 0
    spot_a = jnp.where(even_x, HALO, 0)
    spot_b = HALO - spot_a
    copies = []
    for n, field in enumerate((hp0, hc0)):
        copies.append((face_a.at[n], field.at[pl.ds(spot_a, HALO), pl.ds(0, size_y), :]))
        copies.append((face_b.at[n], field.at[pl.ds(spot_b, HALO), pl.ds(0, size_y), :]))
    copies = start_all(copies, sems)

    top = row_ids((ROWS, size_z)) < HALO

    def put(at, low, high):
        hp0[at, pl.ds(size_y, ROWS), :] = jnp.where(top, high, low)
        hc0[at, pl.ds(size_y, ROWS), :] = pltpu.roll(jnp.where(top, low, high), HALO, 0)

    edges = []
    for above in (False, True):
        use_a = even_x if above else jnp.logical_not(even_x)
        tile = jnp.where(use_a, corner_a[...], corner_b[...])
        place = lambda d: HALO - 1 + d if above else HALO - d
        put(place(1), tile[0], tile[2])
        put(place(2), tile[1], tile[3])
        put(place(3), pltpu.roll(tile[1], 2, 0), pltpu.roll(tile[3], 6, 0))
        put(place(4), jnp.zeros_like(tile[0]), jnp.zeros_like(tile[0]))
        edge = unfold(tile[4:].reshape(-1, 2 * LANES))
        stack = LANES // coarse_y
        edges.append(
            jnp.concatenate([edge[:, q * coarse_y : (q + 1) * coarse_y] for q in range(stack)], axis=0)
        )
    width = coarse.shape[1]
    below = jnp.concatenate([edges[0], coarse[:, :coarse_y]], axis=1)
    above = jnp.concatenate([coarse[:, width - coarse_y :], edges[1]], axis=1)
    fans = interpolate(jnp.concatenate([below, above], axis=1), coarse_y, size_y, size_z)
    last = size_x // 4
    fans = {-1: fans[0], 0: fans[1], last - 1: fans[2], last: fans[3]}
    gradient, difference, laplace = z_matrices(size_z)

    def ref(array, begin, x):
        half = array.shape[0] // 2
        return array.at[x - begin] if x < size_x // 2 else array.at[half + x - (size_x - half - begin)]

    def get(name, x):
        begin, end = span[name]
        if begin <= x < end:
            return kept[name][x - begin]
        own, first = dict(
            p0=(hp0, -4), c0=(hc0, -4), dz0=(dz, -3), cz0=(cz, -2), gx0=(gx, -3), dv0=(dv, -2),
            p1=(p1, -2), c1=(c1, -2), dz1=(dz, -1), cz1=(cz, 0), gx1=(gx, -1), dv1=(dv, 0), th=(th, -2),
        )[name]
        return ref(own, first, x)[...]

    rim = lambda begin, end: [*range(begin, end), *range(size_x - end, size_x - begin)]
    for x in rim(-2, 2):
        ref(th, -2, x)[...] = blend(x, fans)
    wait_all(copies)

    for step, begin in (("0", -3), ("1", -1)):
        p, c, gx_, dv_, dz_, cz_ = (name + step for name in ("p", "c", "gx", "dv", "dz", "cz"))
        fields = (hp0[pl.ds(1, 6)], hc0[pl.ds(2, 4)]) if step == "0" else (p1[pl.ds(1, 6)], c1[pl.ds(2, 4)])
        dz[...] = along(fields[0], gradient)
        cz[...] = along(fields[1], laplace)
        for x in rim(begin, begin + 4):
            flux_x, flux_y, flux_z = flux(get(p, x - 1), get(p, x), get(p, x + 1), get(dz_, x))
            ref(gx, begin, x)[...] = flux_x
            if x not in (begin, size_x - 1 - begin):
                ref(dv, begin + 1, x)[...] = spread(flux_y)
                ref(fz, begin + 1, x)[...] = flux_z
        dv[...] += along(fz[...], difference)
        take = (lambda v: v) if step == "0" else (lambda v: v[:size_y])
        for x in rim(begin + 1, begin + 5):
            here, conc = take(get(p, x)), get(c, x)
            divergence = take(get(gx_, x + 1)) - take(get(gx_, x - 1)) + take(get(dv_, x))
            change = phase_change(here, take(conc), take(get("th", x)), divergence)
            beyond = take(get(c, x + 2)) + take(get(c, x - 2))
            new_conc = solute_step(take(conc), beyond, take(next_row(conc)), take(get(cz_, x)), change)
            if step == "0":
                ref(p1, -2, x)[...] = here + change
                ref(c1, -2, x)[...] = new_conc
            else:
                ref(phase_new, 0, x)[...] = here + change
                ref(solute_new, 0, x)[...] = new_conc
    copies = []
    for n, (new, out) in enumerate(((phase_new, phase_out), (solute_new, solute_out))):
        copies.append((new.at[pl.ds(0, 4)], out.at[pl.ds(0, 4)]))
        copies.append((new.at[pl.ds(4, 4)], out.at[pl.ds(size_x - 4, 4)]))
    copies = start_all(copies, out_sems)
    pool = pools(size_y, size_z)
    latent[pl.ds(1, last - 2)] = inner_latent[...]
    for k in (0, last - 1):
        change = jnp.zeros((size_y, size_z), F32)
        for x in range(4 * k, 4 * k + 4):
            change = change + (ref(phase_new, 0, x)[...] - get("p0", x)[:size_y])
        latent[k] = restrict(change, pool)
    wait_all(copies)


def rims(phase, solute, face_a, face_b, corner_a, corner_b, coarse, inner_latent, kept, coarse_y):
    size_x, size_y, size_z = phase.shape
    rows = size_y + 2 * HALO
    out = jax.ShapeDtypeStruct(phase.shape, F32)
    slabs = lambda count: pltpu.VMEM((count, rows, size_z), F32)
    part = pltpu.VMEM((8, size_y, size_z), F32)
    return pl.pallas_call(
        functools.partial(rim_kernel, coarse_y),
        out_shape=(out, out, jax.ShapeDtypeStruct((size_x // 4, size_y // 4, LANES), F32)),
        in_specs=[hbm(), hbm()] + [vmem()] * (6 + len(kept)),
        out_specs=[hbm(), hbm(), vmem()],
        scratch_shapes=[
            slabs(8), slabs(8), slabs(8), slabs(8), slabs(8), slabs(6), slabs(6), slabs(4), slabs(6), slabs(8), part, part,
            pltpu.SemaphoreType.DMA((4,)), pltpu.SemaphoreType.DMA((4,)),
        ],
        input_output_aliases={0: 0, 1: 1},
        compiler_params=pltpu.CompilerParams(vmem_limit_bytes=VMEM_LIMIT),
        cost_estimate=pl.CostEstimate(flops=2 * 10**7, bytes_accessed=3 * 10**6, transcendentals=0),
        name="rims",
    )(phase, solute, face_a, face_b, corner_a, corner_b, coarse, inner_latent, *kept)


def owner_kernel(coarse_z, mine, core, chip, far, out):
    me = lax.axis_index("gy")
    coarse_x, per, _ = mine.shape
    lane = lane_ids((coarse_x, coarse_z, coarse_x * per))
    total = jnp.zeros(lane.shape, F32)
    shift = lax.rem(LANES - me * coarse_z, LANES)
    for source, ref in zip(flips(me), (mine, core, chip, far)):
        block = jnp.stack([pltpu.roll(ref[k], shift, 1)[:, :coarse_z] for k in range(coarse_x)])
        block = jnp.swapaxes(block, 1, 2)
        block = jnp.concatenate([block] * 4, axis=2)
        total = jnp.where((lane >= source * per) & (lane < (source + 1) * per), block, total)
    out[...] = total


def owner(parts, coarse_y, coarse_z):
    coarse_x = parts[0].shape[0]
    return pl.pallas_call(
        functools.partial(owner_kernel, coarse_z),
        out_shape=jax.ShapeDtypeStruct((coarse_x, coarse_z, coarse_y), F32),
        in_specs=[vmem()] * 4,
        out_specs=vmem(),
        compiler_params=pltpu.CompilerParams(vmem_limit_bytes=VMEM_LIMIT),
        name="owner",
    )(*parts)


def body(phase, solute, macro_temp):
    count_x, count_y = lax.axis_size("gx"), lax.axis_size("gy")
    coarse_x, coarse_y, coarse_z = macro_temp.shape
    near_x, far_x = pairs(count_x, 0), pairs(count_x, 1)
    near_y, far_y = pairs(count_y, 0), pairs(count_y, 1)
    across = [(k, (k + count_y // 2) % count_y) for k in range(count_y)]
    ride = count_y == 4
    macro = jnp.swapaxes(macro_temp, 1, 2)
    face_a, face_b, side_a, side_b, table = pack(phase, solute, macro, ride)
    face_a = lax.ppermute(face_a, "gx", near_x)
    face_b = lax.ppermute(face_b, "gx", far_x)
    side_b = lax.ppermute(side_b, "gy", far_y)
    side_a = lax.ppermute(side_a, "gy", near_y)
    coarse_shape = (coarse_z * count_y, coarse_x * coarse_y)
    if ride:
        tables = (table, lax.ppermute(table, "gy", across))
    else:
        tables = (lax.all_gather(table, "gy").reshape(coarse_shape),)
    coarse, corner_a, corner_b = corners(side_a, side_b, tables, coarse_y, coarse_shape)
    corner_a = lax.ppermute(corner_a, "gx", near_x)
    corner_b = lax.ppermute(corner_b, "gx", far_x)
    phase_out, solute_out, inner_latent, *kept = inner(phase, solute, side_a, side_b, coarse, coarse_y)
    phase_out, solute_out, latent = rims(
        phase_out, solute_out, face_a, face_b, corner_a, corner_b, coarse, inner_latent, kept, coarse_y
    )
    if ride:
        chip = lax.ppermute(latent, "gy", across)
        core = lax.ppermute(latent, "gy", near_y)
        latent = owner((latent, core, chip, lax.ppermute(chip, "gy", near_y)), coarse_y, coarse_z)
        latent = jnp.swapaxes(latent, 1, 2)
    else:
        split = latent[:, :, : coarse_z * count_y].reshape(coarse_x, latent.shape[1], count_y, coarse_z)
        latent = lax.all_to_all(split, "gy", split_axis=2, concat_axis=1, tiled=True)
        latent = latent.reshape(coarse_x, coarse_y, coarse_z)
    return phase_out, solute_out, latent


def solution(mesh):
    in_specs = (P("gx", "gy", None), P("gx", "gy", None), P("gx", None, "gy"))
    out_specs = (P("gx", "gy", None), P("gx", "gy", None), P("gx", None, "gy"))
    return jax.shard_map(body, mesh=mesh, in_specs=in_specs, out_specs=out_specs, check_vma=False)
```

```python
import functools

import jax
import jax.numpy as jnp
from jax import lax
from jax.experimental import pallas as pl
from jax.experimental.pallas import tpu as pltpu
from jax.sharding import PartitionSpec as P

time_step = 0.1
anisotropy = 0.3
coupling = 2.0
rejection = 0.5

F32 = jnp.float32
HIGHEST = lax.Precision.HIGHEST
HALO = 4
ROWS = 8
LANES = 128
VMEM_LIMIT = 24 * 1024 * 1024


def vmem():
    return pl.BlockSpec(memory_space=pltpu.VMEM)


def anywhere():
    return pl.BlockSpec(memory_space=pl.ANY)


def hbm():
    return pl.BlockSpec(memory_space=pltpu.HBM)


def pairs(count, first):
    forward = [((first + k) % count, (first + k + 1) % count) for k in range(0, count, 2)]
    return forward + [(b, a) for a, b in forward]


def flips(me):
    odd = lax.rem(me, 2)
    return me, me + 1 - 2 * odd, lax.rem(me + 2, 4), 3 - me


def row_ids(shape):
    return lax.broadcasted_iota(jnp.int32, shape, len(shape) - 2)


def lane_ids(shape):
    return lax.broadcasted_iota(jnp.int32, shape, len(shape) - 1)


def start_all(copies, sems):
    copies = [pltpu.make_async_copy(source, target, sems.at[n]) for n, (source, target) in enumerate(copies)]
    for copy in copies:
        copy.start()
    return copies


def wait_all(copies):
    for copy in copies:
        copy.wait()


def fold(table):
    half = table.shape[0] // 2
    return jnp.concatenate([table[:half], table[half:]], axis=1)


def unfold(tile):
    return jnp.concatenate([tile[:, :LANES], tile[:, LANES:]], axis=0)


def pack_kernel(phase, solute, macro, face_a, face_b, side_a, side_b, table, low, high, local, sems):
    size_x, size_y, size_z = phase.shape
    odd_x = lax.rem(lax.axis_index("gx"), 2)
    even_y = lax.rem(lax.axis_index("gy"), 2) == 0
    start_a = (1 - odd_x) * (size_x - HALO)
    start_b = odd_x * (size_x - HALO)
    copies = []
    for field, ref in enumerate((phase, solute)):
        copies.append((ref.at[pl.ds(start_a, HALO)], face_a.at[field]))
        copies.append((ref.at[:, pl.ds(0, ROWS), :], low.at[field]))
        copies.append((ref.at[:, pl.ds(size_y - ROWS, ROWS), :], high.at[field]))
        copies.append((ref.at[pl.ds(start_b, HALO)], face_b.at[field]))
    copies.append((macro, local))
    copies = start_all(copies, sems)
    wait_all(copies)
    wide = jnp.concatenate([local[k] for k in range(local.shape[0])], axis=1)
    table[...] = wide
    top = row_ids((size_x, ROWS, size_z)) < HALO
    low_side = jnp.where(top, low[0], pltpu.roll(low[1], HALO, 1))
    high_side = jnp.where(top, pltpu.roll(high[1], HALO, 1), high[0])
    side_a[pl.ds(0, size_x)] = jnp.where(even_y, high_side, low_side)
    side_b[pl.ds(0, size_x)] = jnp.where(even_y, low_side, high_side)
    if side_a.shape[0] > size_x:
        side_a[size_x] = fold(wide)
        side_b[size_x] = fold(wide)


def pack(phase, solute, macro, ride):
    size_x, size_y, size_z = phase.shape
    coarse_x, coarse_z, coarse_y = macro.shape
    face = jax.ShapeDtypeStruct((2, HALO, size_y, size_z), F32)
    sides = [jax.ShapeDtypeStruct((size_x + extra, ROWS, size_z), F32) for extra in ((1, 2) if ride else (0, 0))]
    table = jax.ShapeDtypeStruct((coarse_z, coarse_x * coarse_y), F32)
    return pl.pallas_call(
        pack_kernel,
        out_shape=(face, face, *sides, table),
        in_specs=[hbm()] * 3,
        out_specs=[vmem()] * 5,
        scratch_shapes=[
            pltpu.VMEM((2, size_x, ROWS, size_z), F32),
            pltpu.VMEM((2, size_x, ROWS, size_z), F32),
            pltpu.VMEM(macro.shape, F32),
            pltpu.SemaphoreType.DMA((9,)),
        ],
        compiler_params=pltpu.CompilerParams(vmem_limit_bytes=VMEM_LIMIT),
        cost_estimate=pl.CostEstimate(flops=10**5, bytes_accessed=2 * 10**6, transcendentals=0),
        name="pack",
    )(phase, solute, macro)


def append_kernel(arrived, side, out):
    out[side.shape[0] - 1] = arrived[arrived.shape[0] - 1]


def append(arrived, side):
    return pl.pallas_call(
        append_kernel,
        out_shape=jax.ShapeDtypeStruct(side.shape, F32),
        in_specs=[vmem(), vmem()],
        out_specs=vmem(),
        input_output_aliases={1: 0},
        compiler_params=pltpu.CompilerParams(vmem_limit_bytes=VMEM_LIMIT),
        cost_estimate=pl.CostEstimate(flops=0, bytes_accessed=10**5, transcendentals=0),
        name="append",
    )(arrived, side)


def corner_kernel(coarse_y, gathered, side_a, side_b, table, coarse, corner_a, corner_b):
    size_x = side_a.shape[0] - (0 if gathered else 1)
    me = lax.axis_index("gy")
    even_x = lax.rem(lax.axis_index("gx"), 2) == 0
    even_y = lax.rem(me, 2) == 0
    block = table[...]
    if not gathered:
        near, across, far = flips(me)[1:]
        depth = table.shape[0]
        tiles = (me, block), (near, unfold(side_a[size_x])), (far, unfold(side_b[size_x])), (across, unfold(side_b[size_x + 1]))
        for source, tile in tiles:
            coarse[pl.ds(pl.multiple_of(source * depth, depth), depth), :] = tile
        block = coarse[...]
    depth, width = block.shape
    flipped = [block[:, at : at + coarse_y] for at in range(width - coarse_y, -1, -coarse_y)]
    block = jnp.where(even_x, block, jnp.concatenate(flipped, axis=1))
    coarse[...] = block
    stack = LANES // coarse_y
    height = depth // stack
    row = row_ids(side_a.shape[1:])
    edges = block[:, width - coarse_y :], block[:, :coarse_y]
    for corner, top_side, edge in ((corner_a, even_x, edges[0]), (corner_b, jnp.logical_not(even_x), edges[1])):
        for n, keep in ((0, 5), (1, 2)):
            def layer(d, n=n):
                at = jnp.where(top_side, size_x - d, d - 1)
                first, second = side_a[at], side_b[at]
                return jnp.where(even_y, second, first) if n == 0 else jnp.where(even_y, first, second)

            corner[2 * n] = layer(1)
            corner[2 * n + 1] = jnp.where(row == keep, pltpu.roll(layer(3), 6 if n == 0 else 2, 0), layer(2))
        edge = jnp.concatenate([edge[q * height : (q + 1) * height] for q in range(stack)], axis=1)
        corner[pl.ds(4, height // 16)] = fold(edge).reshape(height // 16, ROWS, 2 * LANES)


def corners(side_a, side_b, table, coarse_y, coarse_shape):
    size_z = side_a.shape[2]
    height = coarse_shape[0] * coarse_y // LANES
    corner = jax.ShapeDtypeStruct((4 + height // 16, ROWS, size_z), F32)
    coarse = jax.ShapeDtypeStruct(coarse_shape, F32)
    return pl.pallas_call(
        functools.partial(corner_kernel, coarse_y, table.shape == coarse_shape),
        out_shape=(coarse, corner, corner),
        in_specs=[vmem()] * 3,
        out_specs=[vmem()] * 3,
        compiler_params=pltpu.CompilerParams(vmem_limit_bytes=VMEM_LIMIT),
        cost_estimate=pl.CostEstimate(flops=10**5, bytes_accessed=4 * 10**5, transcendentals=0),
        name="corners",
    )(side_a, side_b, table)


def weights(lower, frac, shape, tick):
    first, second = lower
    return jnp.where(tick == first, 1.0 - frac, 0.0) + jnp.where(tick == second, frac, 0.0)


def interpolate(block, coarse_y, size_y, size_z):
    depth, width = block.shape
    rows = size_y + 2 * HALO
    shape = (depth, size_z)
    fine = lane_ids(shape)
    lower = (2 * fine + 5) // 8 - 1
    frac = (2 * fine - 3 - 8 * lower).astype(F32) / 8.0
    ends = jnp.clip(lower, 0, depth - 1), jnp.clip(lower + 1, 0, depth - 1)
    along_z = weights(ends, frac, shape, row_ids(shape))
    deep = lax.dot_general(block, along_z, (((0,), (0,)), ((), ())), precision=HIGHEST, preferred_element_type=F32)
    shape = (rows, coarse_y)
    fine = row_ids(shape)
    fine = jnp.where(fine >= size_y + HALO, fine - rows, fine)
    local = (2 * fine + 13) // 8 - 2
    frac = (2 * fine - 3 - 8 * local).astype(F32) / 8.0
    lower = local + lax.axis_index("gy") * (size_y // 4) + coarse_y
    ends = lax.rem(lower, coarse_y), lax.rem(lower + 1, coarse_y)
    along_y = weights(ends, frac, shape, lane_ids(shape))
    return [
        jnp.dot(along_y, deep[k * coarse_y : (k + 1) * coarse_y], precision=HIGHEST, preferred_element_type=F32)
        for k in range(width // coarse_y)
    ]


def blend(x, fans):
    lower = (2 * x - 3) // 8
    frac = (2 * x - 3 - 8 * lower) / 8.0
    return (1.0 - frac) * fans[lower] + frac * fans[lower + 1]


def turn(value, by, axis):
    return pltpu.roll(value, by % value.shape[axis], axis)


def z_matrices(size_z):
    shape = (size_z, size_z)
    source, target = row_ids(shape), lane_ids(shape)
    hit = lambda at: (source == at).astype(F32)
    end = size_z - 1
    gradient = hit(jnp.minimum(target + 1, end)) - hit(jnp.maximum(target - 1, 0))
    difference = hit(target + 1) - hit(target - 1)
    laplace = hit(jnp.minimum(target + 2, end)) + hit(jnp.maximum(target - 2, 0)) - 6.0 * hit(target)
    return tuple(m.astype(jnp.bfloat16) for m in (gradient, difference, laplace))


def matrix_kernel(size_z, tile, out):
    for n, matrix in enumerate(z_matrices(size_z)):
        out[n] = matrix


def z_products(size_z, tile):
    return pl.pallas_call(
        functools.partial(matrix_kernel, size_z),
        out_shape=jax.ShapeDtypeStruct((3, size_z, size_z), jnp.bfloat16),
        in_specs=[anywhere()],
        out_specs=vmem(),
        compiler_params=pltpu.CompilerParams(vmem_limit_bytes=VMEM_LIMIT),
        cost_estimate=pl.CostEstimate(flops=10**6, bytes_accessed=4 * 10**5, transcendentals=0),
        name="products",
    )(tile)


def along(slabs, matrix):
    value = slabs.reshape(-1, slabs.shape[-1])
    coarse = value.astype(jnp.bfloat16)
    rest = (value - coarse.astype(F32)).astype(jnp.bfloat16)
    product = jnp.dot(coarse, matrix, preferred_element_type=F32) + jnp.dot(rest, matrix, preferred_element_type=F32)
    return product.reshape(slabs.shape)


def flux(before, here, after, along_z):
    along_x = after - before
    along_y = turn(here, -1, 0) - turn(here, 1, 0)
    sq_x = along_x * along_x
    sq_y = along_y * along_y
    both = sq_x + sq_y
    inverse = 1.0 / (both + 4.0)
    factor = 1.0 + anisotropy * (both * both - 8.0 * (sq_x * sq_y)) * (inverse * inverse)
    stiff = (0.25 * time_step) * (factor * factor)
    return stiff * along_x, stiff * along_y, stiff * along_z


def spread(flux_y):
    return turn(flux_y, -1, 0) - turn(flux_y, 1, 0)


def phase_change(here, conc, theta, divergence):
    square = 1.0 - here * here
    drive = square * (here - (coupling * square) * (theta + conc))
    return divergence + time_step * drive


def solute_step(conc, beyond_x, beyond_y, along_z, change):
    return conc + (0.25 * time_step) * (beyond_x + beyond_y + along_z) + rejection * change


def next_row(conc):
    return turn(conc, -2, 0) + turn(conc, 2, 0)


def pools(size_y, size_z):
    pool_y = (row_ids((size_y // 4, size_y)) == lane_ids((size_y // 4, size_y)) // 4).astype(F32)
    pool_z = (row_ids((size_z, LANES)) // 4 == lane_ids((size_z, LANES))).astype(F32)
    return pool_y, pool_z


def restrict(change, pool):
    pool_y, pool_z = pool
    change = jnp.dot(change, pool_z, precision=HIGHEST, preferred_element_type=F32)
    return (0.5 / 64.0) * jnp.dot(pool_y, change, precision=HIGHEST, preferred_element_type=F32)


KEPT = ("p0", "c0", "dz0", "cz0", "gx0", "dv0", "p1", "c1", "dz1", "cz1", "gx1", "dv1", "th")


def spans(size_x):
    widths = dict(p0=0, c0=0, dz0=0, cz0=0, gx0=1, dv0=1, p1=2, c1=2, dz1=2, cz1=2, gx1=3, dv1=3, th=2)
    return {name: (widths[name], size_x - widths[name]) for name in KEPT}


def halo_rows(tile, top):
    zero = jnp.zeros_like(tile[0])
    low = tile[0], tile[1], pltpu.roll(tile[1], 2, 0), zero
    high = tile[2], tile[3], pltpu.roll(tile[3], 6, 0), zero
    return [
        (jnp.where(top, h, l), pltpu.roll(jnp.where(top, l, h), HALO, 0)) for l, h in zip(low, high)
    ]


def edge_block(tiles, coarse_y):
    edge = unfold(tiles.reshape(-1, 2 * LANES))
    return jnp.concatenate([edge[:, at : at + coarse_y] for at in range(0, LANES, coarse_y)], axis=0)


def inner_kernel(coarse_y, phase, solute, side_a, side_b, coarse, matrices, phase_out, solute_out, latent, *rest):
    kept = dict(zip(KEPT, rest[: len(KEPT)]))
    fz, phase_new, solute_new, out_sems = rest[len(KEPT) :]
    size_x, size_y, size_z = phase.shape
    span = spans(size_x)
    odd_x = lax.rem(lax.axis_index("gx"), 2)
    even_y = lax.rem(lax.axis_index("gy"), 2) == 0
    at = lambda name, u: kept[name].at[u - span[name][0]]
    get = lambda name, u: kept[name][u - span[name][0]]
    place = lambda u: u + odd_x * (size_x - 1 - 2 * u)
    top = row_ids((ROWS, size_z)) < HALO
    for u in range(size_x):
        first, second = side_a[place(u)], side_b[place(u)]
        low, high = jnp.where(even_y, second, first), jnp.where(even_y, first, second)
        at("p0", u)[pl.ds(0, size_y), :] = phase[place(u)]
        at("c0", u)[pl.ds(0, size_y), :] = solute[place(u)]
        at("p0", u)[pl.ds(size_y, ROWS), :] = jnp.where(top, high, low)
        at("c0", u)[pl.ds(size_y, ROWS), :] = pltpu.roll(jnp.where(top, low, high), HALO, 0)
    fans = dict(enumerate(interpolate(coarse[...], coarse_y, size_y, size_z)))
    for u in range(*span["th"]):
        at("th", u)[...] = blend(u, fans)

    for step in "01":
        p, c, dz, cz, gx, dv = (name + step for name in ("p", "c", "dz", "cz", "gx", "dv"))
        kept[dz][...] = along(kept[p][...], matrices[0])
        kept[cz][...] = along(kept[c][...], matrices[2])
        begin, end = span[gx]
        for u in range(begin, end):
            flux_x, flux_y, flux_z = flux(get(p, u - 1), get(p, u), get(p, u + 1), get(dz, u))
            at(gx, u)[...] = flux_x
            at(dv, u)[...] = spread(flux_y)
            fz[u - begin] = flux_z
        kept[dv][...] += along(fz[pl.ds(0, end - begin)], matrices[1])
        take = (lambda v: v) if step == "0" else (lambda v: v[:size_y])
        for u in range(begin + 1, end - 1):
            here, conc = take(get(p, u)), get(c, u)
            divergence = take(get(gx, u + 1)) - take(get(gx, u - 1)) + take(get(dv, u))
            change = phase_change(here, take(conc), take(get("th", u)), divergence)
            beyond = take(get(c, u + 2)) + take(get(c, u - 2))
            new_conc = solute_step(take(conc), beyond, take(next_row(conc)), take(get(cz, u)), change)
            if step == "0":
                at("p1", u)[...] = here + change
                at("c1", u)[...] = new_conc
            else:
                phase_new[place(u) - HALO] = here + change
                solute_new[place(u) - HALO] = new_conc
    middle = pl.ds(HALO, size_x - 2 * HALO)
    copies = start_all([(phase_new, phase_out.at[middle]), (solute_new, solute_out.at[middle])], out_sems)
    pool = pools(size_y, size_z)
    for k in range(1, size_x // 4 - 1):
        change = jnp.zeros((size_y, size_z), F32)
        for u in range(4 * k, 4 * k + 4):
            change = change + (phase_new[place(u) - HALO] - get("p0", u)[:size_y])
        latent[k - 1] = restrict(change, pool)
    wait_all(copies)


def inner(phase, solute, side_a, side_b, coarse, matrices, coarse_y):
    size_x, size_y, size_z = phase.shape
    rows = size_y + 2 * HALO
    out = jax.ShapeDtypeStruct(phase.shape, F32)
    kept = [jax.ShapeDtypeStruct((end - begin, rows, size_z), F32) for begin, end in spans(size_x).values()]
    latent = jax.ShapeDtypeStruct((size_x // 4 - 2, size_y // 4, LANES), F32)
    part = pltpu.VMEM((size_x - 2 * HALO, size_y, size_z), F32)
    return pl.pallas_call(
        functools.partial(inner_kernel, coarse_y),
        out_shape=(out, out, latent, *kept),
        in_specs=[vmem()] * 6,
        out_specs=[hbm(), hbm()] + [vmem()] * (1 + len(kept)),
        scratch_shapes=[pltpu.VMEM((size_x - 2, rows, size_z), F32), part, part, pltpu.SemaphoreType.DMA((2,))],
        compiler_params=pltpu.CompilerParams(vmem_limit_bytes=VMEM_LIMIT),
        cost_estimate=pl.CostEstimate(flops=10**8, bytes_accessed=10**6, transcendentals=0),
        name="inner",
    )(phase, solute, side_a, side_b, coarse, matrices)


def rim_steps(coarse_y, near, size_x, face, corner, coarse, matrices, kept, scratch, phase_new, solute_new):
    hp0, hc0, p1, c1, gx, dv, dz, cz, fz, th = scratch
    _, size_y, size_z = phase_new.shape
    span = spans(size_x)
    odd_x = lax.rem(lax.axis_index("gx"), 2)
    flip = odd_x if near else 1 - odd_x
    top = row_ids((ROWS, size_z)) < HALO
    for d, (p_rows, c_rows) in enumerate(halo_rows(corner, top)):
        layer = d + flip * (HALO - 1 - 2 * d)
        for n, (field, rows) in enumerate(((hp0, p_rows), (hc0, c_rows))):
            field[HALO - 1 - d, pl.ds(0, size_y), :] = face[n, layer]
            field[HALO - 1 - d, pl.ds(size_y, ROWS), :] = rows
    own = coarse[:, coarse.shape[1] - coarse_y :] if near else coarse[:, :coarse_y]
    block = jnp.concatenate([edge_block(corner[4:], coarse_y), own], axis=1)
    fans = dict(enumerate(interpolate(block, coarse_y, size_y, size_z), -1))
    for v in range(-2, 2):
        th[v + 2] = blend(v, fans)

    def get(name, v):
        begin, end = span[name]
        if v >= begin:
            found = kept[name][(size_x - 1 - v if near else v) - begin]
            return -found if near and name.startswith("gx") else found
        own, first = dict(
            p0=(hp0, -4), c0=(hc0, -4), dz0=(dz, -3), cz0=(cz, -2), gx0=(gx, -3), dv0=(dv, -2),
            p1=(p1, -2), c1=(c1, -2), dz1=(dz, -1), cz1=(cz, 0), gx1=(gx, -1), dv1=(dv, 0), th=(th, -2),
        )[name]
        return own[v - first]

    for step, begin in (("0", -3), ("1", -1)):
        p, c, gx_, dv_, dz_, cz_ = (name + step for name in ("p", "c", "gx", "dv", "dz", "cz"))
        fields = (hp0[pl.ds(1, 3)], hc0[pl.ds(2, 2)]) if step == "0" else (p1[pl.ds(1, 3)], c1[pl.ds(2, 2)])
        dz[...] = along(fields[0], matrices[0])
        cz[...] = along(fields[1], matrices[2])
        for v in range(begin, begin + 4):
            flux_x, flux_y, flux_z = flux(get(p, v - 1), get(p, v), get(p, v + 1), get(dz_, v))
            gx[v - begin] = flux_x
            if v > begin:
                dv[v - begin - 1] = spread(flux_y)
                fz[v - begin - 1] = flux_z
        dv[...] += along(fz[...], matrices[1])
        take = (lambda w: w) if step == "0" else (lambda w: w[:size_y])
        for v in range(begin + 1, begin + 5):
            here, conc = take(get(p, v)), get(c, v)
            divergence = take(get(gx_, v + 1)) - take(get(gx_, v - 1)) + take(get(dv_, v))
            change = phase_change(here, take(conc), take(get("th", v)), divergence)
            beyond = take(get(c, v + 2)) + take(get(c, v - 2))
            new_conc = solute_step(take(conc), beyond, take(next_row(conc)), take(get(cz_, v)), change)
            new = (p1, c1) if step == "0" else (phase_new, solute_new)
            new[0][v - begin - 1] = here + change
            new[1][v - begin - 1] = new_conc
    change = jnp.zeros((size_y, size_z), F32)
    for v in range(HALO):
        change = change + (phase_new[v] - get("p0", v)[:size_y])
    return restrict(change, pools(size_y, size_z))


def near_kernel(coarse_y, size_x, face, corner, coarse, matrices, *rest):
    kept = dict(zip(KEPT, rest[: len(KEPT)]))
    phase_new, solute_new, latent = rest[len(KEPT) : len(KEPT) + 3]
    latent[...] = rim_steps(
        coarse_y, True, size_x, face, corner, coarse, matrices, kept, rest[len(KEPT) + 3 :], phase_new, solute_new
    )


def far_kernel(
    coarse_y, phase_in, solute_in, face, corner, coarse, matrices, inner_latent, near_latent, near_phase, near_solute,
    *rest
):
    kept = dict(zip(KEPT, rest[: len(KEPT)]))
    phase_out, solute_out, latent = rest[len(KEPT) : len(KEPT) + 3]
    *scratch, phase_new, solute_new, sems = rest[len(KEPT) + 3 :]
    size_x = phase_out.shape[0]
    last = size_x // 4 - 1
    odd_x = lax.rem(lax.axis_index("gx"), 2)
    place = lambda u: u + odd_x * (size_x - 1 - 2 * u)
    copies = []
    for v in range(HALO):
        copies.append((near_phase.at[v], phase_out.at[place(size_x - 1 - v)]))
        copies.append((near_solute.at[v], solute_out.at[place(size_x - 1 - v)]))
    copies = start_all(copies, sems)
    total = rim_steps(coarse_y, False, size_x, face, corner, coarse, matrices, kept, scratch, phase_new, solute_new)
    more = []
    for v in range(HALO):
        more.append((phase_new.at[v], phase_out.at[place(v)]))
        more.append((solute_new.at[v], solute_out.at[place(v)]))
    more = start_all(more, sems.at[pl.ds(2 * HALO, 2 * HALO)])
    for k in range(last + 1):
        source = total if k == 0 else near_latent[...] if k == last else inner_latent[k - 1]
        latent[k + odd_x * (last - 2 * k)] = source
    wait_all(copies)
    wait_all(more)


def rim_scratch(size_y, size_z):
    counts = 4, 4, 4, 4, 4, 3, 3, 2, 3, 4
    return [pltpu.VMEM((count, size_y + 2 * HALO, size_z), F32) for count in counts]


def near_rim(shape, face, corner, coarse, matrices, kept, coarse_y):
    size_x, size_y, size_z = shape
    part = jax.ShapeDtypeStruct((HALO, size_y, size_z), F32)
    return pl.pallas_call(
        functools.partial(near_kernel, coarse_y, size_x),
        out_shape=(part, part, jax.ShapeDtypeStruct((size_y // 4, LANES), F32)),
        in_specs=[vmem()] * (4 + len(kept)),
        out_specs=[vmem()] * 3,
        scratch_shapes=rim_scratch(size_y, size_z),
        compiler_params=pltpu.CompilerParams(vmem_limit_bytes=VMEM_LIMIT),
        cost_estimate=pl.CostEstimate(flops=10**9, bytes_accessed=10**7, transcendentals=0),
        name="near",
    )(face, corner, coarse, matrices, *kept)


def far_rim(phase, solute, face, corner, coarse, matrices, inner_latent, near, kept, coarse_y):
    size_x, size_y, size_z = phase.shape
    out = jax.ShapeDtypeStruct(phase.shape, F32)
    near_phase, near_solute, near_latent = near
    part = pltpu.VMEM((HALO, size_y, size_z), F32)
    return pl.pallas_call(
        functools.partial(far_kernel, coarse_y),
        out_shape=(out, out, jax.ShapeDtypeStruct((size_x // 4, size_y // 4, LANES), F32)),
        in_specs=[hbm(), hbm()] + [vmem()] * (8 + len(kept)),
        out_specs=[hbm(), hbm(), vmem()],
        scratch_shapes=[*rim_scratch(size_y, size_z), part, part, pltpu.SemaphoreType.DMA((4 * HALO,))],
        input_output_aliases={0: 0, 1: 1},
        compiler_params=pltpu.CompilerParams(vmem_limit_bytes=VMEM_LIMIT),
        cost_estimate=pl.CostEstimate(flops=10**7, bytes_accessed=3 * 10**6, transcendentals=0),
        name="far",
    )(phase, solute, face, corner, coarse, matrices, inner_latent, near_latent, near_phase, near_solute, *kept)


def owner_kernel(coarse_z, mine, core, chip, far, out):
    me = lax.axis_index("gy")
    coarse_x, per, _ = mine.shape
    lane = lane_ids((coarse_x, coarse_z, coarse_x * per))
    total = jnp.zeros(lane.shape, F32)
    shift = lax.rem(LANES - me * coarse_z, LANES)
    for source, ref in zip(flips(me), (mine, core, chip, far)):
        block = jnp.stack([pltpu.roll(ref[k], shift, 1)[:, :coarse_z] for k in range(coarse_x)])
        block = jnp.swapaxes(block, 1, 2)
        block = jnp.concatenate([block] * 4, axis=2)
        total = jnp.where((lane >= source * per) & (lane < (source + 1) * per), block, total)
    out[...] = total


def owner(parts, coarse_y, coarse_z):
    coarse_x = parts[0].shape[0]
    return pl.pallas_call(
        functools.partial(owner_kernel, coarse_z),
        out_shape=jax.ShapeDtypeStruct((coarse_x, coarse_z, coarse_y), F32),
        in_specs=[vmem()] * 4,
        out_specs=vmem(),
        compiler_params=pltpu.CompilerParams(vmem_limit_bytes=VMEM_LIMIT),
        name="owner",
    )(*parts)


def body(phase, solute, macro_temp):
    count_x, count_y = lax.axis_size("gx"), lax.axis_size("gy")
    coarse_x, coarse_y, coarse_z = macro_temp.shape
    near_x, far_x = pairs(count_x, 0), pairs(count_x, 1)
    near_y, far_y = pairs(count_y, 0), pairs(count_y, 1)
    across = [(k, (k + count_y // 2) % count_y) for k in range(count_y)]
    ride = count_y == 4
    macro = jnp.swapaxes(macro_temp, 1, 2)
    still = [pltpu.with_memory_space_constraint(v, pltpu.HBM) for v in (phase, solute, macro)]
    face_a, face_b, side_a, side_b, table = pack(*still, ride)
    coarse_shape = (coarse_z * count_y, coarse_x * coarse_y)
    face_a = lax.ppermute(face_a, "gx", near_x)
    side_a = lax.ppermute(side_a, "gy", near_y)
    if ride:
        side_b = append(side_a, side_b)
    else:
        table = lax.all_gather(table, "gy").reshape(coarse_shape)
    matrices = z_products(phase.shape[2], side_b)
    face_b, matrices = lax.optimization_barrier((face_b, matrices))
    side_b = lax.ppermute(side_b, "gy", far_y)
    face_b = lax.ppermute(face_b, "gx", far_x)
    coarse, corner_a, corner_b = corners(side_a, side_b, table, coarse_y, coarse_shape)
    corner_a = lax.ppermute(corner_a, "gx", near_x)
    corner_b = lax.ppermute(corner_b, "gx", far_x)
    phase_out, solute_out, inner_latent, *kept = inner(phase, solute, side_a, side_b, coarse, matrices, coarse_y)
    near = near_rim(phase.shape, face_a, corner_a, coarse, matrices, kept, coarse_y)
    phase_out, solute_out, latent = far_rim(
        phase_out, solute_out, face_b, corner_b, coarse, matrices, inner_latent, near, kept, coarse_y
    )
    if ride:
        chip = lax.ppermute(latent, "gy", across)
        core = lax.ppermute(latent, "gy", near_y)
        latent = owner((latent, core, chip, lax.ppermute(chip, "gy", near_y)), coarse_y, coarse_z)
        latent = jnp.swapaxes(latent, 1, 2)
    else:
        split = latent[:, :, : coarse_z * count_y].reshape(coarse_x, latent.shape[1], count_y, coarse_z)
        latent = lax.all_to_all(split, "gy", split_axis=2, concat_axis=1, tiled=True)
        latent = latent.reshape(coarse_x, coarse_y, coarse_z)
    return phase_out, solute_out, latent


def solution(mesh):
    in_specs = (P("gx", "gy", None), P("gx", "gy", None), P("gx", None, "gy"))
    out_specs = (P("gx", "gy", None), P("gx", "gy", None), P("gx", None, "gy"))
    return jax.shard_map(body, mesh=mesh, in_specs=in_specs, out_specs=out_specs, check_vma=False)
```

```python
import functools

import jax
import jax.numpy as jnp
from jax import lax
from jax.experimental import pallas as pl
from jax.experimental.pallas import tpu as pltpu
from jax.sharding import PartitionSpec as P

time_step = 0.1
anisotropy = 0.3
coupling = 2.0
rejection = 0.5

F32 = jnp.float32
HIGHEST = lax.Precision.HIGHEST
HALO = 4
STRIP = 4
ROWS = 8
LANES = 128
VMEM_LIMIT = 24 * 1024 * 1024


def vmem():
    return pl.BlockSpec(memory_space=pltpu.VMEM)


def anywhere():
    return pl.BlockSpec(memory_space=pl.ANY)


def hbm():
    return pl.BlockSpec(memory_space=pltpu.HBM)


def pairs(count, first):
    forward = [((first + k) % count, (first + k + 1) % count) for k in range(0, count, 2)]
    return forward + [(b, a) for a, b in forward]


def flips(me):
    odd = lax.rem(me, 2)
    return me, me + 1 - 2 * odd, lax.rem(me + 2, 4), 3 - me


def row_ids(shape):
    return lax.broadcasted_iota(jnp.int32, shape, len(shape) - 2)


def lane_ids(shape):
    return lax.broadcasted_iota(jnp.int32, shape, len(shape) - 1)


def start_all(copies, sems):
    copies = [pltpu.make_async_copy(source, target, sems.at[n]) for n, (source, target) in enumerate(copies)]
    for copy in copies:
        copy.start()
    return copies


def wait_all(copies):
    for copy in copies:
        copy.wait()


def fold(table):
    half = table.shape[0] // 2
    return jnp.concatenate([table[:half], table[half:]], axis=1)


def unfold(tile):
    return jnp.concatenate([tile[:, :LANES], tile[:, LANES:]], axis=0)


def pack_kernel(
    phase, solute, macro, phase_here, solute_here, face_a, face_b, side_a, strip_b, rest_b, table, local, sems
):
    size_x, size_y, size_z = phase.shape
    odd_x = lax.rem(lax.axis_index("gx"), 2)
    even_y = lax.rem(lax.axis_index("gy"), 2) == 0
    copies = []
    for at in range(0, size_x, HALO):
        for ref, here in ((phase, phase_here), (solute, solute_here)):
            copies.append((ref.at[pl.ds(at, HALO)], here.at[pl.ds(at, HALO)]))
    copies.append((macro, local))
    copies = start_all(copies, sems)
    wait_all(copies)
    for field, here in enumerate((phase_here, solute_here)):
        face_a[field] = here[pl.ds((1 - odd_x) * (size_x - HALO), HALO)]
        face_b[field] = here[pl.ds(odd_x * (size_x - HALO), HALO)]
    low = [here[:, pl.ds(0, ROWS), :] for here in (phase_here, solute_here)]
    high = [here[:, pl.ds(size_y - ROWS, ROWS), :] for here in (phase_here, solute_here)]
    wide = jnp.concatenate([local[k] for k in range(local.shape[0])], axis=1)
    table[...] = wide
    top = row_ids((size_x, ROWS, size_z)) < HALO
    low_side = jnp.where(top, low[0], pltpu.roll(low[1], HALO, 1))
    high_side = jnp.where(top, pltpu.roll(high[1], HALO, 1), high[0])
    side_a[pl.ds(0, size_x)] = jnp.where(even_y, high_side, low_side)
    side_b = jnp.where(even_y, low_side, high_side)
    strip_b[pl.ds(0, STRIP)] = side_b[:STRIP]
    strip_b[pl.ds(STRIP, STRIP)] = side_b[size_x - STRIP :]
    rest_b[...] = side_b[STRIP : size_x - STRIP]
    if side_a.shape[0] > size_x:
        side_a[size_x] = fold(wide)
        strip_b[2 * STRIP] = fold(wide)


def pack(phase, solute, macro, ride):
    size_x, size_y, size_z = phase.shape
    coarse_x, coarse_z, coarse_y = macro.shape
    field = jax.ShapeDtypeStruct(phase.shape, F32)
    face = jax.ShapeDtypeStruct((2, HALO, size_y, size_z), F32)
    counts = (size_x, 2 * STRIP, size_x - 2 * STRIP)
    extra = (1, 2, 0) if ride else (0, 0, 0)
    sides = [jax.ShapeDtypeStruct((count + more, ROWS, size_z), F32) for count, more in zip(counts, extra)]
    table = jax.ShapeDtypeStruct((coarse_z, coarse_x * coarse_y), F32)
    return pl.pallas_call(
        pack_kernel,
        out_shape=(field, field, face, face, *sides, table),
        in_specs=[hbm()] * 3,
        out_specs=[vmem()] * 8,
        scratch_shapes=[pltpu.VMEM(macro.shape, F32), pltpu.SemaphoreType.DMA((1 + 2 * (size_x // HALO),))],
        compiler_params=pltpu.CompilerParams(vmem_limit_bytes=VMEM_LIMIT),
        cost_estimate=pl.CostEstimate(flops=10**5, bytes_accessed=2 * 10**6, transcendentals=0),
        name="pack",
    )(phase, solute, macro)


def append_kernel(arrived, side, out):
    out[side.shape[0] - 1] = arrived[arrived.shape[0] - 1]


def append(arrived, side):
    return pl.pallas_call(
        append_kernel,
        out_shape=jax.ShapeDtypeStruct(side.shape, F32),
        in_specs=[vmem(), vmem()],
        out_specs=vmem(),
        input_output_aliases={1: 0},
        compiler_params=pltpu.CompilerParams(vmem_limit_bytes=VMEM_LIMIT),
        cost_estimate=pl.CostEstimate(flops=0, bytes_accessed=10**5, transcendentals=0),
        name="append",
    )(arrived, side)


def near_rows(block, coarse_y):
    shape = (2 * ROWS, coarse_y)
    wanted = lax.rem(row_ids(shape) + lax.axis_index("gy") * ROWS + coarse_y - 1, coarse_y)
    pick = (lane_ids(shape) == wanted).astype(F32)
    return lax.dot_general(pick, block, (((1,), (1,)), ((), ())), precision=HIGHEST, preferred_element_type=F32)


def pack_edge(rows):
    pieces = rows[:ROWS], pltpu.roll(rows[:ROWS], 4, 0), rows[ROWS:], pltpu.roll(rows[ROWS:], 4, 0)
    return jnp.concatenate(pieces, axis=1)


def unpack_edge(tile):
    quarter = tile.shape[1] // 4
    pieces = [tile[:, at : at + quarter] for at in range(0, tile.shape[1], quarter)]
    top = row_ids(pieces[0].shape) < 4
    halves = [jnp.where(top, pieces[n], pltpu.roll(pieces[n + 1], 4, 0)) for n in (0, 2)]
    return jnp.concatenate(halves, axis=0)


def corner_kernel(coarse_y, gathered, side_a, strip_b, table, coarse, corner_a, corner_b):
    size_x = side_a.shape[0] - (0 if gathered else 1)
    me = lax.axis_index("gy")
    even_x = lax.rem(lax.axis_index("gx"), 2) == 0
    even_y = lax.rem(me, 2) == 0
    block = table[...]
    if not gathered:
        near, across, far = flips(me)[1:]
        depth = table.shape[0]
        tiles = (me, block), (near, unfold(side_a[size_x])), (far, unfold(strip_b[2 * STRIP])), (across, unfold(strip_b[2 * STRIP + 1]))
        for source, tile in tiles:
            coarse[pl.ds(pl.multiple_of(source * depth, depth), depth), :] = tile
        block = coarse[...]
    depth, width = block.shape
    flipped = [block[:, at : at + coarse_y] for at in range(width - coarse_y, -1, -coarse_y)]
    block = jnp.where(even_x, block, jnp.concatenate(flipped, axis=1))
    coarse[...] = block
    row = row_ids(side_a.shape[1:])
    edges = block[:, width - coarse_y :], block[:, :coarse_y]
    for corner, top_side, edge in ((corner_a, even_x, edges[0]), (corner_b, jnp.logical_not(even_x), edges[1])):

        def layer(d, high):
            first = side_a[jnp.where(top_side, size_x - d, d - 1)]
            second = strip_b[jnp.where(top_side, 2 * STRIP - d, d - 1)]
            return jnp.where(even_y, first, second) if high else jnp.where(even_y, second, first)

        spare = pack_edge(near_rows(edge, coarse_y))
        tile = jnp.where(row == 4, pltpu.roll(layer(3, False), 5, 0), layer(1, False))
        corner[0] = jnp.where(row < 2, spare, tile)
        tile = jnp.where(row == 3, pltpu.roll(layer(3, True), 3, 0), layer(1, True))
        corner[1] = jnp.where(row >= 6, pltpu.roll(spare, 4, 0), tile)
        corner[2] = jnp.where(row % 4 < 2, layer(2, True), layer(2, False))


def corners(side_a, strip_b, table, coarse_y, coarse_shape):
    size_z = side_a.shape[2]
    corner = jax.ShapeDtypeStruct((3, ROWS, size_z), F32)
    coarse = jax.ShapeDtypeStruct(coarse_shape, F32)
    return pl.pallas_call(
        functools.partial(corner_kernel, coarse_y, table.shape == coarse_shape),
        out_shape=(coarse, corner, corner),
        in_specs=[vmem()] * 3,
        out_specs=[vmem()] * 3,
        compiler_params=pltpu.CompilerParams(vmem_limit_bytes=VMEM_LIMIT),
        cost_estimate=pl.CostEstimate(flops=10**5, bytes_accessed=4 * 10**5, transcendentals=0),
        name="corners",
    )(side_a, strip_b, table)


def weights(ends, frac, tick):
    first, second = ends
    return jnp.where(tick == first, 1.0 - frac, 0.0) + jnp.where(tick == second, frac, 0.0)


def weights_z(depth, size_z):
    shape = (depth, size_z)
    fine = lane_ids(shape)
    lower = (2 * fine + 5) // 8 - 1
    frac = (2 * fine - 3 - 8 * lower).astype(F32) / 8.0
    ends = jnp.clip(lower, 0, depth - 1), jnp.clip(lower + 1, 0, depth - 1)
    return weights(ends, frac, row_ids(shape))


def interpolate(rows, along_z, size_y):
    deep = jnp.dot(rows, along_z, precision=HIGHEST, preferred_element_type=F32)
    shape = (size_y + 2 * HALO, 2 * ROWS)
    fine = row_ids(shape)
    fine = jnp.where(fine >= size_y + HALO, fine - shape[0], fine)
    lower = (2 * fine + 13) // 8 - 2
    frac = (2 * fine - 3 - 8 * lower).astype(F32) / 8.0
    along_y = weights((lower + 1, lower + 2), frac, lane_ids(shape))
    return [
        jnp.dot(along_y, deep[at : at + 2 * ROWS], precision=HIGHEST, preferred_element_type=F32)
        for at in range(0, rows.shape[0], 2 * ROWS)
    ]


def blend(x, fans):
    lower = (2 * x - 3) // 8
    frac = (2 * x - 3 - 8 * lower) / 8.0
    return (1.0 - frac) * fans[lower] + frac * fans[lower + 1]


def turn(value, by, axis):
    return pltpu.roll(value, by % value.shape[axis], axis)


def z_matrices(size_z):
    shape = (size_z, size_z)
    source, target = row_ids(shape), lane_ids(shape)
    hit = lambda at: (source == at).astype(F32)
    end = size_z - 1
    gradient = hit(jnp.minimum(target + 1, end)) - hit(jnp.maximum(target - 1, 0))
    difference = hit(target + 1) - hit(target - 1)
    laplace = hit(jnp.minimum(target + 2, end)) + hit(jnp.maximum(target - 2, 0)) - 6.0 * hit(target)
    return tuple(m.astype(jnp.bfloat16) for m in (gradient, difference, laplace))


def matrix_kernel(size_z, tile, out, along_z):
    for n, matrix in enumerate(z_matrices(size_z)):
        out[n] = matrix
    along_z[...] = weights_z(*along_z.shape)


def z_products(size_z, tile):
    square = jax.ShapeDtypeStruct((3, size_z, size_z), jnp.bfloat16)
    return pl.pallas_call(
        functools.partial(matrix_kernel, size_z),
        out_shape=(square, jax.ShapeDtypeStruct((size_z // 4, size_z), F32)),
        in_specs=[anywhere()],
        out_specs=[vmem()] * 2,
        compiler_params=pltpu.CompilerParams(vmem_limit_bytes=VMEM_LIMIT),
        cost_estimate=pl.CostEstimate(flops=10**6, bytes_accessed=4 * 10**5, transcendentals=0),
        name="products",
    )(tile)


def along(slabs, matrix):
    value = slabs.reshape(-1, slabs.shape[-1])
    coarse = value.astype(jnp.bfloat16)
    rest = (value - coarse.astype(F32)).astype(jnp.bfloat16)
    product = jnp.dot(coarse, matrix, preferred_element_type=F32) + jnp.dot(rest, matrix, preferred_element_type=F32)
    return product.reshape(slabs.shape)


def flux(before, here, after, along_z):
    along_x = after - before
    along_y = turn(here, -1, 0) - turn(here, 1, 0)
    sq_x = along_x * along_x
    sq_y = along_y * along_y
    both = sq_x + sq_y
    inverse = 1.0 / (both + 4.0)
    factor = 1.0 + anisotropy * (both * both - 8.0 * (sq_x * sq_y)) * (inverse * inverse)
    stiff = (0.25 * time_step) * (factor * factor)
    return stiff * along_x, stiff * along_y, stiff * along_z


def spread(flux_y):
    return turn(flux_y, -1, 0) - turn(flux_y, 1, 0)


def phase_change(here, conc, theta, divergence):
    square = 1.0 - here * here
    drive = square * (here - (coupling * square) * (theta + conc))
    return divergence + time_step * drive


def solute_step(conc, beyond_x, beyond_y, along_z, change):
    return conc + (0.25 * time_step) * (beyond_x + beyond_y + along_z) + rejection * change


def next_row(conc):
    return turn(conc, -2, 0) + turn(conc, 2, 0)


def restrict(change, at, coarse_width):
    size_y, size_z = change.shape
    shape = (size_z // 4, size_z)
    pool_z = (lane_ids(shape) // 4 == row_ids(shape)).astype(F32)
    shape = (size_y, coarse_width)
    pool_y = jnp.where(row_ids(shape) // 4 + at == lane_ids(shape), 0.5 / 64.0, 0.0)
    change = lax.dot_general(
        pool_z, change, (((1,), (1,)), ((), ())), precision=HIGHEST, preferred_element_type=F32
    )
    return jnp.dot(change, pool_y, precision=HIGHEST, preferred_element_type=F32)


def coarse_lane(u, size_x, size_y, coarse_y):
    last = size_x // 4 - 1
    x = u + lax.rem(lax.axis_index("gx"), 2) * (last - 2 * u)
    return x * coarse_y + lax.axis_index("gy") * (size_y // 4)


KEPT = ("p0", "c0", "dz0", "cz0", "gx0", "dv0", "p1", "c1", "dz1", "cz1", "gx1", "dv1", "th")


def spans(size_x):
    widths = dict(p0=0, c0=0, dz0=0, cz0=0, gx0=1, dv0=1, p1=2, c1=2, dz1=2, cz1=2, gx1=3, dv1=3, th=2)
    return {name: (widths[name], size_x - widths[name]) for name in KEPT}


def halo_rows(tile, top):
    zero = jnp.zeros_like(tile[0])
    low = tile[0], tile[2], pltpu.roll(tile[0], 3, 0), zero
    high = tile[1], tile[2], pltpu.roll(tile[1], 5, 0), zero
    return [
        (jnp.where(top, h, l), pltpu.roll(jnp.where(top, l, h), HALO, 0)) for l, h in zip(low, high)
    ]


def inner_kernel(
    coarse_y, phase, solute, side_a, strip_b, rest_b, coarse, matrices, along_z, phase_new, solute_new, latent, ends, *rest
):
    kept = dict(zip(KEPT, rest[: len(KEPT)]))
    (fz,) = rest[len(KEPT) :]
    size_x, size_y, size_z = phase.shape
    span = spans(size_x)
    odd_x = lax.rem(lax.axis_index("gx"), 2)
    even_y = lax.rem(lax.axis_index("gy"), 2) == 0
    at = lambda name, u: kept[name].at[u - span[name][0]]
    get = lambda name, u: kept[name][u - span[name][0]]
    place = lambda u: u + odd_x * (size_x - 1 - 2 * u)
    top = row_ids((ROWS, size_z)) < HALO
    for u in range(size_x):
        first = side_a[place(u)]
        if STRIP <= u < size_x - STRIP:
            second = rest_b[place(u) - STRIP]
        else:
            at_strip = u if u < STRIP else u - size_x + 2 * STRIP
            second = strip_b[at_strip + odd_x * (2 * STRIP - 1 - 2 * at_strip)]
        low, high = jnp.where(even_y, second, first), jnp.where(even_y, first, second)
        at("p0", u)[pl.ds(0, size_y), :] = phase[place(u)]
        at("c0", u)[pl.ds(0, size_y), :] = solute[place(u)]
        at("p0", u)[pl.ds(size_y, ROWS), :] = jnp.where(top, high, low)
        at("c0", u)[pl.ds(size_y, ROWS), :] = pltpu.roll(jnp.where(top, low, high), HALO, 0)
    block = coarse[...]
    block = [near_rows(block[:, at : at + coarse_y], coarse_y) for at in range(0, block.shape[1], coarse_y)]
    fans = dict(enumerate(interpolate(jnp.concatenate(block, axis=0), along_z[...], size_y)))
    ends[0], ends[1] = fans[0], fans[len(fans) - 1]
    for u in range(*span["th"]):
        at("th", u)[...] = blend(u, fans)

    for step in "01":
        p, c, dz, cz, gx, dv = (name + step for name in ("p", "c", "dz", "cz", "gx", "dv"))
        kept[dz][...] = along(kept[p][...], matrices[0])
        kept[cz][...] = along(kept[c][...], matrices[2])
        begin, end = span[gx]
        for u in range(begin, end):
            flux_x, flux_y, flux_z = flux(get(p, u - 1), get(p, u), get(p, u + 1), get(dz, u))
            at(gx, u)[...] = flux_x
            at(dv, u)[...] = spread(flux_y)
            fz[u - begin] = flux_z
        kept[dv][...] += along(fz[pl.ds(0, end - begin)], matrices[1])
        take = (lambda v: v) if step == "0" else (lambda v: v[:size_y])
        for u in range(begin + 1, end - 1):
            here, conc = take(get(p, u)), get(c, u)
            divergence = take(get(gx, u + 1)) - take(get(gx, u - 1)) + take(get(dv, u))
            change = phase_change(here, take(conc), take(get("th", u)), divergence)
            beyond = take(get(c, u + 2)) + take(get(c, u - 2))
            new_conc = solute_step(take(conc), beyond, take(next_row(conc)), take(get(cz, u)), change)
            if step == "0":
                at("p1", u)[...] = here + change
                at("c1", u)[...] = new_conc
            else:
                phase_new[place(u) - HALO] = here + change
                solute_new[place(u) - HALO] = new_conc
    total = jnp.zeros(latent.shape, F32)
    for k in range(1, size_x // 4 - 1):
        change = jnp.zeros((size_y, size_z), F32)
        for u in range(4 * k, 4 * k + 4):
            change = change + (phase_new[place(u) - HALO] - get("p0", u)[:size_y])
        total = total + restrict(change, coarse_lane(k, size_x, size_y, coarse_y), latent.shape[1])
    latent[...] = total


def inner(phase, solute, side_a, strip_b, rest_b, coarse, matrices, along_z, coarse_y):
    size_x, size_y, size_z = phase.shape
    rows = size_y + 2 * HALO
    part = jax.ShapeDtypeStruct((size_x - 2 * HALO, size_y, size_z), F32)
    kept = [jax.ShapeDtypeStruct((end - begin, rows, size_z), F32) for begin, end in spans(size_x).values()]
    latent = jax.ShapeDtypeStruct((size_z // 4, coarse.shape[1]), F32)
    return pl.pallas_call(
        functools.partial(inner_kernel, coarse_y),
        out_shape=(part, part, latent, jax.ShapeDtypeStruct((2, rows, size_z), F32), *kept),
        in_specs=[vmem()] * 8,
        out_specs=[vmem()] * (4 + len(kept)),
        scratch_shapes=[pltpu.VMEM((size_x - 2, rows, size_z), F32)],
        compiler_params=pltpu.CompilerParams(vmem_limit_bytes=VMEM_LIMIT),
        cost_estimate=pl.CostEstimate(flops=10 * 10**8, bytes_accessed=10 * 10**6, transcendentals=0),
        name="inner",
    )(phase, solute, side_a, strip_b, rest_b, coarse, matrices, along_z)


def rim_steps(
    coarse_y, width, near, size_x, face, corner, fans, matrices, along_z, kept, scratch, phase_new, solute_new
):
    hp0, hc0, p1, c1, gx, dv, dz, cz, fz, th = scratch
    _, size_y, size_z = phase_new.shape
    span = spans(size_x)
    odd_x = lax.rem(lax.axis_index("gx"), 2)
    flip = odd_x if near else 1 - odd_x
    spot = lambda v: v + (1 - flip) * (HALO - 1 - 2 * v)
    top = row_ids((ROWS, size_z)) < HALO
    for d, (p_rows, c_rows) in enumerate(halo_rows(corner, top)):
        layer = d + flip * (HALO - 1 - 2 * d)
        for n, (field, rows) in enumerate(((hp0, p_rows), (hc0, c_rows))):
            field[HALO - 1 - d, pl.ds(0, size_y), :] = face[n, layer]
            field[HALO - 1 - d, pl.ds(size_y, ROWS), :] = rows
    edge = jnp.where(row_ids(corner.shape[1:]) < 2, corner[0], pltpu.roll(corner[1], 4, 0))
    fans = {-1: interpolate(unpack_edge(edge), along_z[...], size_y)[0], 0: fans[1 if near else 0]}
    for v in range(-2, 2):
        th[v + 2] = blend(v, fans)

    def get(name, v):
        begin, end = span[name]
        if v >= begin:
            found = kept[name][(size_x - 1 - v if near else v) - begin]
            return -found if near and name.startswith("gx") else found
        own, first = dict(
            p0=(hp0, -4), c0=(hc0, -4), dz0=(dz, -3), cz0=(cz, -2), gx0=(gx, -3), dv0=(dv, -2),
            p1=(p1, -2), c1=(c1, -2), dz1=(dz, -1), cz1=(cz, 0), gx1=(gx, -1), dv1=(dv, 0), th=(th, -2),
        )[name]
        return own[v - first]

    for step, begin in (("0", -3), ("1", -1)):
        p, c, gx_, dv_, dz_, cz_ = (name + step for name in ("p", "c", "gx", "dv", "dz", "cz"))
        fields = (hp0[pl.ds(1, 3)], hc0[pl.ds(2, 2)]) if step == "0" else (p1[pl.ds(1, 3)], c1[pl.ds(2, 2)])
        dz[...] = along(fields[0], matrices[0])
        cz[...] = along(fields[1], matrices[2])
        for v in range(begin, begin + 4):
            flux_x, flux_y, flux_z = flux(get(p, v - 1), get(p, v), get(p, v + 1), get(dz_, v))
            gx[v - begin] = flux_x
            if v > begin:
                dv[v - begin - 1] = spread(flux_y)
                fz[v - begin - 1] = flux_z
        dv[...] += along(fz[...], matrices[1])
        take = (lambda w: w) if step == "0" else (lambda w: w[:size_y])
        for v in range(begin + 1, begin + 5):
            here, conc = take(get(p, v)), get(c, v)
            divergence = take(get(gx_, v + 1)) - take(get(gx_, v - 1)) + take(get(dv_, v))
            change = phase_change(here, take(conc), take(get("th", v)), divergence)
            beyond = take(get(c, v + 2)) + take(get(c, v - 2))
            new_conc = solute_step(take(conc), beyond, take(next_row(conc)), take(get(cz_, v)), change)
            if step == "0":
                p1[v + 2], c1[v + 2] = here + change, new_conc
            else:
                phase_new[spot(v)], solute_new[spot(v)] = here + change, new_conc
    change = jnp.zeros((size_y, size_z), F32)
    for v in range(HALO):
        change = change + (phase_new[spot(v)] - get("p0", v)[:size_y])
    u = size_x // 4 - 1 if near else 0
    return restrict(change, coarse_lane(u, size_x, size_y, coarse_y), width)


def near_kernel(coarse_y, size_x, face, corner, fans, matrices, along_z, *rest):
    kept = dict(zip(KEPT, rest[: len(KEPT)]))
    phase_new, solute_new, latent = rest[len(KEPT) : len(KEPT) + 3]
    latent[...] = rim_steps(
        coarse_y, latent.shape[1], True, size_x, face, corner, fans, matrices, along_z, kept,
        rest[len(KEPT) + 3 :], phase_new, solute_new,
    )


def far_kernel(coarse_y, size_x, face, corner, fans, matrices, along_z, inner_latent, near_latent, *rest):
    kept = dict(zip(KEPT, rest[: len(KEPT)]))
    phase_new, solute_new, keep, send, *scratch, total = rest[len(KEPT) :]
    mine = rim_steps(
        coarse_y, total.shape[1], False, size_x, face, corner, fans, matrices, along_z, kept, scratch, phase_new,
        solute_new,
    )
    total[...] = mine + inner_latent[...] + near_latent[...]
    halve(total, lax.div(2 * lax.axis_index("gy"), lax.axis_size("gy")), keep, send)


def halve(total, side, keep, send):
    half = keep.shape[0]
    keep[...] = total[pl.ds(pl.multiple_of(side * half, half), half), :]
    send[...] = total[pl.ds(pl.multiple_of((1 - side) * half, half), half), :]


def rim_scratch(size_y, size_z):
    counts = 4, 4, 4, 4, 4, 3, 3, 2, 3, 4
    return [pltpu.VMEM((count, size_y + 2 * HALO, size_z), F32) for count in counts]


def near_rim(shape, face, corner, fans, matrices, along_z, kept, width, coarse_y):
    size_x, size_y, size_z = shape
    part = jax.ShapeDtypeStruct((HALO, size_y, size_z), F32)
    return pl.pallas_call(
        functools.partial(near_kernel, coarse_y, size_x),
        out_shape=(part, part, jax.ShapeDtypeStruct((size_z // 4, width), F32)),
        in_specs=[vmem()] * (5 + len(kept)),
        out_specs=[vmem()] * 3,
        scratch_shapes=rim_scratch(size_y, size_z),
        compiler_params=pltpu.CompilerParams(vmem_limit_bytes=VMEM_LIMIT),
        cost_estimate=pl.CostEstimate(flops=20 * 10**8, bytes_accessed=20 * 10**6, transcendentals=0),
        name="near",
    )(face, corner, fans, matrices, along_z, *kept)


def far_rim(shape, face, corner, fans, matrices, along_z, inner_latent, near_latent, kept, coarse_y):
    size_x, size_y, size_z = shape
    part = jax.ShapeDtypeStruct((HALO, size_y, size_z), F32)
    width = inner_latent.shape[1]
    half = jax.ShapeDtypeStruct((size_z // 8, width), F32)
    return pl.pallas_call(
        functools.partial(far_kernel, coarse_y, size_x),
        out_shape=(part, part, half, half),
        in_specs=[vmem()] * (7 + len(kept)),
        out_specs=[vmem()] * 4,
        scratch_shapes=[*rim_scratch(size_y, size_z), pltpu.VMEM((size_z // 4, width), F32)],
        compiler_params=pltpu.CompilerParams(vmem_limit_bytes=VMEM_LIMIT),
        cost_estimate=pl.CostEstimate(flops=10**7, bytes_accessed=3 * 10**6, transcendentals=0),
        name="far",
    )(face, corner, fans, matrices, along_z, inner_latent, near_latent, *kept)


def store_kernel(*refs):
    parts, (phase_out, solute_out, sems) = refs[:6], refs[6:]
    size_x = phase_out.shape[0]
    odd_x = lax.rem(lax.axis_index("gx"), 2)
    near = (1 - odd_x) * (size_x - HALO)
    copies = []
    for begin, pair in ((HALO, parts[:2]), (near, parts[2:4]), (size_x - HALO - near, parts[4:])):
        for part, out in zip(pair, (phase_out, solute_out)):
            copies.append((part, out.at[pl.ds(begin, part.shape[0])]))
    wait_all(start_all(copies, sems))


def store(shape, parts):
    out = jax.ShapeDtypeStruct(shape, F32)
    return pl.pallas_call(
        store_kernel,
        out_shape=(out, out),
        in_specs=[vmem()] * 6,
        out_specs=[hbm()] * 2,
        scratch_shapes=[pltpu.SemaphoreType.DMA((6,))],
        compiler_params=pltpu.CompilerParams(vmem_limit_bytes=VMEM_LIMIT),
        cost_estimate=pl.CostEstimate(flops=0, bytes_accessed=4 * 10**6, transcendentals=0),
        name="store",
    )(*parts)


def merge_kernel(mine, arrived, keep, send, total):
    total[...] = mine[...] + arrived[...]
    halve(total, lax.rem(lax.axis_index("gy"), 2), keep, send)


def merge(mine, arrived):
    half = jax.ShapeDtypeStruct((mine.shape[0] // 2, mine.shape[1]), F32)
    return pl.pallas_call(
        merge_kernel,
        out_shape=(half, half),
        in_specs=[vmem()] * 2,
        out_specs=[vmem()] * 2,
        scratch_shapes=[pltpu.VMEM(mine.shape, F32)],
        compiler_params=pltpu.CompilerParams(vmem_limit_bytes=VMEM_LIMIT),
        cost_estimate=pl.CostEstimate(flops=10**4, bytes_accessed=10**5, transcendentals=0),
        name="merge",
    )(mine, arrived)


def owner_kernel(mine, arrived, out):
    total = mine[...] + arrived[...]
    coarse_x, _, coarse_y = out.shape
    for k in range(coarse_x):
        out[k] = total[:, k * coarse_y : (k + 1) * coarse_y]


def owner(mine, arrived, coarse_x, coarse_y):
    coarse_z = mine.shape[0]
    return pl.pallas_call(
        owner_kernel,
        out_shape=jax.ShapeDtypeStruct((coarse_x, coarse_z, coarse_y), F32),
        in_specs=[vmem()] * 2,
        out_specs=vmem(),
        compiler_params=pltpu.CompilerParams(vmem_limit_bytes=VMEM_LIMIT),
        cost_estimate=pl.CostEstimate(flops=10**4, bytes_accessed=10**5, transcendentals=0),
        name="owner",
    )(mine, arrived)


def body(phase, solute, macro_temp):
    count_x, count_y = lax.axis_size("gx"), lax.axis_size("gy")
    coarse_x, coarse_y, coarse_z = macro_temp.shape
    near_x, far_x = pairs(count_x, 0), pairs(count_x, 1)
    near_y, far_y = pairs(count_y, 0), pairs(count_y, 1)
    across = [(k, (k + count_y // 2) % count_y) for k in range(count_y)]
    ride = count_y == 4
    macro = jnp.swapaxes(macro_temp, 1, 2)
    still = [pltpu.with_memory_space_constraint(v, pltpu.HBM) for v in (phase, solute, macro)]
    phase, solute, face_a, face_b, side_a, strip_b, rest_b, table = pack(*still, ride)
    coarse_shape = (coarse_z * count_y, coarse_x * coarse_y)
    face_a = lax.ppermute(face_a, "gx", near_x)
    side_a = lax.ppermute(side_a, "gy", near_y)
    if ride:
        strip_b = append(side_a, strip_b)
    else:
        table = lax.all_gather(table, "gy").reshape(coarse_shape)
    matrices, along_z = z_products(phase.shape[2], strip_b)
    face_b, rest_b, matrices = lax.optimization_barrier((face_b, rest_b, matrices))
    strip_b = lax.ppermute(strip_b, "gy", far_y)
    rest_b = lax.ppermute(rest_b, "gy", far_y)
    face_b = lax.ppermute(face_b, "gx", far_x)
    coarse, corner_a, corner_b = corners(side_a, strip_b, table, coarse_y, coarse_shape)
    corner_a = lax.ppermute(corner_a, "gx", near_x)
    corner_b = lax.ppermute(corner_b, "gx", far_x)
    results = inner(phase, solute, side_a, strip_b, rest_b, coarse, matrices, along_z, coarse_y)
    middle, inner_latent, fans, kept = results[:2], results[2], results[3], results[4:]
    *near, near_latent = near_rim(
        phase.shape, face_a, corner_a, fans, matrices, along_z, kept, coarse_shape[1], coarse_y
    )
    *far, mine, send = far_rim(
        phase.shape, face_b, corner_b, fans, matrices, along_z, inner_latent, near_latent, kept, coarse_y
    )
    phase_out, solute_out = store(phase.shape, (*middle, *near, *far))
    if ride:
        mine, send = merge(mine, lax.ppermute(send, "gy", across))
        latent = owner(mine, lax.ppermute(send, "gy", near_y), coarse_x, coarse_y)
    else:
        low = lax.axis_index("gy") < count_y // 2
        total = jnp.concatenate([jnp.where(low, mine, send), jnp.where(low, send, mine)])
        latent = lax.psum_scatter(total, "gy", scatter_dimension=0, tiled=True)
        latent = jnp.swapaxes(latent.reshape(coarse_z, coarse_x, coarse_y), 0, 1)
    latent = jnp.swapaxes(latent, 1, 2)
    return phase_out, solute_out, latent


def solution(mesh):
    in_specs = (P("gx", "gy", None), P("gx", "gy", None), P("gx", None, "gy"))
    out_specs = (P("gx", "gy", None), P("gx", "gy", None), P("gx", None, "gy"))
    return jax.shard_map(body, mesh=mesh, in_specs=in_specs, out_specs=out_specs, check_vma=False)
```

```python
import functools

import jax
import jax.numpy as jnp
from jax import lax
from jax.experimental import pallas as pl
from jax.experimental.pallas import tpu as pltpu
from jax.sharding import PartitionSpec as P

time_step = 0.1
anisotropy = 0.3
coupling = 2.0
rejection = 0.5

F32 = jnp.float32
HALO = 4
STRIP = 4
ROWS = 8
LANES = 128
VMEM_LIMIT = 24 * 1024 * 1024


def vmem():
    return pl.BlockSpec(memory_space=pltpu.VMEM)


def anywhere():
    return pl.BlockSpec(memory_space=pl.ANY)


def hbm():
    return pl.BlockSpec(memory_space=pltpu.HBM)


def pairs(count, first):
    forward = [((first + k) % count, (first + k + 1) % count) for k in range(0, count, 2)]
    return forward + [(b, a) for a, b in forward]


def flips(me):
    odd = lax.rem(me, 2)
    return me, me + 1 - 2 * odd, lax.rem(me + 2, 4), 3 - me


def halves(value):
    coarse = value.astype(jnp.bfloat16)
    return coarse, (value - coarse.astype(F32)).astype(jnp.bfloat16)


def product(left, right, contract):
    dot = lambda a, b: lax.dot_general(a, b, ((contract[:1], contract[1:]), ((), ())), preferred_element_type=F32)
    if left.dtype == jnp.bfloat16:
        parts = [dot(left, part) for part in halves(right)]
    else:
        parts = [dot(part, right) for part in halves(left)]
    return parts[0] + parts[1]


def row_ids(shape):
    return lax.broadcasted_iota(jnp.int32, shape, len(shape) - 2)


def lane_ids(shape):
    return lax.broadcasted_iota(jnp.int32, shape, len(shape) - 1)


def start_all(copies, sems):
    copies = [pltpu.make_async_copy(source, target, sems.at[n]) for n, (source, target) in enumerate(copies)]
    for copy in copies:
        copy.start()
    return copies


def wait_all(copies):
    for copy in copies:
        copy.wait()


def fold(table):
    half = table.shape[0] // 2
    return jnp.concatenate([table[:half], table[half:]], axis=1)


def unfold(tile):
    return jnp.concatenate([tile[:, :LANES], tile[:, LANES:]], axis=0)


def pack_kernel(
    phase, solute, macro, phase_here, solute_here, face_a, face_b, side_a, strip_b, rest_b, table, local, sems
):
    size_x, size_y, size_z = phase.shape
    odd_x = lax.rem(lax.axis_index("gx"), 2)
    even_y = lax.rem(lax.axis_index("gy"), 2) == 0
    copies = []
    for at in range(0, size_x, HALO):
        for ref, here in ((phase, phase_here), (solute, solute_here)):
            copies.append((ref.at[pl.ds(at, HALO)], here.at[pl.ds(at, HALO)]))
    copies.append((macro, local))
    copies = start_all(copies, sems)
    wait_all(copies)
    for field, here in enumerate((phase_here, solute_here)):
        face_a[field] = here[pl.ds((1 - odd_x) * (size_x - HALO), HALO)]
        face_b[field] = here[pl.ds(odd_x * (size_x - HALO), HALO)]
    low = [here[:, pl.ds(0, ROWS), :] for here in (phase_here, solute_here)]
    high = [here[:, pl.ds(size_y - ROWS, ROWS), :] for here in (phase_here, solute_here)]
    wide = jnp.concatenate([local[k] for k in range(local.shape[0])], axis=1)
    table[...] = wide
    top = row_ids((size_x, ROWS, size_z)) < HALO
    low_side = jnp.where(top, low[0], pltpu.roll(low[1], HALO, 1))
    high_side = jnp.where(top, pltpu.roll(high[1], HALO, 1), high[0])
    side_a[pl.ds(0, size_x)] = jnp.where(even_y, high_side, low_side)
    side_b = jnp.where(even_y, low_side, high_side)
    strip_b[pl.ds(0, STRIP)] = side_b[:STRIP]
    strip_b[pl.ds(STRIP, STRIP)] = side_b[size_x - STRIP :]
    rest_b[...] = side_b[STRIP : size_x - STRIP]
    if side_a.shape[0] > size_x:
        side_a[size_x] = fold(wide)
        strip_b[2 * STRIP] = fold(wide)


def pack(phase, solute, macro, ride):
    size_x, size_y, size_z = phase.shape
    coarse_x, coarse_z, coarse_y = macro.shape
    field = jax.ShapeDtypeStruct(phase.shape, F32)
    face = jax.ShapeDtypeStruct((2, HALO, size_y, size_z), F32)
    counts = (size_x, 2 * STRIP, size_x - 2 * STRIP)
    extra = (1, 2, 0) if ride else (0, 0, 0)
    sides = [jax.ShapeDtypeStruct((count + more, ROWS, size_z), F32) for count, more in zip(counts, extra)]
    table = jax.ShapeDtypeStruct((coarse_z, coarse_x * coarse_y), F32)
    return pl.pallas_call(
        pack_kernel,
        out_shape=(field, field, face, face, *sides, table),
        in_specs=[hbm()] * 3,
        out_specs=[vmem()] * 8,
        scratch_shapes=[pltpu.VMEM(macro.shape, F32), pltpu.SemaphoreType.DMA((1 + 2 * (size_x // HALO),))],
        compiler_params=pltpu.CompilerParams(vmem_limit_bytes=VMEM_LIMIT),
        cost_estimate=pl.CostEstimate(flops=10**5, bytes_accessed=2 * 10**6, transcendentals=0),
        name="pack",
    )(phase, solute, macro)


def append_kernel(arrived, side, out):
    out[side.shape[0] - 1] = arrived[arrived.shape[0] - 1]


def append(arrived, side):
    return pl.pallas_call(
        append_kernel,
        out_shape=jax.ShapeDtypeStruct(side.shape, F32),
        in_specs=[vmem(), vmem()],
        out_specs=vmem(),
        input_output_aliases={1: 0},
        compiler_params=pltpu.CompilerParams(vmem_limit_bytes=VMEM_LIMIT),
        cost_estimate=pl.CostEstimate(flops=0, bytes_accessed=10**5, transcendentals=0),
        name="append",
    )(arrived, side)


def near_rows(block, coarse_y):
    shape = (2 * ROWS, coarse_y)
    wanted = lax.rem(row_ids(shape) + lax.axis_index("gy") * ROWS + coarse_y - 1, coarse_y)
    pick = (lane_ids(shape) == wanted).astype(F32).astype(jnp.bfloat16)
    return product(pick, block, (1, 1))


def pack_edge(rows):
    pieces = rows[:ROWS], pltpu.roll(rows[:ROWS], 4, 0), rows[ROWS:], pltpu.roll(rows[ROWS:], 4, 0)
    return jnp.concatenate(pieces, axis=1)


def unpack_edge(tile):
    quarter = tile.shape[1] // 4
    pieces = [tile[:, at : at + quarter] for at in range(0, tile.shape[1], quarter)]
    top = row_ids(pieces[0].shape) < 4
    halves = [jnp.where(top, pieces[n], pltpu.roll(pieces[n + 1], 4, 0)) for n in (0, 2)]
    return jnp.concatenate(halves, axis=0)


def corner_kernel(coarse_y, gathered, side_a, strip_b, table, coarse, corner_a, corner_b):
    size_x = side_a.shape[0] - (0 if gathered else 1)
    me = lax.axis_index("gy")
    even_x = lax.rem(lax.axis_index("gx"), 2) == 0
    even_y = lax.rem(me, 2) == 0
    block = table[...]
    if not gathered:
        near, across, far = flips(me)[1:]
        depth = table.shape[0]
        tiles = (me, block), (near, unfold(side_a[size_x])), (far, unfold(strip_b[2 * STRIP])), (across, unfold(strip_b[2 * STRIP + 1]))
        for source, tile in tiles:
            coarse[pl.ds(pl.multiple_of(source * depth, depth), depth), :] = tile
        block = coarse[...]
    depth, width = block.shape
    flipped = [block[:, at : at + coarse_y] for at in range(width - coarse_y, -1, -coarse_y)]
    block = jnp.where(even_x, block, jnp.concatenate(flipped, axis=1))
    coarse[...] = block
    row = row_ids(side_a.shape[1:])
    edges = block[:, width - coarse_y :], block[:, :coarse_y]
    for corner, top_side, edge in ((corner_a, even_x, edges[0]), (corner_b, jnp.logical_not(even_x), edges[1])):

        def layer(d, high):
            first = side_a[jnp.where(top_side, size_x - d, d - 1)]
            second = strip_b[jnp.where(top_side, 2 * STRIP - d, d - 1)]
            return jnp.where(even_y, first, second) if high else jnp.where(even_y, second, first)

        spare = pack_edge(near_rows(edge, coarse_y))
        tile = jnp.where(row == 4, pltpu.roll(layer(3, False), 5, 0), layer(1, False))
        corner[0] = jnp.where(row < 2, spare, tile)
        tile = jnp.where(row == 3, pltpu.roll(layer(3, True), 3, 0), layer(1, True))
        corner[1] = jnp.where(row >= 6, pltpu.roll(spare, 4, 0), tile)
        corner[2] = jnp.where(row % 4 < 2, layer(2, True), layer(2, False))


def corners(side_a, strip_b, table, coarse_y, coarse_shape):
    size_z = side_a.shape[2]
    corner = jax.ShapeDtypeStruct((3, ROWS, size_z), F32)
    coarse = jax.ShapeDtypeStruct(coarse_shape, F32)
    return pl.pallas_call(
        functools.partial(corner_kernel, coarse_y, table.shape == coarse_shape),
        out_shape=(coarse, corner, corner),
        in_specs=[vmem()] * 3,
        out_specs=[vmem()] * 3,
        compiler_params=pltpu.CompilerParams(vmem_limit_bytes=VMEM_LIMIT),
        cost_estimate=pl.CostEstimate(flops=10**5, bytes_accessed=4 * 10**5, transcendentals=0),
        name="corners",
    )(side_a, strip_b, table)


def weights(ends, frac, tick):
    first, second = ends
    return jnp.where(tick == first, 1.0 - frac, 0.0) + jnp.where(tick == second, frac, 0.0)


def weights_z(depth, size_z):
    shape = (depth, size_z)
    fine = lane_ids(shape)
    lower = (2 * fine + 5) // 8 - 1
    frac = (2 * fine - 3 - 8 * lower).astype(F32) / 8.0
    ends = jnp.clip(lower, 0, depth - 1), jnp.clip(lower + 1, 0, depth - 1)
    return weights(ends, frac, row_ids(shape))


def interpolate(rows, along_z, size_y):
    deep = product(rows, along_z, (1, 0))
    shape = (size_y + 2 * HALO, 2 * ROWS)
    fine = row_ids(shape)
    fine = jnp.where(fine >= size_y + HALO, fine - shape[0], fine)
    lower = (2 * fine + 13) // 8 - 2
    frac = (2 * fine - 3 - 8 * lower).astype(F32) / 8.0
    along_y = weights((lower + 1, lower + 2), frac, lane_ids(shape)).astype(jnp.bfloat16)
    return [
        product(along_y, deep[at : at + 2 * ROWS], (1, 0))
        for at in range(0, rows.shape[0], 2 * ROWS)
    ]


def blend(x, fans):
    lower = (2 * x - 3) // 8
    frac = (2 * x - 3 - 8 * lower) / 8.0
    return (1.0 - frac) * fans[lower] + frac * fans[lower + 1]


def turn(value, by, axis):
    return pltpu.roll(value, by % value.shape[axis], axis)


def z_matrices(size_z):
    shape = (size_z, size_z)
    source, target = row_ids(shape), lane_ids(shape)
    hit = lambda at: (source == at).astype(F32)
    end = size_z - 1
    gradient = hit(jnp.minimum(target + 1, end)) - hit(jnp.maximum(target - 1, 0))
    difference = hit(target + 1) - hit(target - 1)
    laplace = hit(jnp.minimum(target + 2, end)) + hit(jnp.maximum(target - 2, 0)) - 6.0 * hit(target)
    return tuple(m.astype(jnp.bfloat16) for m in (gradient, difference, laplace))


def matrix_kernel(size_z, tile, out, along_z):
    for n, matrix in enumerate(z_matrices(size_z)):
        out[n] = matrix
    along_z[...] = weights_z(*along_z.shape).astype(jnp.bfloat16)


def z_products(size_z, tile):
    square = jax.ShapeDtypeStruct((3, size_z, size_z), jnp.bfloat16)
    return pl.pallas_call(
        functools.partial(matrix_kernel, size_z),
        out_shape=(square, jax.ShapeDtypeStruct((size_z // 4, size_z), jnp.bfloat16)),
        in_specs=[anywhere()],
        out_specs=[vmem()] * 2,
        compiler_params=pltpu.CompilerParams(vmem_limit_bytes=VMEM_LIMIT),
        cost_estimate=pl.CostEstimate(flops=10**6, bytes_accessed=4 * 10**5, transcendentals=0),
        name="products",
    )(tile)


def along(slabs, matrix):
    return product(slabs.reshape(-1, slabs.shape[-1]), matrix, (1, 0)).reshape(slabs.shape)


def flux(before, here, after, along_z):
    along_x = after - before
    along_y = turn(here, -1, 0) - turn(here, 1, 0)
    sq_x = along_x * along_x
    sq_y = along_y * along_y
    both = sq_x + sq_y
    inverse = 1.0 / (both + 4.0)
    factor = 1.0 + anisotropy * (both * both - 8.0 * (sq_x * sq_y)) * (inverse * inverse)
    stiff = (0.25 * time_step) * (factor * factor)
    return stiff * along_x, stiff * along_y, stiff * along_z


def spread(flux_y):
    return turn(flux_y, -1, 0) - turn(flux_y, 1, 0)


def phase_change(here, conc, theta, divergence):
    square = 1.0 - here * here
    drive = square * (here - (coupling * square) * (theta + conc))
    return divergence + time_step * drive


def solute_step(conc, beyond_x, beyond_y, along_z, change):
    return conc + (0.25 * time_step) * (beyond_x + beyond_y + along_z) + rejection * change


def next_row(conc):
    return turn(conc, -2, 0) + turn(conc, 2, 0)


def restrict(changes, lanes, size_y, size_z, coarse_width):
    shape = (size_z // 4, size_z)
    pool_z = (lane_ids(shape) // 4 == row_ids(shape)).astype(F32).astype(jnp.bfloat16)
    shape = (size_y, coarse_width)
    cell, lane = row_ids(shape) // 4, lane_ids(shape)
    pool_y = [jnp.where(cell + at == lane, 0.5 / 64.0, 0.0).astype(jnp.bfloat16) for at in lanes]
    pooled = product(pool_z, jnp.concatenate(changes, axis=0), (1, 1))
    return product(pooled, jnp.concatenate(pool_y, axis=0), (1, 0))


def coarse_lane(u, size_x, size_y, coarse_y):
    last = size_x // 4 - 1
    x = u + lax.rem(lax.axis_index("gx"), 2) * (last - 2 * u)
    return x * coarse_y + lax.axis_index("gy") * (size_y // 4)


KEPT = ("p0", "c0", "dz0", "cz0", "gx0", "dv0", "p1", "c1", "dz1", "cz1", "gx1", "dv1", "th")


def spans(size_x):
    widths = dict(p0=0, c0=0, dz0=0, cz0=0, gx0=1, dv0=1, p1=2, c1=2, dz1=2, cz1=2, gx1=3, dv1=3, th=2)
    return {name: (widths[name], size_x - widths[name]) for name in KEPT}


def halo_rows(tile, top):
    zero = jnp.zeros_like(tile[0])
    low = tile[0], tile[2], pltpu.roll(tile[0], 3, 0), zero
    high = tile[1], tile[2], pltpu.roll(tile[1], 5, 0), zero
    return [
        (jnp.where(top, h, l), pltpu.roll(jnp.where(top, l, h), HALO, 0)) for l, h in zip(low, high)
    ]


def inner_kernel(
    coarse_y, phase, solute, side_a, strip_b, rest_b, coarse, matrices, along_z, phase_new, solute_new, latent, ends, *rest
):
    kept = dict(zip(KEPT, rest[: len(KEPT)]))
    (fz,) = rest[len(KEPT) :]
    size_x, size_y, size_z = phase.shape
    span = spans(size_x)
    odd_x = lax.rem(lax.axis_index("gx"), 2)
    even_y = lax.rem(lax.axis_index("gy"), 2) == 0
    at = lambda name, u: kept[name].at[u - span[name][0]]
    get = lambda name, u: kept[name][u - span[name][0]]
    place = lambda u: u + odd_x * (size_x - 1 - 2 * u)
    top = row_ids((ROWS, size_z)) < HALO
    for u in range(size_x):
        first = side_a[place(u)]
        if STRIP <= u < size_x - STRIP:
            second = rest_b[place(u) - STRIP]
        else:
            at_strip = u if u < STRIP else u - size_x + 2 * STRIP
            second = strip_b[at_strip + odd_x * (2 * STRIP - 1 - 2 * at_strip)]
        low, high = jnp.where(even_y, second, first), jnp.where(even_y, first, second)
        at("p0", u)[pl.ds(0, size_y), :] = phase[place(u)]
        at("c0", u)[pl.ds(0, size_y), :] = solute[place(u)]
        at("p0", u)[pl.ds(size_y, ROWS), :] = jnp.where(top, high, low)
        at("c0", u)[pl.ds(size_y, ROWS), :] = pltpu.roll(jnp.where(top, low, high), HALO, 0)
    block = coarse[...]
    block = [near_rows(block[:, at : at + coarse_y], coarse_y) for at in range(0, block.shape[1], coarse_y)]
    fans = dict(enumerate(interpolate(jnp.concatenate(block, axis=0), along_z[...], size_y)))
    ends[0], ends[1] = fans[0], fans[len(fans) - 1]
    for u in range(*span["th"]):
        at("th", u)[...] = blend(u, fans)

    for step in "01":
        p, c, dz, cz, gx, dv = (name + step for name in ("p", "c", "dz", "cz", "gx", "dv"))
        kept[dz][...] = along(kept[p][...], matrices[0])
        kept[cz][...] = along(kept[c][...], matrices[2])
        begin, end = span[gx]
        for u in range(begin, end):
            flux_x, flux_y, flux_z = flux(get(p, u - 1), get(p, u), get(p, u + 1), get(dz, u))
            at(gx, u)[...] = flux_x
            at(dv, u)[...] = spread(flux_y)
            fz[u - begin] = flux_z
        kept[dv][...] += along(fz[pl.ds(0, end - begin)], matrices[1])
        take = (lambda v: v) if step == "0" else (lambda v: v[:size_y])
        for u in range(begin + 1, end - 1):
            here, conc = take(get(p, u)), get(c, u)
            divergence = take(get(gx, u + 1)) - take(get(gx, u - 1)) + take(get(dv, u))
            change = phase_change(here, take(conc), take(get("th", u)), divergence)
            beyond = take(get(c, u + 2)) + take(get(c, u - 2))
            new_conc = solute_step(take(conc), beyond, take(next_row(conc)), take(get(cz, u)), change)
            if step == "0":
                at("p1", u)[...] = here + change
                at("c1", u)[...] = new_conc
            else:
                phase_new[place(u) - HALO] = here + change
                solute_new[place(u) - HALO] = new_conc
    changes, lanes = [], []
    for k in range(1, size_x // 4 - 1):
        change = jnp.zeros((size_y, size_z), F32)
        for u in range(4 * k, 4 * k + 4):
            change = change + (phase_new[place(u) - HALO] - get("p0", u)[:size_y])
        changes.append(change)
        lanes.append(coarse_lane(k, size_x, size_y, coarse_y))
    latent[...] = restrict(changes, lanes, size_y, size_z, latent.shape[1])


def inner(phase, solute, side_a, strip_b, rest_b, coarse, matrices, along_z, coarse_y):
    size_x, size_y, size_z = phase.shape
    rows = size_y + 2 * HALO
    part = jax.ShapeDtypeStruct((size_x - 2 * HALO, size_y, size_z), F32)
    kept = [jax.ShapeDtypeStruct((end - begin, rows, size_z), F32) for begin, end in spans(size_x).values()]
    latent = jax.ShapeDtypeStruct((size_z // 4, coarse.shape[1]), F32)
    return pl.pallas_call(
        functools.partial(inner_kernel, coarse_y),
        out_shape=(part, part, latent, jax.ShapeDtypeStruct((2, rows, size_z), F32), *kept),
        in_specs=[vmem()] * 8,
        out_specs=[vmem()] * (4 + len(kept)),
        scratch_shapes=[pltpu.VMEM((size_x - 2, rows, size_z), F32)],
        compiler_params=pltpu.CompilerParams(vmem_limit_bytes=VMEM_LIMIT),
        cost_estimate=pl.CostEstimate(flops=5 * 10**8, bytes_accessed=5 * 10**6, transcendentals=0),
        name="inner",
    )(phase, solute, side_a, strip_b, rest_b, coarse, matrices, along_z)


def rim_halo(near, face, corner, along_z, phase_halo, solute_halo, fan):
    _, _, size_y, size_z = face.shape
    odd_x = lax.rem(lax.axis_index("gx"), 2)
    flip = odd_x if near else 1 - odd_x
    top = row_ids((ROWS, size_z)) < HALO
    for d, (p_rows, c_rows) in enumerate(halo_rows(corner, top)):
        layer = d + flip * (HALO - 1 - 2 * d)
        for n, (field, rows) in enumerate(((phase_halo, p_rows), (solute_halo, c_rows))):
            field[HALO - 1 - d, pl.ds(0, size_y), :] = face[n, layer]
            field[HALO - 1 - d, pl.ds(size_y, ROWS), :] = rows
    edge = jnp.where(row_ids(corner.shape[1:]) < 2, corner[0], pltpu.roll(corner[1], 4, 0))
    fan[...] = interpolate(unpack_edge(edge), along_z[...], size_y)[0]


def rim_march(near, size_x, halo, fans, matrices, kept, scratch, phase_new, solute_new, result):
    hp0, hc0, fan = halo
    p1, c1, gx, dv, dz, cz, fz, th = scratch
    _, size_y, size_z = phase_new.shape
    span = spans(size_x)
    odd_x = lax.rem(lax.axis_index("gx"), 2)
    flip = odd_x if near else 1 - odd_x
    spot = lambda v: v + (1 - flip) * (HALO - 1 - 2 * v)

    def get(name, v):
        begin, end = span[name]
        if v >= begin:
            found = kept[name][(size_x - 1 - v if near else v) - begin]
            return -found if near and name.startswith("gx") else found
        own, first = dict(
            p0=(hp0, -4), c0=(hc0, -4), dz0=(dz, -3), cz0=(cz, -2), gx0=(gx, -3), dv0=(dv, -2),
            p1=(p1, -2), c1=(c1, -2), dz1=(dz, -1), cz1=(cz, 0), gx1=(gx, -1), dv1=(dv, 0), th=(th, -2),
        )[name]
        return own[v - first]

    ends = {-1: fan[...], 0: fans[1 if near else 0]}
    for v in range(-2, 2):
        th[v + 2] = blend(v, ends)
    for step, begin in (("0", -3), ("1", -1)):
        p, c, gx_, dv_, dz_, cz_ = (name + step for name in ("p", "c", "gx", "dv", "dz", "cz"))
        fields = (hp0[pl.ds(1, 3)], hc0[pl.ds(2, 2)]) if step == "0" else (p1[pl.ds(1, 3)], c1[pl.ds(2, 2)])
        dz[...] = along(fields[0], matrices[0])
        cz[...] = along(fields[1], matrices[2])
        yield
        for v in range(begin, begin + 4):
            flux_x, flux_y, flux_z = flux(get(p, v - 1), get(p, v), get(p, v + 1), get(dz_, v))
            gx[v - begin] = flux_x
            if v > begin:
                dv[v - begin - 1] = spread(flux_y)
                fz[v - begin - 1] = flux_z
        yield
        dv[...] += along(fz[...], matrices[1])
        yield
        take = (lambda w: w) if step == "0" else (lambda w: w[:size_y])
        for v in range(begin + 1, begin + 5):
            here, conc = take(get(p, v)), get(c, v)
            divergence = take(get(gx_, v + 1)) - take(get(gx_, v - 1)) + take(get(dv_, v))
            change = phase_change(here, take(conc), take(get("th", v)), divergence)
            beyond = take(get(c, v + 2)) + take(get(c, v - 2))
            new_conc = solute_step(take(conc), beyond, take(next_row(conc)), take(get(cz_, v)), change)
            if step == "0":
                p1[v + 2], c1[v + 2] = here + change, new_conc
            else:
                phase_new[spot(v)], solute_new[spot(v)] = here + change, new_conc
        yield
    change = jnp.zeros((size_y, size_z), F32)
    for v in range(HALO):
        change = change + (phase_new[spot(v)] - get("p0", v)[:size_y])
    result.append(change)


def near_kernel(face, corner, along_z, phase_halo, solute_halo, fan):
    rim_halo(True, face, corner, along_z, phase_halo, solute_halo, fan)


def near_halo(face, corner, along_z):
    _, _, size_y, size_z = face.shape
    rows = size_y + 2 * HALO
    slabs = jax.ShapeDtypeStruct((HALO, rows, size_z), F32)
    return pl.pallas_call(
        near_kernel,
        out_shape=(slabs, slabs, jax.ShapeDtypeStruct((rows, size_z), F32)),
        in_specs=[vmem()] * 3,
        out_specs=[vmem()] * 3,
        compiler_params=pltpu.CompilerParams(vmem_limit_bytes=VMEM_LIMIT),
        cost_estimate=pl.CostEstimate(flops=15 * 10**8, bytes_accessed=15 * 10**6, transcendentals=0),
        name="near",
    )(face, corner, along_z)


def rim_kernel(
    coarse_y, size_x, face, corner, near_phase, near_solute, near_fan, fans, matrices, along_z, inner_latent, *rest
):
    kept = dict(zip(KEPT, rest[: len(KEPT)]))
    near_new, far_new, (keep, send) = rest[len(KEPT) :][:2], rest[len(KEPT) :][2:4], rest[len(KEPT) :][4:6]
    far_phase, far_solute, far_fan, total, *scratch = rest[len(KEPT) + 6 :]
    _, _, size_y, size_z = face.shape
    width = total.shape[1]
    rim_halo(False, face, corner, along_z, far_phase, far_solute, far_fan)
    changes = []
    half = len(scratch) // 2
    sides = [
        rim_march(True, size_x, (near_phase, near_solute, near_fan), fans, matrices, kept, scratch[:half], *near_new, changes),
        rim_march(False, size_x, (far_phase, far_solute, far_fan), fans, matrices, kept, scratch[half:], *far_new, changes),
    ]
    while sides:
        sides = [side for side in sides if next(side, sides) is not sides]
    lanes = [coarse_lane(u, size_x, size_y, coarse_y) for u in (size_x // 4 - 1, 0)]
    total[...] = restrict(changes, lanes, size_y, size_z, width) + inner_latent[...]
    halve(total, lax.div(2 * lax.axis_index("gy"), lax.axis_size("gy")), keep, send)


def halve(total, side, keep, send):
    half = keep.shape[0]
    keep[...] = total[pl.ds(pl.multiple_of(side * half, half), half), :]
    send[...] = total[pl.ds(pl.multiple_of((1 - side) * half, half), half), :]


def rims(shape, face, corner, near, fans, matrices, along_z, inner_latent, kept, coarse_y):
    size_x, size_y, size_z = shape
    rows = size_y + 2 * HALO
    part = jax.ShapeDtypeStruct((HALO, size_y, size_z), F32)
    width = inner_latent.shape[1]
    half = jax.ShapeDtypeStruct((size_z // 8, width), F32)
    slabs = lambda count: pltpu.VMEM((count, rows, size_z), F32)
    return pl.pallas_call(
        functools.partial(rim_kernel, coarse_y, size_x),
        out_shape=(part, part, part, part, half, half),
        in_specs=[vmem()] * (9 + len(kept)),
        out_specs=[vmem()] * 6,
        scratch_shapes=[
            slabs(HALO), slabs(HALO), pltpu.VMEM((rows, size_z), F32), pltpu.VMEM((size_z // 4, width), F32),
            *[slabs(count) for count in 2 * (4, 4, 4, 3, 3, 2, 3, 4)],
        ],
        compiler_params=pltpu.CompilerParams(vmem_limit_bytes=VMEM_LIMIT),
        cost_estimate=pl.CostEstimate(flops=10**7, bytes_accessed=3 * 10**6, transcendentals=0),
        name="rims",
    )(face, corner, *near, fans, matrices, along_z, inner_latent, *kept)


def store_kernel(*refs):
    parts, (phase_out, solute_out, sems) = refs[:6], refs[6:]
    size_x = phase_out.shape[0]
    odd_x = lax.rem(lax.axis_index("gx"), 2)
    near = (1 - odd_x) * (size_x - HALO)
    copies = []
    for begin, pair in ((HALO, parts[:2]), (near, parts[2:4]), (size_x - HALO - near, parts[4:])):
        for part, out in zip(pair, (phase_out, solute_out)):
            copies.append((part, out.at[pl.ds(begin, part.shape[0])]))
    wait_all(start_all(copies, sems))


def store(shape, parts):
    out = jax.ShapeDtypeStruct(shape, F32)
    return pl.pallas_call(
        store_kernel,
        out_shape=(out, out),
        in_specs=[vmem()] * 6,
        out_specs=[hbm()] * 2,
        scratch_shapes=[pltpu.SemaphoreType.DMA((6,))],
        compiler_params=pltpu.CompilerParams(vmem_limit_bytes=VMEM_LIMIT),
        cost_estimate=pl.CostEstimate(flops=0, bytes_accessed=4 * 10**6, transcendentals=0),
        name="store",
    )(*parts)


def merge_kernel(mine, arrived, keep, send, total):
    total[...] = mine[...] + arrived[...]
    halve(total, lax.rem(lax.axis_index("gy"), 2), keep, send)


def merge(mine, arrived):
    half = jax.ShapeDtypeStruct((mine.shape[0] // 2, mine.shape[1]), F32)
    return pl.pallas_call(
        merge_kernel,
        out_shape=(half, half),
        in_specs=[vmem()] * 2,
        out_specs=[vmem()] * 2,
        scratch_shapes=[pltpu.VMEM(mine.shape, F32)],
        compiler_params=pltpu.CompilerParams(vmem_limit_bytes=VMEM_LIMIT),
        cost_estimate=pl.CostEstimate(flops=10**4, bytes_accessed=10**5, transcendentals=0),
        name="merge",
    )(mine, arrived)


def owner_kernel(mine, arrived, out):
    total = mine[...] + arrived[...]
    coarse_x, _, coarse_y = out.shape
    for k in range(coarse_x):
        out[k] = total[:, k * coarse_y : (k + 1) * coarse_y]


def owner(mine, arrived, coarse_x, coarse_y):
    coarse_z = mine.shape[0]
    return pl.pallas_call(
        owner_kernel,
        out_shape=jax.ShapeDtypeStruct((coarse_x, coarse_z, coarse_y), F32),
        in_specs=[vmem()] * 2,
        out_specs=vmem(),
        compiler_params=pltpu.CompilerParams(vmem_limit_bytes=VMEM_LIMIT),
        cost_estimate=pl.CostEstimate(flops=10**4, bytes_accessed=10**5, transcendentals=0),
        name="owner",
    )(mine, arrived)


def body(phase, solute, macro_temp):
    count_x, count_y = lax.axis_size("gx"), lax.axis_size("gy")
    coarse_x, coarse_y, coarse_z = macro_temp.shape
    near_x, far_x = pairs(count_x, 0), pairs(count_x, 1)
    near_y, far_y = pairs(count_y, 0), pairs(count_y, 1)
    across = [(k, (k + count_y // 2) % count_y) for k in range(count_y)]
    ride = count_y == 4
    macro = jnp.swapaxes(macro_temp, 1, 2)
    still = [pltpu.with_memory_space_constraint(v, pltpu.HBM) for v in (phase, solute, macro)]
    phase, solute, face_a, face_b, side_a, strip_b, rest_b, table = pack(*still, ride)
    coarse_shape = (coarse_z * count_y, coarse_x * coarse_y)
    face_a = lax.ppermute(face_a, "gx", near_x)
    side_a = lax.ppermute(side_a, "gy", near_y)
    if ride:
        strip_b = append(side_a, strip_b)
    else:
        table = lax.all_gather(table, "gy").reshape(coarse_shape)
    matrices, along_z = z_products(phase.shape[2], strip_b)
    face_b, rest_b, matrices = lax.optimization_barrier((face_b, rest_b, matrices))
    strip_b = lax.ppermute(strip_b, "gy", far_y)
    rest_b = lax.ppermute(rest_b, "gy", far_y)
    face_b = lax.ppermute(face_b, "gx", far_x)
    coarse, corner_a, corner_b = corners(side_a, strip_b, table, coarse_y, coarse_shape)
    corner_a = lax.ppermute(corner_a, "gx", near_x)
    corner_b = lax.ppermute(corner_b, "gx", far_x)
    results = inner(phase, solute, side_a, strip_b, rest_b, coarse, matrices, along_z, coarse_y)
    middle, inner_latent, fans, kept = results[:2], results[2], results[3], results[4:]
    near = near_halo(face_a, corner_a, along_z)
    *edges, mine, send = rims(
        phase.shape, face_b, corner_b, near, fans, matrices, along_z, inner_latent, kept, coarse_y
    )
    phase_out, solute_out = store(phase.shape, (*middle, *edges))
    if ride:
        mine, send = merge(mine, lax.ppermute(send, "gy", across))
        latent = owner(mine, lax.ppermute(send, "gy", near_y), coarse_x, coarse_y)
    else:
        low = lax.axis_index("gy") < count_y // 2
        total = jnp.concatenate([jnp.where(low, mine, send), jnp.where(low, send, mine)])
        latent = lax.psum_scatter(total, "gy", scatter_dimension=0, tiled=True)
        latent = jnp.swapaxes(latent.reshape(coarse_z, coarse_x, coarse_y), 0, 1)
    latent = jnp.swapaxes(latent, 1, 2)
    return phase_out, solute_out, latent


def solution(mesh):
    in_specs = (P("gx", "gy", None), P("gx", "gy", None), P("gx", None, "gy"))
    out_specs = (P("gx", "gy", None), P("gx", "gy", None), P("gx", None, "gy"))
    return jax.shard_map(body, mesh=mesh, in_specs=in_specs, out_specs=out_specs, check_vma=False)
```

```python
import functools

import jax
import jax.numpy as jnp
from jax import lax
from jax.experimental import pallas as pl
from jax.experimental.pallas import tpu as pltpu
from jax.sharding import PartitionSpec as P

time_step = 0.1
anisotropy = 0.3
coupling = 2.0
rejection = 0.5

F32 = jnp.float32
HALO = 4
STRIP = 4
ROWS = 8
LANES = 128
VMEM_LIMIT = 24 * 1024 * 1024


def vmem():
    return pl.BlockSpec(memory_space=pltpu.VMEM)


def anywhere():
    return pl.BlockSpec(memory_space=pl.ANY)


def hbm():
    return pl.BlockSpec(memory_space=pltpu.HBM)


def pairs(count, first):
    forward = [((first + k) % count, (first + k + 1) % count) for k in range(0, count, 2)]
    return forward + [(b, a) for a, b in forward]


def flips(me):
    odd = lax.rem(me, 2)
    return me, me + 1 - 2 * odd, lax.rem(me + 2, 4), 3 - me


def halves(value):
    coarse = value.astype(jnp.bfloat16)
    return coarse, (value - coarse.astype(F32)).astype(jnp.bfloat16)


def product(left, right, contract):
    dot = lambda a, b: lax.dot_general(a, b, ((contract[:1], contract[1:]), ((), ())), preferred_element_type=F32)
    if left.dtype == jnp.bfloat16:
        parts = [dot(left, part) for part in halves(right)]
    else:
        parts = [dot(part, right) for part in halves(left)]
    return parts[0] + parts[1]


def row_ids(shape):
    return lax.broadcasted_iota(jnp.int32, shape, len(shape) - 2)


def lane_ids(shape):
    return lax.broadcasted_iota(jnp.int32, shape, len(shape) - 1)


def start_all(copies, sems):
    copies = [pltpu.make_async_copy(source, target, sems.at[n]) for n, (source, target) in enumerate(copies)]
    for copy in copies:
        copy.start()
    return copies


def wait_all(copies):
    for copy in copies:
        copy.wait()


def fold(table):
    half = table.shape[0] // 2
    return jnp.concatenate([table[:half], table[half:]], axis=1)


def unfold(tile):
    return jnp.concatenate([tile[:, :LANES], tile[:, LANES:]], axis=0)


def pack_kernel(
    phase, solute, macro, phase_here, solute_here, face_a, face_b, side_a, strip_b, rest_b, table, local, sems
):
    size_x, size_y, size_z = phase.shape
    odd_x = lax.rem(lax.axis_index("gx"), 2)
    even_y = lax.rem(lax.axis_index("gy"), 2) == 0
    copies = []
    for at in range(0, size_x, HALO):
        for ref, here in ((phase, phase_here), (solute, solute_here)):
            copies.append((ref.at[pl.ds(at, HALO)], here.at[pl.ds(at, HALO)]))
    copies.append((macro, local))
    copies = start_all(copies, sems)
    wait_all(copies)
    for field, here in enumerate((phase_here, solute_here)):
        face_a[field] = here[pl.ds((1 - odd_x) * (size_x - HALO), HALO)]
        face_b[field] = here[pl.ds(odd_x * (size_x - HALO), HALO)]
    low = [here[:, pl.ds(0, ROWS), :] for here in (phase_here, solute_here)]
    high = [here[:, pl.ds(size_y - ROWS, ROWS), :] for here in (phase_here, solute_here)]
    wide = jnp.concatenate([local[k] for k in range(local.shape[0])], axis=1)
    table[...] = wide
    top = row_ids((size_x, ROWS, size_z)) < HALO
    low_side = jnp.where(top, low[0], pltpu.roll(low[1], HALO, 1))
    high_side = jnp.where(top, pltpu.roll(high[1], HALO, 1), high[0])
    side_a[pl.ds(0, size_x)] = jnp.where(even_y, high_side, low_side)
    side_b = jnp.where(even_y, low_side, high_side)
    strip_b[pl.ds(0, STRIP)] = side_b[:STRIP]
    strip_b[pl.ds(STRIP, STRIP)] = side_b[size_x - STRIP :]
    rest_b[...] = side_b[STRIP : size_x - STRIP]
    if side_a.shape[0] > size_x:
        side_a[size_x] = fold(wide)
        strip_b[2 * STRIP] = fold(wide)


def pack(phase, solute, macro, ride):
    size_x, size_y, size_z = phase.shape
    coarse_x, coarse_z, coarse_y = macro.shape
    field = jax.ShapeDtypeStruct(phase.shape, F32)
    face = jax.ShapeDtypeStruct((2, HALO, size_y, size_z), F32)
    counts = (size_x, 2 * STRIP, size_x - 2 * STRIP)
    extra = (1, 2, 0) if ride else (0, 0, 0)
    sides = [jax.ShapeDtypeStruct((count + more, ROWS, size_z), F32) for count, more in zip(counts, extra)]
    table = jax.ShapeDtypeStruct((coarse_z, coarse_x * coarse_y), F32)
    return pl.pallas_call(
        pack_kernel,
        out_shape=(field, field, face, face, *sides, table),
        in_specs=[hbm()] * 3,
        out_specs=[vmem()] * 8,
        scratch_shapes=[pltpu.VMEM(macro.shape, F32), pltpu.SemaphoreType.DMA((1 + 2 * (size_x // HALO),))],
        compiler_params=pltpu.CompilerParams(vmem_limit_bytes=VMEM_LIMIT),
        cost_estimate=pl.CostEstimate(flops=10**5, bytes_accessed=2 * 10**6, transcendentals=0),
        name="pack",
    )(phase, solute, macro)


def append_kernel(arrived, side, out):
    out[side.shape[0] - 1] = arrived[arrived.shape[0] - 1]


def append(arrived, side):
    return pl.pallas_call(
        append_kernel,
        out_shape=jax.ShapeDtypeStruct(side.shape, F32),
        in_specs=[vmem(), vmem()],
        out_specs=vmem(),
        input_output_aliases={1: 0},
        compiler_params=pltpu.CompilerParams(vmem_limit_bytes=VMEM_LIMIT),
        cost_estimate=pl.CostEstimate(flops=0, bytes_accessed=10**5, transcendentals=0),
        name="append",
    )(arrived, side)


def near_rows(block, coarse_y):
    shape = (2 * ROWS, coarse_y)
    wanted = lax.rem(row_ids(shape) + lax.axis_index("gy") * ROWS + coarse_y - 1, coarse_y)
    pick = (lane_ids(shape) == wanted).astype(F32).astype(jnp.bfloat16)
    return product(pick, block, (1, 1))


def pack_edge(rows):
    pieces = rows[:ROWS], pltpu.roll(rows[:ROWS], 4, 0), rows[ROWS:], pltpu.roll(rows[ROWS:], 4, 0)
    return jnp.concatenate(pieces, axis=1)


def unpack_edge(tile):
    quarter = tile.shape[1] // 4
    pieces = [tile[:, at : at + quarter] for at in range(0, tile.shape[1], quarter)]
    top = row_ids(pieces[0].shape) < 4
    halves = [jnp.where(top, pieces[n], pltpu.roll(pieces[n + 1], 4, 0)) for n in (0, 2)]
    return jnp.concatenate(halves, axis=0)


def corner_kernel(coarse_y, gathered, side_a, strip_b, table, coarse, corner_a, corner_b):
    size_x = side_a.shape[0] - (0 if gathered else 1)
    me = lax.axis_index("gy")
    even_x = lax.rem(lax.axis_index("gx"), 2) == 0
    even_y = lax.rem(me, 2) == 0
    block = table[...]
    if not gathered:
        near, across, far = flips(me)[1:]
        depth = table.shape[0]
        tiles = (me, block), (near, unfold(side_a[size_x])), (far, unfold(strip_b[2 * STRIP])), (across, unfold(strip_b[2 * STRIP + 1]))
        for source, tile in tiles:
            coarse[pl.ds(pl.multiple_of(source * depth, depth), depth), :] = tile
        block = coarse[...]
    depth, width = block.shape
    flipped = [block[:, at : at + coarse_y] for at in range(width - coarse_y, -1, -coarse_y)]
    block = jnp.where(even_x, block, jnp.concatenate(flipped, axis=1))
    coarse[...] = block
    row = row_ids(side_a.shape[1:])
    edges = block[:, width - coarse_y :], block[:, :coarse_y]
    for corner, top_side, edge in ((corner_a, even_x, edges[0]), (corner_b, jnp.logical_not(even_x), edges[1])):

        def layer(d, high):
            first = side_a[jnp.where(top_side, size_x - d, d - 1)]
            second = strip_b[jnp.where(top_side, 2 * STRIP - d, d - 1)]
            return jnp.where(even_y, first, second) if high else jnp.where(even_y, second, first)

        spare = pack_edge(near_rows(edge, coarse_y))
        tile = jnp.where(row == 4, pltpu.roll(layer(3, False), 5, 0), layer(1, False))
        corner[0] = jnp.where(row < 2, spare, tile)
        tile = jnp.where(row == 3, pltpu.roll(layer(3, True), 3, 0), layer(1, True))
        corner[1] = jnp.where(row >= 6, pltpu.roll(spare, 4, 0), tile)
        corner[2] = jnp.where(row % 4 < 2, layer(2, True), layer(2, False))


def corners(side_a, strip_b, table, coarse_y, coarse_shape):
    size_z = side_a.shape[2]
    corner = jax.ShapeDtypeStruct((3, ROWS, size_z), F32)
    coarse = jax.ShapeDtypeStruct(coarse_shape, F32)
    return pl.pallas_call(
        functools.partial(corner_kernel, coarse_y, table.shape == coarse_shape),
        out_shape=(coarse, corner, corner),
        in_specs=[vmem()] * 3,
        out_specs=[vmem()] * 3,
        compiler_params=pltpu.CompilerParams(vmem_limit_bytes=VMEM_LIMIT),
        cost_estimate=pl.CostEstimate(flops=10**5, bytes_accessed=4 * 10**5, transcendentals=0),
        name="corners",
    )(side_a, strip_b, table)


def weights(ends, frac, tick):
    first, second = ends
    return jnp.where(tick == first, 1.0 - frac, 0.0) + jnp.where(tick == second, frac, 0.0)


def weights_z(depth, size_z):
    shape = (depth, size_z)
    fine = lane_ids(shape)
    lower = (2 * fine + 5) // 8 - 1
    frac = (2 * fine - 3 - 8 * lower).astype(F32) / 8.0
    ends = jnp.clip(lower, 0, depth - 1), jnp.clip(lower + 1, 0, depth - 1)
    return weights(ends, frac, row_ids(shape))


def interpolate(rows, along_z, size_y):
    deep = product(rows, along_z, (1, 0))
    shape = (size_y + 2 * HALO, 2 * ROWS)
    fine = row_ids(shape)
    fine = jnp.where(fine >= size_y + HALO, fine - shape[0], fine)
    lower = (2 * fine + 13) // 8 - 2
    frac = (2 * fine - 3 - 8 * lower).astype(F32) / 8.0
    along_y = weights((lower + 1, lower + 2), frac, lane_ids(shape)).astype(jnp.bfloat16)
    return [
        product(along_y, deep[at : at + 2 * ROWS], (1, 0))
        for at in range(0, rows.shape[0], 2 * ROWS)
    ]


def blend(x, fans):
    lower = (2 * x - 3) // 8
    frac = (2 * x - 3 - 8 * lower) / 8.0
    return (1.0 - frac) * fans[lower] + frac * fans[lower + 1]


def turn(value, by, axis):
    return pltpu.roll(value, by % value.shape[axis], axis)


def z_matrices(size_z):
    shape = (size_z, size_z)
    source, target = row_ids(shape), lane_ids(shape)
    hit = lambda at: (source == at).astype(F32)
    end = size_z - 1
    gradient = hit(jnp.minimum(target + 1, end)) - hit(jnp.maximum(target - 1, 0))
    difference = hit(target + 1) - hit(target - 1)
    laplace = hit(jnp.minimum(target + 2, end)) + hit(jnp.maximum(target - 2, 0)) - 6.0 * hit(target)
    return tuple(m.astype(jnp.bfloat16) for m in (gradient, difference, laplace))


def matrix_kernel(size_z, tile, out, along_z):
    for n, matrix in enumerate(z_matrices(size_z)):
        out[n] = matrix
    along_z[...] = weights_z(*along_z.shape).astype(jnp.bfloat16)


def z_products(size_z, tile):
    square = jax.ShapeDtypeStruct((3, size_z, size_z), jnp.bfloat16)
    return pl.pallas_call(
        functools.partial(matrix_kernel, size_z),
        out_shape=(square, jax.ShapeDtypeStruct((size_z // 4, size_z), jnp.bfloat16)),
        in_specs=[anywhere()],
        out_specs=[vmem()] * 2,
        compiler_params=pltpu.CompilerParams(vmem_limit_bytes=VMEM_LIMIT),
        cost_estimate=pl.CostEstimate(flops=10**6, bytes_accessed=4 * 10**5, transcendentals=0),
        name="products",
    )(tile)


def along(slabs, matrix):
    return product(slabs.reshape(-1, slabs.shape[-1]), matrix, (1, 0)).reshape(slabs.shape)


def z_difference(value, clamp):
    first, second = value[:, :LANES], value[:, LANES:]
    lane = lane_ids(first.shape)
    head, tail = lane == 0, lane == LANES - 1
    ends = (first, second) if clamp else (0.0, 0.0)
    ahead = turn(first, -1, 1), turn(second, -1, 1)
    behind = turn(first, 1, 1), turn(second, 1, 1)
    low = jnp.where(tail, ahead[1], ahead[0]) - jnp.where(head, ends[0], behind[0])
    high = jnp.where(tail, ends[1], ahead[1]) - jnp.where(head, behind[0], behind[1])
    return jnp.concatenate([low, high], axis=1)


def flux(before, here, after, along_z):
    along_x = after - before
    along_y = turn(here, -1, 0) - turn(here, 1, 0)
    sq_x = along_x * along_x
    sq_y = along_y * along_y
    both = sq_x + sq_y
    inverse = 1.0 / (both + 4.0)
    factor = 1.0 + anisotropy * (both * both - 8.0 * (sq_x * sq_y)) * (inverse * inverse)
    stiff = (0.25 * time_step) * (factor * factor)
    return stiff * along_x, stiff * along_y, stiff * along_z


def spread(flux_y):
    return turn(flux_y, -1, 0) - turn(flux_y, 1, 0)


def phase_change(here, conc, theta, divergence):
    square = 1.0 - here * here
    drive = square * (here - (coupling * square) * (theta + conc))
    return divergence + time_step * drive


def solute_step(conc, beyond_x, beyond_y, along_z, change):
    return conc + (0.25 * time_step) * (beyond_x + beyond_y + along_z) + rejection * change


def next_row(conc):
    return turn(conc, -2, 0) + turn(conc, 2, 0)


def restrict(changes, lanes, size_y, size_z, coarse_width):
    shape = (size_z, size_z // 4)
    pool_z = (row_ids(shape) // 4 == lane_ids(shape)).astype(F32).astype(jnp.bfloat16)
    shape = (size_y, coarse_width)
    cell, lane = row_ids(shape) // 4, lane_ids(shape)
    pool_y = [jnp.where(cell + at == lane, 0.5 / 64.0, 0.0).astype(jnp.bfloat16) for at in lanes]
    pooled = product(jnp.concatenate(changes, axis=0), pool_z, (1, 0))
    return product(pooled, jnp.concatenate(pool_y, axis=0), (0, 0))


def coarse_lane(u, size_x, size_y, coarse_y):
    last = size_x // 4 - 1
    x = u + lax.rem(lax.axis_index("gx"), 2) * (last - 2 * u)
    return x * coarse_y + lax.axis_index("gy") * (size_y // 4)


KEPT = ("p0", "c0", "dz0", "cz0", "gx0", "dv0", "p1", "c1", "dz1", "cz1", "gx1", "dv1", "th")


def spans(size_x):
    widths = dict(p0=0, c0=0, dz0=0, cz0=0, gx0=1, dv0=1, p1=2, c1=2, dz1=2, cz1=2, gx1=3, dv1=3, th=2)
    return {name: (widths[name], size_x - widths[name]) for name in KEPT}


def halo_rows(tile, top):
    zero = jnp.zeros_like(tile[0])
    low = tile[0], tile[2], pltpu.roll(tile[0], 3, 0), zero
    high = tile[1], tile[2], pltpu.roll(tile[1], 5, 0), zero
    return [
        (jnp.where(top, h, l), pltpu.roll(jnp.where(top, l, h), HALO, 0)) for l, h in zip(low, high)
    ]


def inner_kernel(
    coarse_y, phase, solute, side_a, strip_b, rest_b, coarse, matrices, along_z, phase_new, solute_new, latent, ends, *rest
):
    kept = dict(zip(KEPT, rest[: len(KEPT)]))
    (fz,) = rest[len(KEPT) :]
    size_x, size_y, size_z = phase.shape
    span = spans(size_x)
    odd_x = lax.rem(lax.axis_index("gx"), 2)
    even_y = lax.rem(lax.axis_index("gy"), 2) == 0
    at = lambda name, u: kept[name].at[u - span[name][0]]
    get = lambda name, u: kept[name][u - span[name][0]]
    place = lambda u: u + odd_x * (size_x - 1 - 2 * u)
    top = row_ids((ROWS, size_z)) < HALO
    for u in range(size_x):
        first = side_a[place(u)]
        if STRIP <= u < size_x - STRIP:
            second = rest_b[place(u) - STRIP]
        else:
            at_strip = u if u < STRIP else u - size_x + 2 * STRIP
            second = strip_b[at_strip + odd_x * (2 * STRIP - 1 - 2 * at_strip)]
        low, high = jnp.where(even_y, second, first), jnp.where(even_y, first, second)
        at("p0", u)[pl.ds(0, size_y), :] = phase[place(u)]
        at("c0", u)[pl.ds(0, size_y), :] = solute[place(u)]
        at("p0", u)[pl.ds(size_y, ROWS), :] = jnp.where(top, high, low)
        at("c0", u)[pl.ds(size_y, ROWS), :] = pltpu.roll(jnp.where(top, low, high), HALO, 0)
    block = coarse[...]
    block = [near_rows(block[:, at : at + coarse_y], coarse_y) for at in range(0, block.shape[1], coarse_y)]
    fans = dict(enumerate(interpolate(jnp.concatenate(block, axis=0), along_z[...], size_y)))
    ends[0], ends[1] = fans[0], fans[len(fans) - 1]
    for u in range(*span["th"]):
        at("th", u)[...] = blend(u, fans)

    for step in "01":
        p, c, dz, cz, gx, dv = (name + step for name in ("p", "c", "dz", "cz", "gx", "dv"))
        kept[dz][...] = along(kept[p][...], matrices[0])
        kept[cz][...] = along(kept[c][...], matrices[2])
        begin, end = span[gx]
        for u in range(begin, end):
            flux_x, flux_y, flux_z = flux(get(p, u - 1), get(p, u), get(p, u + 1), get(dz, u))
            at(gx, u)[...] = flux_x
            at(dv, u)[...] = spread(flux_y)
            fz[u - begin] = flux_z
        kept[dv][...] += along(fz[pl.ds(0, end - begin)], matrices[1])
        take = (lambda v: v) if step == "0" else (lambda v: v[:size_y])
        for u in range(begin + 1, end - 1):
            here, conc = take(get(p, u)), get(c, u)
            divergence = take(get(gx, u + 1)) - take(get(gx, u - 1)) + take(get(dv, u))
            change = phase_change(here, take(conc), take(get("th", u)), divergence)
            beyond = take(get(c, u + 2)) + take(get(c, u - 2))
            new_conc = solute_step(take(conc), beyond, take(next_row(conc)), take(get(cz, u)), change)
            if step == "0":
                at("p1", u)[...] = here + change
                at("c1", u)[...] = new_conc
            else:
                phase_new[place(u) - HALO] = here + change
                solute_new[place(u) - HALO] = new_conc
    changes, lanes = [], []
    for k in range(1, size_x // 4 - 1):
        change = jnp.zeros((size_y, size_z), F32)
        for u in range(4 * k, 4 * k + 4):
            change = change + (phase_new[place(u) - HALO] - get("p0", u)[:size_y])
        changes.append(change)
        lanes.append(coarse_lane(k, size_x, size_y, coarse_y))
    latent[...] = restrict(changes, lanes, size_y, size_z, latent.shape[1])


def inner(phase, solute, side_a, strip_b, rest_b, coarse, matrices, along_z, coarse_y):
    size_x, size_y, size_z = phase.shape
    rows = size_y + 2 * HALO
    part = jax.ShapeDtypeStruct((size_x - 2 * HALO, size_y, size_z), F32)
    kept = [jax.ShapeDtypeStruct((end - begin, rows, size_z), F32) for begin, end in spans(size_x).values()]
    latent = jax.ShapeDtypeStruct((size_z // 4, coarse.shape[1]), F32)
    return pl.pallas_call(
        functools.partial(inner_kernel, coarse_y),
        out_shape=(part, part, latent, jax.ShapeDtypeStruct((2, rows, size_z), F32), *kept),
        in_specs=[vmem()] * 8,
        out_specs=[vmem()] * (4 + len(kept)),
        scratch_shapes=[pltpu.VMEM((size_x - 2, rows, size_z), F32)],
        compiler_params=pltpu.CompilerParams(vmem_limit_bytes=VMEM_LIMIT),
        cost_estimate=pl.CostEstimate(flops=5 * 10**8, bytes_accessed=5 * 10**6, transcendentals=0),
        name="inner",
    )(phase, solute, side_a, strip_b, rest_b, coarse, matrices, along_z)


def rim_halo(near, face, corner, phase_halo, solute_halo):
    _, _, size_y, size_z = face.shape
    odd_x = lax.rem(lax.axis_index("gx"), 2)
    flip = odd_x if near else 1 - odd_x
    top = row_ids((ROWS, size_z)) < HALO
    for d, (p_rows, c_rows) in enumerate(halo_rows(corner, top)):
        layer = d + flip * (HALO - 1 - 2 * d)
        for n, (field, rows) in enumerate(((phase_halo, p_rows), (solute_halo, c_rows))):
            field[HALO - 1 - d, pl.ds(0, size_y), :] = face[n, layer]
            field[HALO - 1 - d, pl.ds(size_y, ROWS), :] = rows


def edge_fan(corner, along_z, size_y):
    edge = jnp.where(row_ids(corner.shape[1:]) < 2, corner[0], pltpu.roll(corner[1], 4, 0))
    return interpolate(unpack_edge(edge), along_z[...], size_y)[0]


def rim_spot(near):
    odd_x = lax.rem(lax.axis_index("gx"), 2)
    flip = odd_x if near else 1 - odd_x
    return lambda v: v + (1 - flip) * (HALO - 1 - 2 * v)


def rim_march(near, size_x, halo, fans, matrices, kept, scratch, p1, c1, phase_new, result):
    hp0, hc0, fan = halo
    gx, dv, dz, cz, th = scratch
    _, size_y, size_z = phase_new.shape
    span = spans(size_x)
    spot = rim_spot(near)

    def get(name, v):
        begin, end = span[name]
        if v >= begin:
            found = kept[name][(size_x - 1 - v if near else v) - begin]
            return -found if near and name.startswith("gx") else found
        own, first = dict(
            p0=(hp0, -4), c0=(hc0, -4), dz0=(dz, -3), cz0=(cz, -2), gx0=(gx, -3), dv0=(dv, -2),
            p1=(p1, -2), c1=(c1, -2), dz1=(dz, -1), gx1=(gx, -1), dv1=(dv, 0), th=(th, -2),
        )[name]
        return own[v - first]

    moved = []
    ends = {-1: fan, 0: fans[1 if near else 0]}
    for v in range(-2, 2):
        th[v + 2] = blend(v, ends)
    for step, begin in (("0", -3), ("1", -1)):
        p, c, gx_, dv_, dz_, cz_ = (name + step for name in ("p", "c", "gx", "dv", "dz", "cz"))
        for n in range(3):
            dz[n] = z_difference((hp0 if step == "0" else p1)[n + 1], True)
        if step == "0":
            cz[...] = along(hc0[pl.ds(2, 2)], matrices[2])
        yield
        for v in range(begin, begin + 4):
            flux_x, flux_y, flux_z = flux(get(p, v - 1), get(p, v), get(p, v + 1), get(dz_, v))
            gx[v - begin] = flux_x
            if v > begin:
                dv[v - begin - 1] = spread(flux_y) + z_difference(flux_z, False)
        yield
        take = (lambda w: w) if step == "0" else (lambda w: w[:size_y])
        for v in range(begin + 1, begin + 5):
            here, conc = take(get(p, v)), get(c, v)
            divergence = take(get(gx_, v + 1)) - take(get(gx_, v - 1)) + take(get(dv_, v))
            change = phase_change(here, take(conc), take(get("th", v)), divergence)
            if step == "0":
                beyond = get(c, v + 2) + get(c, v - 2)
                p1[v + 2] = here + change
                c1[v + 2] = solute_step(conc, beyond, next_row(conc), get(cz_, v), change)
            else:
                phase_new[spot(v)] = here + change
                moved.append(here + change - get("p0", v)[:size_y])
        yield
    result.append((moved[0] + moved[1]) + (moved[2] + moved[3]))


def near_kernel(face, corner, phase_halo, solute_halo):
    rim_halo(True, face, corner, phase_halo, solute_halo)


def near_halo(face, corner):
    _, _, size_y, size_z = face.shape
    slabs = jax.ShapeDtypeStruct((HALO, size_y + 2 * HALO, size_z), F32)
    return pl.pallas_call(
        near_kernel,
        out_shape=(slabs, slabs),
        in_specs=[vmem()] * 2,
        out_specs=[vmem()] * 2,
        compiler_params=pltpu.CompilerParams(vmem_limit_bytes=VMEM_LIMIT),
        cost_estimate=pl.CostEstimate(flops=15 * 10**8, bytes_accessed=15 * 10**6, transcendentals=0),
        name="near",
    )(face, corner)


def rim_kernel(
    coarse_y, size_x, face, corner, near_phase, near_solute, near_corner, fans, matrices, along_z, inner_latent, *rest
):
    kept = dict(zip(KEPT, rest[: len(KEPT)]))
    outs, (far_phase, far_solute, total, *scratch) = rest[len(KEPT) : len(KEPT) + 8], rest[len(KEPT) + 8 :]
    near_new, far_new, keep, send = outs[:3], outs[3:6], outs[6], outs[7]
    _, _, size_y, size_z = face.shape
    width = total.shape[1]
    rim_halo(False, face, corner, far_phase, far_solute)
    changes = []
    half = len(scratch) // 2
    near = near_phase, near_solute, edge_fan(near_corner, along_z, size_y)
    far = far_phase, far_solute, edge_fan(corner, along_z, size_y)
    sides = [
        rim_march(True, size_x, near, fans, matrices, kept, scratch[:half], *near_new, changes),
        rim_march(False, size_x, far, fans, matrices, kept, scratch[half:], *far_new, changes),
    ]
    while sides:
        sides = [side for side in sides if next(side, sides) is not sides]
    lanes = [coarse_lane(u, size_x, size_y, coarse_y) for u in (size_x // 4 - 1, 0)]
    total[...] = restrict(changes, lanes, size_y, size_z, width) + inner_latent[...]
    halve(total, lax.div(2 * lax.axis_index("gy"), lax.axis_size("gy")), keep, send)


def halve(total, side, keep, send):
    half = keep.shape[0]
    keep[...] = total[pl.ds(pl.multiple_of(side * half, half), half), :]
    send[...] = total[pl.ds(pl.multiple_of((1 - side) * half, half), half), :]


def rims(shape, face, corner, near, fans, matrices, along_z, inner_latent, kept, coarse_y):
    size_x, size_y, size_z = shape
    rows = size_y + 2 * HALO
    part = jax.ShapeDtypeStruct((HALO, size_y, size_z), F32)
    width = inner_latent.shape[1]
    half = jax.ShapeDtypeStruct((size_z // 8, width), F32)
    state = jax.ShapeDtypeStruct((HALO, rows, size_z), F32)
    slabs = lambda count: pltpu.VMEM((count, rows, size_z), F32)
    return pl.pallas_call(
        functools.partial(rim_kernel, coarse_y, size_x),
        out_shape=(state, state, part, state, state, part, half, half),
        in_specs=[vmem()] * (9 + len(kept)),
        out_specs=[vmem()] * 8,
        scratch_shapes=[
            slabs(HALO), slabs(HALO), pltpu.VMEM((size_z // 4, width), F32),
            *[slabs(count) for count in 2 * (4, 3, 3, 2, 4)],
        ],
        compiler_params=pltpu.CompilerParams(vmem_limit_bytes=VMEM_LIMIT),
        cost_estimate=pl.CostEstimate(flops=10**7, bytes_accessed=3 * 10**6, transcendentals=0),
        name="rims",
    )(face, corner, *near, fans, matrices, along_z, inner_latent, *kept)


def rim_solute(near, size_x, p1, c1, phase_new, matrices, kept, out):
    _, size_y, size_z = phase_new.shape
    span = spans(size_x)
    spot = rim_spot(near)
    own = {"p1": p1[...], "c1": c1[...], "cz1": along(c1[pl.ds(2, 2)], matrices[2])}

    def get(name, v):
        begin, _ = span[name]
        if v >= begin:
            return kept[name][(size_x - 1 - v if near else v) - begin]
        return own[name][v if name == "cz1" else v + 2]

    for v in range(HALO):
        conc = get("c1", v)
        change = phase_new[spot(v)] - get("p1", v)[:size_y]
        beyond = get("c1", v + 2)[:size_y] + get("c1", v - 2)[:size_y]
        out[spot(v)] = solute_step(
            conc[:size_y], beyond, next_row(conc)[:size_y], get("cz1", v)[:size_y], change
        )


def store_kernel(
    middle_phase, middle_solute, near_p1, near_c1, near_phase, far_p1, far_c1, far_phase, matrices, p1, c1, cz1,
    phase_out, solute_out, near_solute, far_solute, sems,
):
    size_x = phase_out.shape[0]
    odd_x = lax.rem(lax.axis_index("gx"), 2)
    near = (1 - odd_x) * (size_x - HALO)
    far = size_x - HALO - near
    put = lambda part, out, at: (part, out.at[pl.ds(at, part.shape[0])])
    copies = start_all(
        [
            put(middle_phase, phase_out, HALO), put(middle_solute, solute_out, HALO), put(near_phase, phase_out, near),
            put(far_phase, phase_out, far),
        ],
        sems,
    )
    kept = dict(p1=p1, c1=c1, cz1=cz1)
    rim_solute(True, size_x, near_p1, near_c1, near_phase, matrices, kept, near_solute)
    rim_solute(False, size_x, far_p1, far_c1, far_phase, matrices, kept, far_solute)
    copies += start_all(
        [put(near_solute, solute_out, near), put(far_solute, solute_out, far)], sems.at[pl.ds(4, 2)]
    )
    wait_all(copies)


def store(shape, middle, edges, matrices, kept):
    kept = dict(zip(KEPT, kept))
    out = jax.ShapeDtypeStruct(shape, F32)
    part = pltpu.VMEM((HALO, *shape[1:]), F32)
    return pl.pallas_call(
        store_kernel,
        out_shape=(out, out),
        in_specs=[vmem()] * 12,
        out_specs=[hbm()] * 2,
        scratch_shapes=[part, part, pltpu.SemaphoreType.DMA((6,))],
        compiler_params=pltpu.CompilerParams(vmem_limit_bytes=VMEM_LIMIT),
        cost_estimate=pl.CostEstimate(flops=0, bytes_accessed=4 * 10**6, transcendentals=0),
        name="store",
    )(*middle, *edges, matrices, kept["p1"], kept["c1"], kept["cz1"])


def merge_kernel(mine, arrived, keep, send, total):
    total[...] = mine[...] + arrived[...]
    halve(total, lax.rem(lax.axis_index("gy"), 2), keep, send)


def merge(mine, arrived):
    half = jax.ShapeDtypeStruct((mine.shape[0] // 2, mine.shape[1]), F32)
    return pl.pallas_call(
        merge_kernel,
        out_shape=(half, half),
        in_specs=[vmem()] * 2,
        out_specs=[vmem()] * 2,
        scratch_shapes=[pltpu.VMEM(mine.shape, F32)],
        compiler_params=pltpu.CompilerParams(vmem_limit_bytes=VMEM_LIMIT),
        cost_estimate=pl.CostEstimate(flops=10**4, bytes_accessed=10**5, transcendentals=0),
        name="merge",
    )(mine, arrived)


def owner_kernel(mine, arrived, out):
    total = mine[...] + arrived[...]
    coarse_x, _, coarse_y = out.shape
    for k in range(coarse_x):
        out[k] = total[:, k * coarse_y : (k + 1) * coarse_y]


def owner(mine, arrived, coarse_x, coarse_y):
    coarse_z = mine.shape[0]
    return pl.pallas_call(
        owner_kernel,
        out_shape=jax.ShapeDtypeStruct((coarse_x, coarse_z, coarse_y), F32),
        in_specs=[vmem()] * 2,
        out_specs=vmem(),
        compiler_params=pltpu.CompilerParams(vmem_limit_bytes=VMEM_LIMIT),
        cost_estimate=pl.CostEstimate(flops=10**4, bytes_accessed=10**5, transcendentals=0),
        name="owner",
    )(mine, arrived)


def body(phase, solute, macro_temp):
    count_x, count_y = lax.axis_size("gx"), lax.axis_size("gy")
    coarse_x, coarse_y, coarse_z = macro_temp.shape
    near_x, far_x = pairs(count_x, 0), pairs(count_x, 1)
    near_y, far_y = pairs(count_y, 0), pairs(count_y, 1)
    across = [(k, (k + count_y // 2) % count_y) for k in range(count_y)]
    ride = count_y == 4
    macro = jnp.swapaxes(macro_temp, 1, 2)
    still = [pltpu.with_memory_space_constraint(v, pltpu.HBM) for v in (phase, solute, macro)]
    phase, solute, face_a, face_b, side_a, strip_b, rest_b, table = pack(*still, ride)
    coarse_shape = (coarse_z * count_y, coarse_x * coarse_y)
    face_a = lax.ppermute(face_a, "gx", near_x)
    side_a = lax.ppermute(side_a, "gy", near_y)
    if ride:
        strip_b = append(side_a, strip_b)
    else:
        table = lax.all_gather(table, "gy").reshape(coarse_shape)
    matrices, along_z = z_products(phase.shape[2], strip_b)
    face_b, rest_b, matrices = lax.optimization_barrier((face_b, rest_b, matrices))
    strip_b = lax.ppermute(strip_b, "gy", far_y)
    rest_b = lax.ppermute(rest_b, "gy", far_y)
    face_b = lax.ppermute(face_b, "gx", far_x)
    coarse, corner_a, corner_b = corners(side_a, strip_b, table, coarse_y, coarse_shape)
    corner_a = lax.ppermute(corner_a, "gx", near_x)
    corner_b = lax.ppermute(corner_b, "gx", far_x)
    results = inner(phase, solute, side_a, strip_b, rest_b, coarse, matrices, along_z, coarse_y)
    middle, inner_latent, fans, kept = results[:2], results[2], results[3], results[4:]
    near = (*near_halo(face_a, corner_a), corner_a)
    *edges, mine, send = rims(
        phase.shape, face_b, corner_b, near, fans, matrices, along_z, inner_latent, kept, coarse_y
    )
    phase_out, solute_out = store(phase.shape, middle, edges, matrices, kept)
    if ride:
        mine, send = merge(mine, lax.ppermute(send, "gy", across))
        latent = owner(mine, lax.ppermute(send, "gy", near_y), coarse_x, coarse_y)
    else:
        low = lax.axis_index("gy") < count_y // 2
        total = jnp.concatenate([jnp.where(low, mine, send), jnp.where(low, send, mine)])
        latent = lax.psum_scatter(total, "gy", scatter_dimension=0, tiled=True)
        latent = jnp.swapaxes(latent.reshape(coarse_z, coarse_x, coarse_y), 0, 1)
    latent = jnp.swapaxes(latent, 1, 2)
    return phase_out, solute_out, latent


def solution(mesh):
    in_specs = (P("gx", "gy", None), P("gx", "gy", None), P("gx", None, "gy"))
    out_specs = (P("gx", "gy", None), P("gx", "gy", None), P("gx", None, "gy"))
    return jax.shard_map(body, mesh=mesh, in_specs=in_specs, out_specs=out_specs, check_vma=False)
```

```python
import functools

import jax
import jax.numpy as jnp
from jax import lax
from jax.experimental import pallas as pl
from jax.experimental.pallas import tpu as pltpu
from jax.sharding import PartitionSpec as P

time_step = 0.1
anisotropy = 0.3
coupling = 2.0
rejection = 0.5

F32 = jnp.float32
HALO = 4
STRIP = 4
ROWS = 8
LANES = 128
VMEM_LIMIT = 24 * 1024 * 1024


def vmem():
    return pl.BlockSpec(memory_space=pltpu.VMEM)


def anywhere():
    return pl.BlockSpec(memory_space=pl.ANY)


def hbm():
    return pl.BlockSpec(memory_space=pltpu.HBM)


def pairs(count, first):
    forward = [((first + k) % count, (first + k + 1) % count) for k in range(0, count, 2)]
    return forward + [(b, a) for a, b in forward]


def flips(me):
    odd = lax.rem(me, 2)
    return me, me + 1 - 2 * odd, lax.rem(me + 2, 4), 3 - me


def halves(value):
    coarse = value.astype(jnp.bfloat16)
    return coarse, (value - coarse.astype(F32)).astype(jnp.bfloat16)


def product(left, right, contract):
    dot = lambda a, b: lax.dot_general(a, b, ((contract[:1], contract[1:]), ((), ())), preferred_element_type=F32)
    if left.dtype == jnp.bfloat16:
        parts = [dot(left, part) for part in halves(right)]
    else:
        parts = [dot(part, right) for part in halves(left)]
    return parts[0] + parts[1]


def row_ids(shape):
    return lax.broadcasted_iota(jnp.int32, shape, len(shape) - 2)


def lane_ids(shape):
    return lax.broadcasted_iota(jnp.int32, shape, len(shape) - 1)


def start_all(copies, sems):
    copies = [pltpu.make_async_copy(source, target, sems.at[n]) for n, (source, target) in enumerate(copies)]
    for copy in copies:
        copy.start()
    return copies


def wait_all(copies):
    for copy in copies:
        copy.wait()


def fold(table):
    half = table.shape[0] // 2
    return jnp.concatenate([table[:half], table[half:]], axis=1)


def unfold(tile):
    return jnp.concatenate([tile[:, :LANES], tile[:, LANES:]], axis=0)


def pack_kernel(
    phase, solute, macro, phase_here, solute_here, face_a, face_b, side_a, strip_b, rest_b, table, local, sems
):
    size_x, size_y, size_z = phase.shape
    odd_x = lax.rem(lax.axis_index("gx"), 2)
    even_y = lax.rem(lax.axis_index("gy"), 2) == 0
    copies = []
    for at in range(0, size_x, HALO):
        for ref, here in ((phase, phase_here), (solute, solute_here)):
            copies.append((ref.at[pl.ds(at, HALO)], here.at[pl.ds(at, HALO)]))
    copies.append((macro, local))
    copies = start_all(copies, sems)
    wait_all(copies)
    for field, here in enumerate((phase_here, solute_here)):
        face_a[field] = here[pl.ds((1 - odd_x) * (size_x - HALO), HALO)]
        face_b[field] = here[pl.ds(odd_x * (size_x - HALO), HALO)]
    low = [here[:, pl.ds(0, ROWS), :] for here in (phase_here, solute_here)]
    high = [here[:, pl.ds(size_y - ROWS, ROWS), :] for here in (phase_here, solute_here)]
    wide = jnp.concatenate([local[k] for k in range(local.shape[0])], axis=1)
    table[...] = wide
    top = row_ids((size_x, ROWS, size_z)) < HALO
    low_side = jnp.where(top, low[0], pltpu.roll(low[1], HALO, 1))
    high_side = jnp.where(top, pltpu.roll(high[1], HALO, 1), high[0])
    side_a[pl.ds(0, size_x)] = jnp.where(even_y, high_side, low_side)
    side_b = jnp.where(even_y, low_side, high_side)
    strip_b[pl.ds(0, STRIP)] = side_b[:STRIP]
    strip_b[pl.ds(STRIP, STRIP)] = side_b[size_x - STRIP :]
    rest_b[...] = side_b[STRIP : size_x - STRIP]
    if side_a.shape[0] > size_x:
        side_a[size_x] = fold(wide)
        strip_b[2 * STRIP] = fold(wide)


def pack(phase, solute, macro, ride):
    size_x, size_y, size_z = phase.shape
    coarse_x, coarse_z, coarse_y = macro.shape
    field = jax.ShapeDtypeStruct(phase.shape, F32)
    face = jax.ShapeDtypeStruct((2, HALO, size_y, size_z), F32)
    counts = (size_x, 2 * STRIP, size_x - 2 * STRIP)
    extra = (1, 2, 0) if ride else (0, 0, 0)
    sides = [jax.ShapeDtypeStruct((count + more, ROWS, size_z), F32) for count, more in zip(counts, extra)]
    table = jax.ShapeDtypeStruct((coarse_z, coarse_x * coarse_y), F32)
    return pl.pallas_call(
        pack_kernel,
        out_shape=(field, field, face, face, *sides, table),
        in_specs=[hbm()] * 3,
        out_specs=[vmem()] * 8,
        scratch_shapes=[pltpu.VMEM(macro.shape, F32), pltpu.SemaphoreType.DMA((1 + 2 * (size_x // HALO),))],
        compiler_params=pltpu.CompilerParams(vmem_limit_bytes=VMEM_LIMIT),
        cost_estimate=pl.CostEstimate(flops=10**5, bytes_accessed=2 * 10**6, transcendentals=0),
        name="pack",
    )(phase, solute, macro)


def append_kernel(arrived, side, out):
    out[side.shape[0] - 1] = arrived[arrived.shape[0] - 1]


def append(arrived, side):
    return pl.pallas_call(
        append_kernel,
        out_shape=jax.ShapeDtypeStruct(side.shape, F32),
        in_specs=[vmem(), vmem()],
        out_specs=vmem(),
        input_output_aliases={1: 0},
        compiler_params=pltpu.CompilerParams(vmem_limit_bytes=VMEM_LIMIT),
        cost_estimate=pl.CostEstimate(flops=0, bytes_accessed=10**5, transcendentals=0),
        name="append",
    )(arrived, side)


def near_rows(block, coarse_y):
    shape = (2 * ROWS, coarse_y)
    wanted = lax.rem(row_ids(shape) + lax.axis_index("gy") * ROWS + coarse_y - 1, coarse_y)
    pick = (lane_ids(shape) == wanted).astype(F32).astype(jnp.bfloat16)
    return product(pick, block, (1, 1))


def pack_edge(rows):
    pieces = rows[:ROWS], pltpu.roll(rows[:ROWS], 4, 0), rows[ROWS:], pltpu.roll(rows[ROWS:], 4, 0)
    return jnp.concatenate(pieces, axis=1)


def unpack_edge(tile):
    quarter = tile.shape[1] // 4
    pieces = [tile[:, at : at + quarter] for at in range(0, tile.shape[1], quarter)]
    top = row_ids(pieces[0].shape) < 4
    halves = [jnp.where(top, pieces[n], pltpu.roll(pieces[n + 1], 4, 0)) for n in (0, 2)]
    return jnp.concatenate(halves, axis=0)


def corner_kernel(coarse_y, gathered, side_a, strip_b, table, coarse, corner_a, corner_b):
    size_x = side_a.shape[0] - (0 if gathered else 1)
    me = lax.axis_index("gy")
    even_x = lax.rem(lax.axis_index("gx"), 2) == 0
    even_y = lax.rem(me, 2) == 0
    block = table[...]
    if not gathered:
        near, across, far = flips(me)[1:]
        depth = table.shape[0]
        tiles = (me, block), (near, unfold(side_a[size_x])), (far, unfold(strip_b[2 * STRIP])), (across, unfold(strip_b[2 * STRIP + 1]))
        for source, tile in tiles:
            coarse[pl.ds(pl.multiple_of(source * depth, depth), depth), :] = tile
        block = coarse[...]
    depth, width = block.shape
    flipped = [block[:, at : at + coarse_y] for at in range(width - coarse_y, -1, -coarse_y)]
    block = jnp.where(even_x, block, jnp.concatenate(flipped, axis=1))
    coarse[...] = block
    row = row_ids(side_a.shape[1:])
    edges = block[:, width - coarse_y :], block[:, :coarse_y]
    for corner, top_side, edge in ((corner_a, even_x, edges[0]), (corner_b, jnp.logical_not(even_x), edges[1])):

        def layer(d, high):
            first = side_a[jnp.where(top_side, size_x - d, d - 1)]
            second = strip_b[jnp.where(top_side, 2 * STRIP - d, d - 1)]
            return jnp.where(even_y, first, second) if high else jnp.where(even_y, second, first)

        spare = pack_edge(near_rows(edge, coarse_y))
        tile = jnp.where(row == 4, pltpu.roll(layer(3, False), 5, 0), layer(1, False))
        corner[0] = jnp.where(row < 2, spare, tile)
        tile = jnp.where(row == 3, pltpu.roll(layer(3, True), 3, 0), layer(1, True))
        corner[1] = jnp.where(row >= 6, pltpu.roll(spare, 4, 0), tile)
        corner[2] = jnp.where(row % 4 < 2, layer(2, True), layer(2, False))


def corners(side_a, strip_b, table, coarse_y, coarse_shape):
    size_z = side_a.shape[2]
    corner = jax.ShapeDtypeStruct((3, ROWS, size_z), F32)
    coarse = jax.ShapeDtypeStruct(coarse_shape, F32)
    return pl.pallas_call(
        functools.partial(corner_kernel, coarse_y, table.shape == coarse_shape),
        out_shape=(coarse, corner, corner),
        in_specs=[vmem()] * 3,
        out_specs=[vmem()] * 3,
        compiler_params=pltpu.CompilerParams(vmem_limit_bytes=VMEM_LIMIT),
        cost_estimate=pl.CostEstimate(flops=10**5, bytes_accessed=4 * 10**5, transcendentals=0),
        name="corners",
    )(side_a, strip_b, table)


def weights(ends, frac, tick):
    first, second = ends
    return jnp.where(tick == first, 1.0 - frac, 0.0) + jnp.where(tick == second, frac, 0.0)


def weights_z(depth, size_z):
    shape = (depth, size_z)
    fine = lane_ids(shape)
    lower = (2 * fine + 5) // 8 - 1
    frac = (2 * fine - 3 - 8 * lower).astype(F32) / 8.0
    ends = jnp.clip(lower, 0, depth - 1), jnp.clip(lower + 1, 0, depth - 1)
    return weights(ends, frac, row_ids(shape))


def interpolate(rows, along_z, size_y):
    deep = product(rows, along_z, (1, 0))
    shape = (size_y + 2 * HALO, 2 * ROWS)
    fine = row_ids(shape)
    fine = jnp.where(fine >= size_y + HALO, fine - shape[0], fine)
    lower = (2 * fine + 13) // 8 - 2
    frac = (2 * fine - 3 - 8 * lower).astype(F32) / 8.0
    along_y = weights((lower + 1, lower + 2), frac, lane_ids(shape)).astype(jnp.bfloat16)
    return [
        product(along_y, deep[at : at + 2 * ROWS], (1, 0))
        for at in range(0, rows.shape[0], 2 * ROWS)
    ]


def blend(x, fans):
    lower = (2 * x - 3) // 8
    frac = (2 * x - 3 - 8 * lower) / 8.0
    return (1.0 - frac) * fans[lower] + frac * fans[lower + 1]


def turn(value, by, axis):
    return pltpu.roll(value, by % value.shape[axis], axis)


def z_matrices(size_z):
    shape = (size_z, size_z)
    source, target = row_ids(shape), lane_ids(shape)
    hit = lambda at: (source == at).astype(F32)
    end = size_z - 1
    gradient = hit(jnp.minimum(target + 1, end)) - hit(jnp.maximum(target - 1, 0))
    difference = hit(target + 1) - hit(target - 1)
    laplace = hit(jnp.minimum(target + 2, end)) + hit(jnp.maximum(target - 2, 0)) - 6.0 * hit(target)
    return tuple(m.astype(jnp.bfloat16) for m in (gradient, difference, laplace))


def matrix_kernel(size_z, tile, out, along_z):
    for n, matrix in enumerate(z_matrices(size_z)):
        out[n] = matrix
    along_z[...] = weights_z(*along_z.shape).astype(jnp.bfloat16)


def z_products(size_z, tile):
    square = jax.ShapeDtypeStruct((3, size_z, size_z), jnp.bfloat16)
    return pl.pallas_call(
        functools.partial(matrix_kernel, size_z),
        out_shape=(square, jax.ShapeDtypeStruct((size_z // 4, size_z), jnp.bfloat16)),
        in_specs=[anywhere()],
        out_specs=[vmem()] * 2,
        compiler_params=pltpu.CompilerParams(vmem_limit_bytes=VMEM_LIMIT),
        cost_estimate=pl.CostEstimate(flops=10**6, bytes_accessed=4 * 10**5, transcendentals=0),
        name="products",
    )(tile)


def along(slabs, matrix):
    return product(slabs.reshape(-1, slabs.shape[-1]), matrix, (1, 0)).reshape(slabs.shape)


def z_difference(value, clamp):
    first, second = value[:, :LANES], value[:, LANES:]
    lane = lane_ids(first.shape)
    head, tail = lane == 0, lane == LANES - 1
    ends = (first, second) if clamp else (0.0, 0.0)
    ahead = turn(first, -1, 1), turn(second, -1, 1)
    behind = turn(first, 1, 1), turn(second, 1, 1)
    low = jnp.where(tail, ahead[1], ahead[0]) - jnp.where(head, ends[0], behind[0])
    high = jnp.where(tail, ends[1], ahead[1]) - jnp.where(head, behind[0], behind[1])
    return jnp.concatenate([low, high], axis=1)


def flux(before, here, after, along_z):
    along_x = after - before
    along_y = turn(here, -1, 0) - turn(here, 1, 0)
    sq_x = along_x * along_x
    sq_y = along_y * along_y
    both = sq_x + sq_y
    inverse = 1.0 / (both + 4.0)
    factor = 1.0 + anisotropy * (both * both - 8.0 * (sq_x * sq_y)) * (inverse * inverse)
    stiff = (0.25 * time_step) * (factor * factor)
    return stiff * along_x, stiff * along_y, stiff * along_z


def spread(flux_y):
    return turn(flux_y, -1, 0) - turn(flux_y, 1, 0)


def phase_change(here, conc, theta, divergence):
    square = 1.0 - here * here
    drive = square * (here - (coupling * square) * (theta + conc))
    return divergence + time_step * drive


def solute_step(conc, beyond_x, beyond_y, along_z, change):
    return conc + (0.25 * time_step) * (beyond_x + beyond_y + along_z) + rejection * change


def next_row(conc):
    return turn(conc, -2, 0) + turn(conc, 2, 0)


def restrict(changes, lanes, size_y, size_z, coarse_width):
    shape = (size_z, size_z // 4)
    pool_z = (row_ids(shape) // 4 == lane_ids(shape)).astype(F32).astype(jnp.bfloat16)
    shape = (size_y, coarse_width)
    cell, lane = row_ids(shape) // 4, lane_ids(shape)
    pool_y = [jnp.where(cell + at == lane, 0.5 / 64.0, 0.0).astype(jnp.bfloat16) for at in lanes]
    pooled = product(jnp.concatenate(changes, axis=0), pool_z, (1, 0))
    return product(pooled, jnp.concatenate(pool_y, axis=0), (0, 0))


def coarse_lane(u, size_x, size_y, coarse_y):
    last = size_x // 4 - 1
    x = u + lax.rem(lax.axis_index("gx"), 2) * (last - 2 * u)
    return x * coarse_y + lax.axis_index("gy") * (size_y // 4)


KEPT = ("p0", "c0", "dz0", "cz0", "gx0", "dv0", "p1", "c1", "dz1", "cz1", "gx1", "dv1", "th")


def spans(size_x):
    widths = dict(p0=0, c0=0, dz0=0, cz0=0, gx0=1, dv0=1, p1=2, c1=2, dz1=2, cz1=2, gx1=3, dv1=3, th=2)
    return {name: (widths[name], size_x - widths[name]) for name in KEPT}


def halo_rows(tile, top):
    zero = jnp.zeros_like(tile[0])
    low = tile[0], tile[2], pltpu.roll(tile[0], 3, 0), zero
    high = tile[1], tile[2], pltpu.roll(tile[1], 5, 0), zero
    return [
        (jnp.where(top, h, l), pltpu.roll(jnp.where(top, l, h), HALO, 0)) for l, h in zip(low, high)
    ]


def inner_kernel(
    coarse_y, phase, solute, side_a, strip_b, rest_b, coarse, matrices, along_z, phase_new, solute_new, latent, ends, *rest
):
    kept = dict(zip(KEPT, rest[: len(KEPT)]))
    (fz,) = rest[len(KEPT) :]
    size_x, size_y, size_z = phase.shape
    span = spans(size_x)
    odd_x = lax.rem(lax.axis_index("gx"), 2)
    even_y = lax.rem(lax.axis_index("gy"), 2) == 0
    at = lambda name, u: kept[name].at[u - span[name][0]]
    get = lambda name, u: kept[name][u - span[name][0]]
    place = lambda u: u + odd_x * (size_x - 1 - 2 * u)
    top = row_ids((ROWS, size_z)) < HALO
    for u in range(size_x):
        first = side_a[place(u)]
        if STRIP <= u < size_x - STRIP:
            second = rest_b[place(u) - STRIP]
        else:
            at_strip = u if u < STRIP else u - size_x + 2 * STRIP
            second = strip_b[at_strip + odd_x * (2 * STRIP - 1 - 2 * at_strip)]
        low, high = jnp.where(even_y, second, first), jnp.where(even_y, first, second)
        at("p0", u)[pl.ds(0, size_y), :] = phase[place(u)]
        at("c0", u)[pl.ds(0, size_y), :] = solute[place(u)]
        at("p0", u)[pl.ds(size_y, ROWS), :] = jnp.where(top, high, low)
        at("c0", u)[pl.ds(size_y, ROWS), :] = pltpu.roll(jnp.where(top, low, high), HALO, 0)
    block = coarse[...]
    block = [near_rows(block[:, at : at + coarse_y], coarse_y) for at in range(0, block.shape[1], coarse_y)]
    fans = dict(enumerate(interpolate(jnp.concatenate(block, axis=0), along_z[...], size_y)))
    ends[0], ends[1] = fans[0], fans[len(fans) - 1]
    for u in range(*span["th"]):
        at("th", u)[...] = blend(u, fans)

    for step in "01":
        p, c, dz, cz, gx, dv = (name + step for name in ("p", "c", "dz", "cz", "gx", "dv"))
        kept[dz][...] = along(kept[p][...], matrices[0])
        kept[cz][...] = along(kept[c][...], matrices[2])
        begin, end = span[gx]
        for u in range(begin, end):
            flux_x, flux_y, flux_z = flux(get(p, u - 1), get(p, u), get(p, u + 1), get(dz, u))
            at(gx, u)[...] = flux_x
            at(dv, u)[...] = spread(flux_y)
            fz[u - begin] = flux_z
        kept[dv][...] += along(fz[pl.ds(0, end - begin)], matrices[1])
        take = (lambda v: v) if step == "0" else (lambda v: v[:size_y])
        for u in range(begin + 1, end - 1):
            here, conc = take(get(p, u)), get(c, u)
            divergence = take(get(gx, u + 1)) - take(get(gx, u - 1)) + take(get(dv, u))
            change = phase_change(here, take(conc), take(get("th", u)), divergence)
            beyond = take(get(c, u + 2)) + take(get(c, u - 2))
            new_conc = solute_step(take(conc), beyond, take(next_row(conc)), take(get(cz, u)), change)
            if step == "0":
                at("p1", u)[...] = here + change
                at("c1", u)[...] = new_conc
            else:
                phase_new[place(u) - HALO] = here + change
                solute_new[place(u) - HALO] = new_conc
    changes, lanes = [], []
    for k in range(1, size_x // 4 - 1):
        change = jnp.zeros((size_y, size_z), F32)
        for u in range(4 * k, 4 * k + 4):
            change = change + (phase_new[place(u) - HALO] - get("p0", u)[:size_y])
        changes.append(change)
        lanes.append(coarse_lane(k, size_x, size_y, coarse_y))
    latent[...] = restrict(changes, lanes, size_y, size_z, latent.shape[1])


def inner(phase, solute, side_a, strip_b, rest_b, coarse, matrices, along_z, coarse_y):
    size_x, size_y, size_z = phase.shape
    rows = size_y + 2 * HALO
    part = jax.ShapeDtypeStruct((size_x - 2 * HALO, size_y, size_z), F32)
    kept = [jax.ShapeDtypeStruct((end - begin, rows, size_z), F32) for begin, end in spans(size_x).values()]
    latent = jax.ShapeDtypeStruct((size_z // 4, coarse.shape[1]), F32)
    return pl.pallas_call(
        functools.partial(inner_kernel, coarse_y),
        out_shape=(part, part, latent, jax.ShapeDtypeStruct((2, rows, size_z), F32), *kept),
        in_specs=[vmem()] * 8,
        out_specs=[vmem()] * (4 + len(kept)),
        scratch_shapes=[pltpu.VMEM((size_x - 2, rows, size_z), F32)],
        compiler_params=pltpu.CompilerParams(vmem_limit_bytes=VMEM_LIMIT),
        cost_estimate=pl.CostEstimate(flops=5 * 10**8, bytes_accessed=5 * 10**6, transcendentals=0),
        name="inner",
    )(phase, solute, side_a, strip_b, rest_b, coarse, matrices, along_z)


def rim_halo(near, face, corner, phase_halo, solute_halo):
    _, _, size_y, size_z = face.shape
    odd_x = lax.rem(lax.axis_index("gx"), 2)
    flip = odd_x if near else 1 - odd_x
    top = row_ids((ROWS, size_z)) < HALO
    for d, (p_rows, c_rows) in enumerate(halo_rows(corner, top)):
        layer = d + flip * (HALO - 1 - 2 * d)
        for n, (field, rows) in enumerate(((phase_halo, p_rows), (solute_halo, c_rows))):
            field[HALO - 1 - d, pl.ds(0, size_y), :] = face[n, layer]
            field[HALO - 1 - d, pl.ds(size_y, ROWS), :] = rows


def edge_fan(corner, along_z, size_y):
    edge = jnp.where(row_ids(corner.shape[1:]) < 2, corner[0], pltpu.roll(corner[1], 4, 0))
    return interpolate(unpack_edge(edge), along_z[...], size_y)[0]


def rim_spot(near):
    odd_x = lax.rem(lax.axis_index("gx"), 2)
    flip = odd_x if near else 1 - odd_x
    return lambda v: v + (1 - flip) * (HALO - 1 - 2 * v)


def rim_march(near, size_x, halo, fans, matrices, kept, scratch, p1, c1, phase_new, result):
    hp0, hc0, fan = halo
    gx, dv, dz, cz, th = scratch
    _, size_y, size_z = phase_new.shape
    span = spans(size_x)
    spot = rim_spot(near)

    def get(name, v):
        begin, end = span[name]
        if v >= begin:
            found = kept[name][(size_x - 1 - v if near else v) - begin]
            return -found if near and name.startswith("gx") else found
        own, first = dict(
            p0=(hp0, -4), c0=(hc0, -4), dz0=(dz, -3), cz0=(cz, -2), gx0=(gx, -3), dv0=(dv, -2),
            p1=(p1, -2), c1=(c1, -2), dz1=(dz, -1), gx1=(gx, -1), dv1=(dv, 0), th=(th, -2),
        )[name]
        return own[v - first]

    moved = []
    ends = {-1: fan, 0: fans[1 if near else 0]}
    for v in range(-2, 2):
        th[v + 2] = blend(v, ends)
    for step, begin in (("0", -3), ("1", -1)):
        p, c, gx_, dv_, dz_, cz_ = (name + step for name in ("p", "c", "gx", "dv", "dz", "cz"))
        for n in range(3):
            dz[n] = z_difference((hp0 if step == "0" else p1)[n + 1], True)
        if step == "0":
            cz[...] = along(hc0[pl.ds(2, 2)], matrices[2])
        yield
        for v in range(begin, begin + 4):
            flux_x, flux_y, flux_z = flux(get(p, v - 1), get(p, v), get(p, v + 1), get(dz_, v))
            gx[v - begin] = flux_x
            if v > begin:
                dv[v - begin - 1] = spread(flux_y) + z_difference(flux_z, False)
        yield
        take = (lambda w: w) if step == "0" else (lambda w: w[:size_y])
        for v in range(begin + 1, begin + 5):
            here, conc = take(get(p, v)), get(c, v)
            divergence = take(get(gx_, v + 1)) - take(get(gx_, v - 1)) + take(get(dv_, v))
            change = phase_change(here, take(conc), take(get("th", v)), divergence)
            if step == "0":
                beyond = get(c, v + 2) + get(c, v - 2)
                p1[v + 2] = here + change
                c1[v + 2] = solute_step(conc, beyond, next_row(conc), get(cz_, v), change)
            else:
                phase_new[spot(v)] = here + change
                moved.append(here + change - get("p0", v)[:size_y])
        yield
    result.append((moved[0] + moved[1]) + (moved[2] + moved[3]))


def near_kernel(face, corner, phase_halo, solute_halo):
    rim_halo(True, face, corner, phase_halo, solute_halo)


def near_halo(face, corner):
    _, _, size_y, size_z = face.shape
    slabs = jax.ShapeDtypeStruct((HALO, size_y + 2 * HALO, size_z), F32)
    return pl.pallas_call(
        near_kernel,
        out_shape=(slabs, slabs),
        in_specs=[vmem()] * 2,
        out_specs=[vmem()] * 2,
        compiler_params=pltpu.CompilerParams(vmem_limit_bytes=VMEM_LIMIT),
        cost_estimate=pl.CostEstimate(flops=15 * 10**8, bytes_accessed=15 * 10**6, transcendentals=0),
        name="near",
    )(face, corner)


def rim_kernel(
    coarse_y, size_x, face, corner, near_phase, near_solute, near_corner, fans, matrices, along_z, inner_latent, *rest
):
    kept = dict(zip(KEPT, rest[: len(KEPT)]))
    outs, (far_phase, far_solute, total, *scratch) = rest[len(KEPT) : len(KEPT) + 8], rest[len(KEPT) + 8 :]
    near_new, far_new, keep, send = outs[:3], outs[3:6], outs[6], outs[7]
    _, _, size_y, size_z = face.shape
    width = total.shape[1]
    rim_halo(False, face, corner, far_phase, far_solute)
    changes = []
    half = len(scratch) // 2
    near = near_phase, near_solute, edge_fan(near_corner, along_z, size_y)
    far = far_phase, far_solute, edge_fan(corner, along_z, size_y)
    sides = [
        rim_march(True, size_x, near, fans, matrices, kept, scratch[:half], *near_new, changes),
        rim_march(False, size_x, far, fans, matrices, kept, scratch[half:], *far_new, changes),
    ]
    while sides:
        sides = [side for side in sides if next(side, sides) is not sides]
    lanes = [coarse_lane(u, size_x, size_y, coarse_y) for u in (size_x // 4 - 1, 0)]
    total[...] = restrict(changes, lanes, size_y, size_z, width) + inner_latent[...]
    halve(total, lax.div(2 * lax.axis_index("gy"), lax.axis_size("gy")), keep, send)


def halve(total, side, keep, send):
    half = keep.shape[0]
    keep[...] = total[pl.ds(pl.multiple_of(side * half, half), half), :]
    send[...] = total[pl.ds(pl.multiple_of((1 - side) * half, half), half), :]


def rims(shape, face, corner, near, fans, matrices, along_z, inner_latent, kept, coarse_y):
    size_x, size_y, size_z = shape
    rows = size_y + 2 * HALO
    part = jax.ShapeDtypeStruct((HALO, size_y, size_z), F32)
    width = inner_latent.shape[1]
    half = jax.ShapeDtypeStruct((size_z // 8, width), F32)
    state = jax.ShapeDtypeStruct((HALO, rows, size_z), F32)
    slabs = lambda count: pltpu.VMEM((count, rows, size_z), F32)
    return pl.pallas_call(
        functools.partial(rim_kernel, coarse_y, size_x),
        out_shape=(state, state, part, state, state, part, half, half),
        in_specs=[vmem()] * (9 + len(kept)),
        out_specs=[vmem()] * 8,
        scratch_shapes=[
            slabs(HALO), slabs(HALO), pltpu.VMEM((size_z // 4, width), F32),
            *[slabs(count) for count in 2 * (4, 3, 3, 2, 4)],
        ],
        compiler_params=pltpu.CompilerParams(vmem_limit_bytes=VMEM_LIMIT),
        cost_estimate=pl.CostEstimate(flops=10**7, bytes_accessed=3 * 10**6, transcendentals=0),
        name="rims",
    )(face, corner, *near, fans, matrices, along_z, inner_latent, *kept)


def rim_solute(near, size_x, p1, c1, phase_new, matrices, kept, out):
    _, size_y, size_z = phase_new.shape
    span = spans(size_x)
    spot = rim_spot(near)
    own = {"p1": p1[...], "c1": c1[...], "cz1": along(c1[pl.ds(2, 2)], matrices[2])}

    def get(name, v):
        begin, _ = span[name]
        if v >= begin:
            return kept[name][(size_x - 1 - v if near else v) - begin]
        return own[name][v if name == "cz1" else v + 2]

    for v in range(HALO):
        conc = get("c1", v)
        change = phase_new[spot(v)] - get("p1", v)[:size_y]
        beyond = get("c1", v + 2)[:size_y] + get("c1", v - 2)[:size_y]
        out[spot(v)] = solute_step(
            conc[:size_y], beyond, next_row(conc)[:size_y], get("cz1", v)[:size_y], change
        )


def store_kernel(
    middle_phase, middle_solute, near_p1, near_c1, near_phase, far_p1, far_c1, far_phase, matrices, p1, c1, cz1,
    phase_out, solute_out, near_solute, far_solute, sems,
):
    size_x = phase_out.shape[0]
    odd_x = lax.rem(lax.axis_index("gx"), 2)
    near = (1 - odd_x) * (size_x - HALO)
    far = size_x - HALO - near
    put = lambda part, out, at: (part, out.at[pl.ds(at, part.shape[0])])
    copies = start_all(
        [
            put(middle_phase, phase_out, HALO), put(middle_solute, solute_out, HALO), put(near_phase, phase_out, near),
            put(far_phase, phase_out, far),
        ],
        sems,
    )
    kept = dict(p1=p1, c1=c1, cz1=cz1)
    rim_solute(True, size_x, near_p1, near_c1, near_phase, matrices, kept, near_solute)
    rim_solute(False, size_x, far_p1, far_c1, far_phase, matrices, kept, far_solute)
    copies += start_all(
        [put(near_solute, solute_out, near), put(far_solute, solute_out, far)], sems.at[pl.ds(4, 2)]
    )
    wait_all(copies)


def store(shape, middle, edges, matrices, kept):
    kept = dict(zip(KEPT, kept))
    out = jax.ShapeDtypeStruct(shape, F32)
    part = pltpu.VMEM((HALO, *shape[1:]), F32)
    return pl.pallas_call(
        store_kernel,
        out_shape=(out, out),
        in_specs=[vmem()] * 12,
        out_specs=[hbm()] * 2,
        scratch_shapes=[part, part, pltpu.SemaphoreType.DMA((6,))],
        compiler_params=pltpu.CompilerParams(vmem_limit_bytes=VMEM_LIMIT),
        cost_estimate=pl.CostEstimate(flops=0, bytes_accessed=4 * 10**6, transcendentals=0),
        name="store",
    )(*middle, *edges, matrices, kept["p1"], kept["c1"], kept["cz1"])


def merge_kernel(mine, arrived, keep, send, total):
    total[...] = mine[...] + arrived[...]
    halve(total, lax.rem(lax.axis_index("gy"), 2), keep, send)


def merge(mine, arrived):
    half = jax.ShapeDtypeStruct((mine.shape[0] // 2, mine.shape[1]), F32)
    return pl.pallas_call(
        merge_kernel,
        out_shape=(half, half),
        in_specs=[vmem()] * 2,
        out_specs=[vmem()] * 2,
        scratch_shapes=[pltpu.VMEM(mine.shape, F32)],
        compiler_params=pltpu.CompilerParams(vmem_limit_bytes=VMEM_LIMIT),
        cost_estimate=pl.CostEstimate(flops=10**4, bytes_accessed=10**5, transcendentals=0),
        name="merge",
    )(mine, arrived)


def owner_kernel(mine, arrived, out):
    total = mine[...] + arrived[...]
    coarse_x, _, coarse_y = out.shape
    for k in range(coarse_x):
        out[k] = total[:, k * coarse_y : (k + 1) * coarse_y]


def owner(mine, arrived, coarse_x, coarse_y):
    coarse_z = mine.shape[0]
    return pl.pallas_call(
        owner_kernel,
        out_shape=jax.ShapeDtypeStruct((coarse_x, coarse_z, coarse_y), F32),
        in_specs=[vmem()] * 2,
        out_specs=vmem(),
        compiler_params=pltpu.CompilerParams(vmem_limit_bytes=VMEM_LIMIT),
        cost_estimate=pl.CostEstimate(flops=10**4, bytes_accessed=10**5, transcendentals=0),
        name="owner",
    )(mine, arrived)


def body(phase, solute, macro_temp):
    count_x, count_y = lax.axis_size("gx"), lax.axis_size("gy")
    coarse_x, coarse_y, coarse_z = macro_temp.shape
    near_x, far_x = pairs(count_x, 0), pairs(count_x, 1)
    near_y, far_y = pairs(count_y, 0), pairs(count_y, 1)
    across = [(k, count_y - 1 - k) for k in range(count_y)]
    ride = count_y == 4
    macro = jnp.swapaxes(macro_temp, 1, 2)
    still = [pltpu.with_memory_space_constraint(v, pltpu.HBM) for v in (phase, solute, macro)]
    phase, solute, face_a, face_b, side_a, strip_b, rest_b, table = pack(*still, ride)
    coarse_shape = (coarse_z * count_y, coarse_x * coarse_y)
    face_a = lax.ppermute(face_a, "gx", near_x)
    side_a = lax.ppermute(side_a, "gy", near_y)
    if ride:
        strip_b = append(side_a, strip_b)
    else:
        table = lax.all_gather(table, "gy").reshape(coarse_shape)
    matrices, along_z = z_products(phase.shape[2], strip_b)
    face_b, rest_b, matrices = lax.optimization_barrier((face_b, rest_b, matrices))
    strip_b = lax.ppermute(strip_b, "gy", far_y)
    rest_b = lax.ppermute(rest_b, "gy", far_y)
    face_b = lax.ppermute(face_b, "gx", far_x)
    coarse, corner_a, corner_b = corners(side_a, strip_b, table, coarse_y, coarse_shape)
    corner_a = lax.ppermute(corner_a, "gx", near_x)
    corner_b = lax.ppermute(corner_b, "gx", far_x)
    results = inner(phase, solute, side_a, strip_b, rest_b, coarse, matrices, along_z, coarse_y)
    middle, inner_latent, fans, kept = results[:2], results[2], results[3], results[4:]
    near = (*near_halo(face_a, corner_a), corner_a)
    *edges, mine, send = rims(
        phase.shape, face_b, corner_b, near, fans, matrices, along_z, inner_latent, kept, coarse_y
    )
    phase_out, solute_out = store(phase.shape, middle, edges, matrices, kept)
    if ride:
        mine, send = merge(mine, lax.ppermute(send, "gy", across))
        latent = owner(mine, lax.ppermute(send, "gy", near_y), coarse_x, coarse_y)
    else:
        low = lax.axis_index("gy") < count_y // 2
        total = jnp.concatenate([jnp.where(low, mine, send), jnp.where(low, send, mine)])
        latent = lax.psum_scatter(total, "gy", scatter_dimension=0, tiled=True)
        latent = jnp.swapaxes(latent.reshape(coarse_z, coarse_x, coarse_y), 0, 1)
    latent = jnp.swapaxes(latent, 1, 2)
    return phase_out, solute_out, latent


def solution(mesh):
    in_specs = (P("gx", "gy", None), P("gx", "gy", None), P("gx", None, "gy"))
    out_specs = (P("gx", "gy", None), P("gx", "gy", None), P("gx", None, "gy"))
    return jax.shard_map(body, mesh=mesh, in_specs=in_specs, out_specs=out_specs, check_vma=False)
```

```python
import functools

import jax
import jax.numpy as jnp
from jax import lax
from jax.experimental import pallas as pl
from jax.experimental.pallas import tpu as pltpu
from jax.sharding import PartitionSpec as P

time_step = 0.1
anisotropy = 0.3
coupling = 2.0
rejection = 0.5

F32 = jnp.float32
HALO = 4
STRIP = 4
ROWS = 8
LANES = 128
VMEM_LIMIT = 24 * 1024 * 1024


def vmem():
    return pl.BlockSpec(memory_space=pltpu.VMEM)


def anywhere():
    return pl.BlockSpec(memory_space=pl.ANY)


def hbm():
    return pl.BlockSpec(memory_space=pltpu.HBM)


def pairs(count, first):
    forward = [((first + k) % count, (first + k + 1) % count) for k in range(0, count, 2)]
    return forward + [(b, a) for a, b in forward]


def flips(me):
    odd = lax.rem(me, 2)
    return me, me + 1 - 2 * odd, lax.rem(me + 2, 4), 3 - me


def halves(value):
    coarse = value.astype(jnp.bfloat16)
    return coarse, (value - coarse.astype(F32)).astype(jnp.bfloat16)


def product(left, right, contract):
    dot = lambda a, b: lax.dot_general(a, b, ((contract[:1], contract[1:]), ((), ())), preferred_element_type=F32)
    if left.dtype == jnp.bfloat16:
        parts = [dot(left, part) for part in halves(right)]
    else:
        parts = [dot(part, right) for part in halves(left)]
    return parts[0] + parts[1]


def row_ids(shape):
    return lax.broadcasted_iota(jnp.int32, shape, len(shape) - 2)


def lane_ids(shape):
    return lax.broadcasted_iota(jnp.int32, shape, len(shape) - 1)


def start_all(copies, sems):
    copies = [pltpu.make_async_copy(source, target, sems.at[n]) for n, (source, target) in enumerate(copies)]
    for copy in copies:
        copy.start()
    return copies


def wait_all(copies):
    for copy in copies:
        copy.wait()


def fold(table):
    half = table.shape[0] // 2
    return jnp.concatenate([table[:half], table[half:]], axis=1)


def unfold(tile):
    return jnp.concatenate([tile[:, :LANES], tile[:, LANES:]], axis=0)


def pack_kernel(
    phase, solute, macro, phase_here, solute_here, face_a, face_b, side_a, strip_b, rest_b, table, local, sems
):
    size_x, size_y, size_z = phase.shape
    odd_x = lax.rem(lax.axis_index("gx"), 2)
    even_y = lax.rem(lax.axis_index("gy"), 2) == 0
    copies = [(macro, local)]
    for ref, here in ((phase, phase_here), (solute, solute_here)):
        for at in range(0, size_x, HALO):
            copies.append((ref.at[pl.ds(at, HALO)], here.at[pl.ds(at, HALO)]))
    copies = start_all(copies, sems)
    half = 1 + size_x // HALO
    for field, (here, batch) in enumerate(((phase_here, copies[:half]), (solute_here, copies[half:]))):
        wait_all(batch)
        face_a[field] = here[pl.ds((1 - odd_x) * (size_x - HALO), HALO)]
        face_b[field] = here[pl.ds(odd_x * (size_x - HALO), HALO)]
        if field == 0:
            wide = jnp.concatenate([local[k] for k in range(local.shape[0])], axis=1)
            table[...] = wide
    low = [here[:, pl.ds(0, ROWS), :] for here in (phase_here, solute_here)]
    high = [here[:, pl.ds(size_y - ROWS, ROWS), :] for here in (phase_here, solute_here)]
    top = row_ids((size_x, ROWS, size_z)) < HALO
    low_side = jnp.where(top, low[0], pltpu.roll(low[1], HALO, 1))
    high_side = jnp.where(top, pltpu.roll(high[1], HALO, 1), high[0])
    side_a[pl.ds(0, size_x)] = jnp.where(even_y, high_side, low_side)
    side_b = jnp.where(even_y, low_side, high_side)
    strip_b[pl.ds(0, STRIP)] = side_b[:STRIP]
    strip_b[pl.ds(STRIP, STRIP)] = side_b[size_x - STRIP :]
    rest_b[...] = side_b[STRIP : size_x - STRIP]
    if side_a.shape[0] > size_x:
        side_a[size_x] = fold(wide)
        strip_b[2 * STRIP] = fold(wide)


def pack(phase, solute, macro, ride):
    size_x, size_y, size_z = phase.shape
    coarse_x, coarse_z, coarse_y = macro.shape
    field = jax.ShapeDtypeStruct(phase.shape, F32)
    face = jax.ShapeDtypeStruct((2, HALO, size_y, size_z), F32)
    counts = (size_x, 2 * STRIP, size_x - 2 * STRIP)
    extra = (1, 2, 0) if ride else (0, 0, 0)
    sides = [jax.ShapeDtypeStruct((count + more, ROWS, size_z), F32) for count, more in zip(counts, extra)]
    table = jax.ShapeDtypeStruct((coarse_z, coarse_x * coarse_y), F32)
    return pl.pallas_call(
        pack_kernel,
        out_shape=(field, field, face, face, *sides, table),
        in_specs=[hbm()] * 3,
        out_specs=[vmem()] * 8,
        scratch_shapes=[pltpu.VMEM(macro.shape, F32), pltpu.SemaphoreType.DMA((1 + 2 * (size_x // HALO),))],
        compiler_params=pltpu.CompilerParams(vmem_limit_bytes=VMEM_LIMIT),
        cost_estimate=pl.CostEstimate(flops=10**5, bytes_accessed=2 * 10**6, transcendentals=0),
        name="pack",
    )(phase, solute, macro)


def append_kernel(arrived, side, out):
    out[side.shape[0] - 1] = arrived[arrived.shape[0] - 1]


def append(arrived, side):
    return pl.pallas_call(
        append_kernel,
        out_shape=jax.ShapeDtypeStruct(side.shape, F32),
        in_specs=[vmem(), vmem()],
        out_specs=vmem(),
        input_output_aliases={1: 0},
        compiler_params=pltpu.CompilerParams(vmem_limit_bytes=VMEM_LIMIT),
        cost_estimate=pl.CostEstimate(flops=0, bytes_accessed=10**5, transcendentals=0),
        name="append",
    )(arrived, side)


def near_rows(block, coarse_y):
    shape = (2 * ROWS, coarse_y)
    wanted = lax.rem(row_ids(shape) + lax.axis_index("gy") * ROWS + coarse_y - 1, coarse_y)
    pick = (lane_ids(shape) == wanted).astype(F32).astype(jnp.bfloat16)
    return product(pick, block, (1, 1))


def pack_edge(rows):
    pieces = rows[:ROWS], pltpu.roll(rows[:ROWS], 4, 0), rows[ROWS:], pltpu.roll(rows[ROWS:], 4, 0)
    return jnp.concatenate(pieces, axis=1)


def unpack_edge(tile):
    quarter = tile.shape[1] // 4
    pieces = [tile[:, at : at + quarter] for at in range(0, tile.shape[1], quarter)]
    top = row_ids(pieces[0].shape) < 4
    halves = [jnp.where(top, pieces[n], pltpu.roll(pieces[n + 1], 4, 0)) for n in (0, 2)]
    return jnp.concatenate(halves, axis=0)


def corner_kernel(coarse_y, gathered, side_a, strip_b, table, coarse, corner_a, corner_b):
    size_x = side_a.shape[0] - (0 if gathered else 1)
    me = lax.axis_index("gy")
    even_x = lax.rem(lax.axis_index("gx"), 2) == 0
    even_y = lax.rem(me, 2) == 0
    block = table[...]
    if not gathered:
        near, across, far = flips(me)[1:]
        depth = table.shape[0]
        tiles = (me, block), (near, unfold(side_a[size_x])), (far, unfold(strip_b[2 * STRIP])), (across, unfold(strip_b[2 * STRIP + 1]))
        for source, tile in tiles:
            coarse[pl.ds(pl.multiple_of(source * depth, depth), depth), :] = tile
        block = coarse[...]
    depth, width = block.shape
    flipped = [block[:, at : at + coarse_y] for at in range(width - coarse_y, -1, -coarse_y)]
    block = jnp.where(even_x, block, jnp.concatenate(flipped, axis=1))
    coarse[...] = block
    row = row_ids(side_a.shape[1:])
    edges = block[:, width - coarse_y :], block[:, :coarse_y]
    for corner, top_side, edge in ((corner_a, even_x, edges[0]), (corner_b, jnp.logical_not(even_x), edges[1])):

        def layer(d, high):
            first = side_a[jnp.where(top_side, size_x - d, d - 1)]
            second = strip_b[jnp.where(top_side, 2 * STRIP - d, d - 1)]
            return jnp.where(even_y, first, second) if high else jnp.where(even_y, second, first)

        spare = pack_edge(near_rows(edge, coarse_y))
        tile = jnp.where(row == 4, pltpu.roll(layer(3, False), 5, 0), layer(1, False))
        corner[0] = jnp.where(row < 2, spare, tile)
        tile = jnp.where(row == 3, pltpu.roll(layer(3, True), 3, 0), layer(1, True))
        corner[1] = jnp.where(row >= 6, pltpu.roll(spare, 4, 0), tile)
        corner[2] = jnp.where(row % 4 < 2, layer(2, True), layer(2, False))


def corners(side_a, strip_b, table, coarse_y, coarse_shape):
    size_z = side_a.shape[2]
    corner = jax.ShapeDtypeStruct((3, ROWS, size_z), F32)
    coarse = jax.ShapeDtypeStruct(coarse_shape, F32)
    return pl.pallas_call(
        functools.partial(corner_kernel, coarse_y, table.shape == coarse_shape),
        out_shape=(coarse, corner, corner),
        in_specs=[vmem()] * 3,
        out_specs=[vmem()] * 3,
        compiler_params=pltpu.CompilerParams(vmem_limit_bytes=VMEM_LIMIT),
        cost_estimate=pl.CostEstimate(flops=10**5, bytes_accessed=4 * 10**5, transcendentals=0),
        name="corners",
    )(side_a, strip_b, table)


def weights(ends, frac, tick):
    first, second = ends
    return jnp.where(tick == first, 1.0 - frac, 0.0) + jnp.where(tick == second, frac, 0.0)


def weights_z(depth, size_z):
    shape = (depth, size_z)
    fine = lane_ids(shape)
    lower = (2 * fine + 5) // 8 - 1
    frac = (2 * fine - 3 - 8 * lower).astype(F32) / 8.0
    ends = jnp.clip(lower, 0, depth - 1), jnp.clip(lower + 1, 0, depth - 1)
    return weights(ends, frac, row_ids(shape))


def interpolate(rows, along_z, size_y):
    deep = product(rows, along_z, (1, 0))
    shape = (size_y + 2 * HALO, 2 * ROWS)
    fine = row_ids(shape)
    fine = jnp.where(fine >= size_y + HALO, fine - shape[0], fine)
    lower = (2 * fine + 13) // 8 - 2
    frac = (2 * fine - 3 - 8 * lower).astype(F32) / 8.0
    along_y = weights((lower + 1, lower + 2), frac, lane_ids(shape)).astype(jnp.bfloat16)
    return [
        product(along_y, deep[at : at + 2 * ROWS], (1, 0))
        for at in range(0, rows.shape[0], 2 * ROWS)
    ]


def blend(x, fans):
    lower = (2 * x - 3) // 8
    frac = (2 * x - 3 - 8 * lower) / 8.0
    return (1.0 - frac) * fans[lower] + frac * fans[lower + 1]


def turn(value, by, axis):
    return pltpu.roll(value, by % value.shape[axis], axis)


def z_matrices(size_z):
    shape = (size_z, size_z)
    source, target = row_ids(shape), lane_ids(shape)
    hit = lambda at: (source == at).astype(F32)
    end = size_z - 1
    gradient = hit(jnp.minimum(target + 1, end)) - hit(jnp.maximum(target - 1, 0))
    difference = hit(target + 1) - hit(target - 1)
    laplace = hit(jnp.minimum(target + 2, end)) + hit(jnp.maximum(target - 2, 0)) - 6.0 * hit(target)
    return tuple(m.astype(jnp.bfloat16) for m in (gradient, difference, laplace))


def matrix_kernel(size_z, tile, out, along_z):
    for n, matrix in enumerate(z_matrices(size_z)):
        out[n] = matrix
    along_z[...] = weights_z(*along_z.shape).astype(jnp.bfloat16)


def z_products(size_z, tile):
    square = jax.ShapeDtypeStruct((3, size_z, size_z), jnp.bfloat16)
    return pl.pallas_call(
        functools.partial(matrix_kernel, size_z),
        out_shape=(square, jax.ShapeDtypeStruct((size_z // 4, size_z), jnp.bfloat16)),
        in_specs=[anywhere()],
        out_specs=[vmem()] * 2,
        compiler_params=pltpu.CompilerParams(vmem_limit_bytes=VMEM_LIMIT),
        cost_estimate=pl.CostEstimate(flops=10**6, bytes_accessed=4 * 10**5, transcendentals=0),
        name="products",
    )(tile)


def along(slabs, matrix):
    return product(slabs.reshape(-1, slabs.shape[-1]), matrix, (1, 0)).reshape(slabs.shape)


def z_difference(value, clamp):
    first, second = value[:, :LANES], value[:, LANES:]
    lane = lane_ids(first.shape)
    head, tail = lane == 0, lane == LANES - 1
    ends = (first, second) if clamp else (0.0, 0.0)
    ahead = turn(first, -1, 1), turn(second, -1, 1)
    behind = turn(first, 1, 1), turn(second, 1, 1)
    low = jnp.where(tail, ahead[1], ahead[0]) - jnp.where(head, ends[0], behind[0])
    high = jnp.where(tail, ends[1], ahead[1]) - jnp.where(head, behind[0], behind[1])
    return jnp.concatenate([low, high], axis=1)


def flux(before, here, after, along_z):
    along_x = after - before
    along_y = turn(here, -1, 0) - turn(here, 1, 0)
    sq_x = along_x * along_x
    sq_y = along_y * along_y
    both = sq_x + sq_y
    inverse = 1.0 / (both + 4.0)
    factor = 1.0 + anisotropy * (both * both - 8.0 * (sq_x * sq_y)) * (inverse * inverse)
    stiff = (0.25 * time_step) * (factor * factor)
    return stiff * along_x, stiff * along_y, stiff * along_z


def spread(flux_y):
    return turn(flux_y, -1, 0) - turn(flux_y, 1, 0)


def phase_change(here, conc, theta, divergence):
    square = 1.0 - here * here
    drive = square * (here - (coupling * square) * (theta + conc))
    return divergence + time_step * drive


def solute_step(conc, beyond_x, beyond_y, along_z, change):
    return conc + (0.25 * time_step) * (beyond_x + beyond_y + along_z) + rejection * change


def next_row(conc):
    return turn(conc, -2, 0) + turn(conc, 2, 0)


def restrict(changes, lanes, size_y, size_z, coarse_width):
    shape = (size_z, size_z // 4)
    pool_z = (row_ids(shape) // 4 == lane_ids(shape)).astype(F32).astype(jnp.bfloat16)
    shape = (size_y, coarse_width)
    cell, lane = row_ids(shape) // 4, lane_ids(shape)
    pool_y = [jnp.where(cell + at == lane, 0.5 / 64.0, 0.0).astype(jnp.bfloat16) for at in lanes]
    pooled = product(jnp.concatenate(changes, axis=0), pool_z, (1, 0))
    return product(pooled, jnp.concatenate(pool_y, axis=0), (0, 0))


def coarse_lane(u, size_x, size_y, coarse_y):
    last = size_x // 4 - 1
    x = u + lax.rem(lax.axis_index("gx"), 2) * (last - 2 * u)
    return x * coarse_y + lax.axis_index("gy") * (size_y // 4)


KEPT = ("p0", "c0", "dz0", "cz0", "gx0", "dv0", "p1", "c1", "dz1", "cz1", "gx1", "dv1", "th")


def spans(size_x):
    widths = dict(p0=0, c0=0, dz0=0, cz0=0, gx0=1, dv0=1, p1=2, c1=2, dz1=2, cz1=2, gx1=3, dv1=3, th=2)
    return {name: (widths[name], size_x - widths[name]) for name in KEPT}


def halo_rows(tile, top):
    zero = jnp.zeros_like(tile[0])
    low = tile[0], tile[2], pltpu.roll(tile[0], 3, 0), zero
    high = tile[1], tile[2], pltpu.roll(tile[1], 5, 0), zero
    return [
        (jnp.where(top, h, l), pltpu.roll(jnp.where(top, l, h), HALO, 0)) for l, h in zip(low, high)
    ]


def inner_kernel(
    coarse_y, phase, solute, side_a, strip_b, rest_b, coarse, matrices, along_z, phase_new, solute_new, latent, ends, *rest
):
    kept = dict(zip(KEPT, rest[: len(KEPT)]))
    (fz,) = rest[len(KEPT) :]
    size_x, size_y, size_z = phase.shape
    span = spans(size_x)
    odd_x = lax.rem(lax.axis_index("gx"), 2)
    even_y = lax.rem(lax.axis_index("gy"), 2) == 0
    at = lambda name, u: kept[name].at[u - span[name][0]]
    get = lambda name, u: kept[name][u - span[name][0]]
    place = lambda u: u + odd_x * (size_x - 1 - 2 * u)
    top = row_ids((ROWS, size_z)) < HALO
    for u in range(size_x):
        first = side_a[place(u)]
        if STRIP <= u < size_x - STRIP:
            second = rest_b[place(u) - STRIP]
        else:
            at_strip = u if u < STRIP else u - size_x + 2 * STRIP
            second = strip_b[at_strip + odd_x * (2 * STRIP - 1 - 2 * at_strip)]
        low, high = jnp.where(even_y, second, first), jnp.where(even_y, first, second)
        at("p0", u)[pl.ds(0, size_y), :] = phase[place(u)]
        at("c0", u)[pl.ds(0, size_y), :] = solute[place(u)]
        at("p0", u)[pl.ds(size_y, ROWS), :] = jnp.where(top, high, low)
        at("c0", u)[pl.ds(size_y, ROWS), :] = pltpu.roll(jnp.where(top, low, high), HALO, 0)
    block = coarse[...]
    block = [near_rows(block[:, at : at + coarse_y], coarse_y) for at in range(0, block.shape[1], coarse_y)]
    fans = dict(enumerate(interpolate(jnp.concatenate(block, axis=0), along_z[...], size_y)))
    ends[0], ends[1] = fans[0], fans[len(fans) - 1]
    for u in range(*span["th"]):
        at("th", u)[...] = blend(u, fans)

    for step in "01":
        p, c, dz, cz, gx, dv = (name + step for name in ("p", "c", "dz", "cz", "gx", "dv"))
        kept[dz][...] = along(kept[p][...], matrices[0])
        kept[cz][...] = along(kept[c][...], matrices[2])
        begin, end = span[gx]
        for u in range(begin, end):
            flux_x, flux_y, flux_z = flux(get(p, u - 1), get(p, u), get(p, u + 1), get(dz, u))
            at(gx, u)[...] = flux_x
            at(dv, u)[...] = spread(flux_y)
            fz[u - begin] = flux_z
        kept[dv][...] += along(fz[pl.ds(0, end - begin)], matrices[1])
        take = (lambda v: v) if step == "0" else (lambda v: v[:size_y])
        for u in range(begin + 1, end - 1):
            here, conc = take(get(p, u)), get(c, u)
            divergence = take(get(gx, u + 1)) - take(get(gx, u - 1)) + take(get(dv, u))
            change = phase_change(here, take(conc), take(get("th", u)), divergence)
            beyond = take(get(c, u + 2)) + take(get(c, u - 2))
            new_conc = solute_step(take(conc), beyond, take(next_row(conc)), take(get(cz, u)), change)
            if step == "0":
                at("p1", u)[...] = here + change
                at("c1", u)[...] = new_conc
            else:
                phase_new[place(u) - HALO] = here + change
                solute_new[place(u) - HALO] = new_conc
    changes, lanes = [], []
    for k in range(1, size_x // 4 - 1):
        change = jnp.zeros((size_y, size_z), F32)
        for u in range(4 * k, 4 * k + 4):
            change = change + (phase_new[place(u) - HALO] - get("p0", u)[:size_y])
        changes.append(change)
        lanes.append(coarse_lane(k, size_x, size_y, coarse_y))
    latent[...] = restrict(changes, lanes, size_y, size_z, latent.shape[1])


def inner(phase, solute, side_a, strip_b, rest_b, coarse, matrices, along_z, coarse_y):
    size_x, size_y, size_z = phase.shape
    rows = size_y + 2 * HALO
    part = jax.ShapeDtypeStruct((size_x - 2 * HALO, size_y, size_z), F32)
    kept = [jax.ShapeDtypeStruct((end - begin, rows, size_z), F32) for begin, end in spans(size_x).values()]
    latent = jax.ShapeDtypeStruct((size_z // 4, coarse.shape[1]), F32)
    return pl.pallas_call(
        functools.partial(inner_kernel, coarse_y),
        out_shape=(part, part, latent, jax.ShapeDtypeStruct((2, rows, size_z), F32), *kept),
        in_specs=[vmem()] * 8,
        out_specs=[vmem()] * (4 + len(kept)),
        scratch_shapes=[pltpu.VMEM((size_x - 2, rows, size_z), F32)],
        compiler_params=pltpu.CompilerParams(vmem_limit_bytes=VMEM_LIMIT),
        cost_estimate=pl.CostEstimate(flops=5 * 10**8, bytes_accessed=5 * 10**6, transcendentals=0),
        name="inner",
    )(phase, solute, side_a, strip_b, rest_b, coarse, matrices, along_z)


def rim_halo(near, face, corner, phase_halo, solute_halo):
    _, _, size_y, size_z = face.shape
    odd_x = lax.rem(lax.axis_index("gx"), 2)
    flip = odd_x if near else 1 - odd_x
    top = row_ids((ROWS, size_z)) < HALO
    for d, (p_rows, c_rows) in enumerate(halo_rows(corner, top)):
        layer = d + flip * (HALO - 1 - 2 * d)
        for n, (field, rows) in enumerate(((phase_halo, p_rows), (solute_halo, c_rows))):
            field[HALO - 1 - d, pl.ds(0, size_y), :] = face[n, layer]
            field[HALO - 1 - d, pl.ds(size_y, ROWS), :] = rows


def edge_fan(corner, along_z, size_y):
    edge = jnp.where(row_ids(corner.shape[1:]) < 2, corner[0], pltpu.roll(corner[1], 4, 0))
    return interpolate(unpack_edge(edge), along_z[...], size_y)[0]


def rim_spot(near):
    odd_x = lax.rem(lax.axis_index("gx"), 2)
    flip = odd_x if near else 1 - odd_x
    return lambda v: v + (1 - flip) * (HALO - 1 - 2 * v)


def rim_march(near, size_x, halo, fans, matrices, kept, scratch, p1, c1, phase_new, result):
    hp0, hc0, fan = halo
    gx, dv, dz, cz, th = scratch
    _, size_y, size_z = phase_new.shape
    span = spans(size_x)
    spot = rim_spot(near)

    def get(name, v):
        begin, end = span[name]
        if v >= begin:
            found = kept[name][(size_x - 1 - v if near else v) - begin]
            return -found if near and name.startswith("gx") else found
        own, first = dict(
            p0=(hp0, -4), c0=(hc0, -4), dz0=(dz, -3), cz0=(cz, -2), gx0=(gx, -3), dv0=(dv, -2),
            p1=(p1, -2), c1=(c1, -2), dz1=(dz, -1), gx1=(gx, -1), dv1=(dv, 0), th=(th, -2),
        )[name]
        return own[v - first]

    moved = []
    ends = {-1: fan, 0: fans[1 if near else 0]}
    for v in range(-2, 2):
        th[v + 2] = blend(v, ends)
    for step, begin in (("0", -3), ("1", -1)):
        p, c, gx_, dv_, dz_, cz_ = (name + step for name in ("p", "c", "gx", "dv", "dz", "cz"))
        for n in range(3):
            dz[n] = z_difference((hp0 if step == "0" else p1)[n + 1], True)
        if step == "0":
            cz[...] = along(hc0[pl.ds(2, 2)], matrices[2])
        yield
        for v in range(begin, begin + 4):
            flux_x, flux_y, flux_z = flux(get(p, v - 1), get(p, v), get(p, v + 1), get(dz_, v))
            gx[v - begin] = flux_x
            if v > begin:
                dv[v - begin - 1] = spread(flux_y) + z_difference(flux_z, False)
        yield
        take = (lambda w: w) if step == "0" else (lambda w: w[:size_y])
        for v in range(begin + 1, begin + 5):
            here, conc = take(get(p, v)), get(c, v)
            divergence = take(get(gx_, v + 1)) - take(get(gx_, v - 1)) + take(get(dv_, v))
            change = phase_change(here, take(conc), take(get("th", v)), divergence)
            if step == "0":
                beyond = get(c, v + 2) + get(c, v - 2)
                p1[v + 2] = here + change
                c1[v + 2] = solute_step(conc, beyond, next_row(conc), get(cz_, v), change)
            else:
                phase_new[spot(v)] = here + change
                moved.append(here + change - get("p0", v)[:size_y])
        yield
    result.append((moved[0] + moved[1]) + (moved[2] + moved[3]))


def near_kernel(face, corner, phase_halo, solute_halo):
    rim_halo(True, face, corner, phase_halo, solute_halo)


def near_halo(face, corner):
    _, _, size_y, size_z = face.shape
    slabs = jax.ShapeDtypeStruct((HALO, size_y + 2 * HALO, size_z), F32)
    return pl.pallas_call(
        near_kernel,
        out_shape=(slabs, slabs),
        in_specs=[vmem()] * 2,
        out_specs=[vmem()] * 2,
        compiler_params=pltpu.CompilerParams(vmem_limit_bytes=VMEM_LIMIT),
        cost_estimate=pl.CostEstimate(flops=15 * 10**8, bytes_accessed=15 * 10**6, transcendentals=0),
        name="near",
    )(face, corner)


def rim_kernel(
    coarse_y, size_x, face, corner, near_phase, near_solute, near_corner, fans, matrices, along_z, inner_latent, *rest
):
    kept = dict(zip(KEPT, rest[: len(KEPT)]))
    outs, (far_phase, far_solute, total, *scratch) = rest[len(KEPT) : len(KEPT) + 8], rest[len(KEPT) + 8 :]
    near_new, far_new, keep, send = outs[:3], outs[3:6], outs[6], outs[7]
    _, _, size_y, size_z = face.shape
    width = total.shape[1]
    rim_halo(False, face, corner, far_phase, far_solute)
    changes = []
    half = len(scratch) // 2
    near = near_phase, near_solute, edge_fan(near_corner, along_z, size_y)
    far = far_phase, far_solute, edge_fan(corner, along_z, size_y)
    sides = [
        rim_march(True, size_x, near, fans, matrices, kept, scratch[:half], *near_new, changes),
        rim_march(False, size_x, far, fans, matrices, kept, scratch[half:], *far_new, changes),
    ]
    while sides:
        sides = [side for side in sides if next(side, sides) is not sides]
    lanes = [coarse_lane(u, size_x, size_y, coarse_y) for u in (size_x // 4 - 1, 0)]
    total[...] = restrict(changes, lanes, size_y, size_z, width) + inner_latent[...]
    halve(total, lax.div(2 * lax.axis_index("gy"), lax.axis_size("gy")), keep, send)


def halve(total, side, keep, send):
    half = keep.shape[0]
    keep[...] = total[pl.ds(pl.multiple_of(side * half, half), half), :]
    send[...] = total[pl.ds(pl.multiple_of((1 - side) * half, half), half), :]


def rims(shape, face, corner, near, fans, matrices, along_z, inner_latent, kept, coarse_y):
    size_x, size_y, size_z = shape
    rows = size_y + 2 * HALO
    part = jax.ShapeDtypeStruct((HALO, size_y, size_z), F32)
    width = inner_latent.shape[1]
    half = jax.ShapeDtypeStruct((size_z // 8, width), F32)
    state = jax.ShapeDtypeStruct((HALO, rows, size_z), F32)
    slabs = lambda count: pltpu.VMEM((count, rows, size_z), F32)
    return pl.pallas_call(
        functools.partial(rim_kernel, coarse_y, size_x),
        out_shape=(state, state, part, state, state, part, half, half),
        in_specs=[vmem()] * (9 + len(kept)),
        out_specs=[vmem()] * 8,
        scratch_shapes=[
            slabs(HALO), slabs(HALO), pltpu.VMEM((size_z // 4, width), F32),
            *[slabs(count) for count in 2 * (4, 3, 3, 2, 4)],
        ],
        compiler_params=pltpu.CompilerParams(vmem_limit_bytes=VMEM_LIMIT),
        cost_estimate=pl.CostEstimate(flops=10**7, bytes_accessed=3 * 10**6, transcendentals=0),
        name="rims",
    )(face, corner, *near, fans, matrices, along_z, inner_latent, *kept)


def rim_solute(near, size_x, p1, c1, phase_new, matrices, kept, out):
    _, size_y, size_z = phase_new.shape
    span = spans(size_x)
    spot = rim_spot(near)
    own = {"p1": p1[...], "c1": c1[...], "cz1": along(c1[pl.ds(2, 2)], matrices[2])}

    def get(name, v):
        begin, _ = span[name]
        if v >= begin:
            return kept[name][(size_x - 1 - v if near else v) - begin]
        return own[name][v if name == "cz1" else v + 2]

    for v in range(HALO):
        conc = get("c1", v)
        change = phase_new[spot(v)] - get("p1", v)[:size_y]
        beyond = get("c1", v + 2)[:size_y] + get("c1", v - 2)[:size_y]
        out[spot(v)] = solute_step(
            conc[:size_y], beyond, next_row(conc)[:size_y], get("cz1", v)[:size_y], change
        )


def store_kernel(
    middle_phase, middle_solute, near_p1, near_c1, near_phase, far_p1, far_c1, far_phase, matrices, p1, c1, cz1,
    phase_out, solute_out, near_solute, far_solute, sems,
):
    size_x = phase_out.shape[0]
    odd_x = lax.rem(lax.axis_index("gx"), 2)
    near = (1 - odd_x) * (size_x - HALO)
    far = size_x - HALO - near
    put = lambda part, out, at: (part, out.at[pl.ds(at, part.shape[0])])
    copies = start_all(
        [
            put(middle_phase, phase_out, HALO), put(middle_solute, solute_out, HALO), put(near_phase, phase_out, near),
            put(far_phase, phase_out, far),
        ],
        sems,
    )
    kept = dict(p1=p1, c1=c1, cz1=cz1)
    rim_solute(True, size_x, near_p1, near_c1, near_phase, matrices, kept, near_solute)
    rim_solute(False, size_x, far_p1, far_c1, far_phase, matrices, kept, far_solute)
    copies += start_all(
        [put(near_solute, solute_out, near), put(far_solute, solute_out, far)], sems.at[pl.ds(4, 2)]
    )
    wait_all(copies)


def store(shape, middle, edges, matrices, kept):
    kept = dict(zip(KEPT, kept))
    out = jax.ShapeDtypeStruct(shape, F32)
    part = pltpu.VMEM((HALO, *shape[1:]), F32)
    return pl.pallas_call(
        store_kernel,
        out_shape=(out, out),
        in_specs=[vmem()] * 12,
        out_specs=[hbm()] * 2,
        scratch_shapes=[part, part, pltpu.SemaphoreType.DMA((6,))],
        compiler_params=pltpu.CompilerParams(vmem_limit_bytes=VMEM_LIMIT),
        cost_estimate=pl.CostEstimate(flops=0, bytes_accessed=4 * 10**6, transcendentals=0),
        name="store",
    )(*middle, *edges, matrices, kept["p1"], kept["c1"], kept["cz1"])


def merge_kernel(mine, arrived, keep, send, total):
    total[...] = mine[...] + arrived[...]
    halve(total, lax.rem(lax.axis_index("gy"), 2), keep, send)


def merge(mine, arrived):
    half = jax.ShapeDtypeStruct((mine.shape[0] // 2, mine.shape[1]), F32)
    return pl.pallas_call(
        merge_kernel,
        out_shape=(half, half),
        in_specs=[vmem()] * 2,
        out_specs=[vmem()] * 2,
        scratch_shapes=[pltpu.VMEM(mine.shape, F32)],
        compiler_params=pltpu.CompilerParams(vmem_limit_bytes=VMEM_LIMIT),
        cost_estimate=pl.CostEstimate(flops=10**4, bytes_accessed=10**5, transcendentals=0),
        name="merge",
    )(mine, arrived)


def owner_kernel(mine, arrived, out):
    total = mine[...] + arrived[...]
    coarse_x, _, coarse_y = out.shape
    for k in range(coarse_x):
        out[k] = total[:, k * coarse_y : (k + 1) * coarse_y]


def owner(mine, arrived, coarse_x, coarse_y):
    coarse_z = mine.shape[0]
    return pl.pallas_call(
        owner_kernel,
        out_shape=jax.ShapeDtypeStruct((coarse_x, coarse_z, coarse_y), F32),
        in_specs=[vmem()] * 2,
        out_specs=vmem(),
        compiler_params=pltpu.CompilerParams(vmem_limit_bytes=VMEM_LIMIT),
        cost_estimate=pl.CostEstimate(flops=10**4, bytes_accessed=10**5, transcendentals=0),
        name="owner",
    )(mine, arrived)


def body(phase, solute, macro_temp):
    count_x, count_y = lax.axis_size("gx"), lax.axis_size("gy")
    coarse_x, coarse_y, coarse_z = macro_temp.shape
    near_x, far_x = pairs(count_x, 0), pairs(count_x, 1)
    near_y, far_y = pairs(count_y, 0), pairs(count_y, 1)
    across = [(k, count_y - 1 - k) for k in range(count_y)]
    ride = count_y == 4
    macro = jnp.swapaxes(macro_temp, 1, 2)
    still = [pltpu.with_memory_space_constraint(v, pltpu.HBM) for v in (phase, solute, macro)]
    phase, solute, face_a, face_b, side_a, strip_b, rest_b, table = pack(*still, ride)
    coarse_shape = (coarse_z * count_y, coarse_x * coarse_y)
    face_a = lax.ppermute(face_a, "gx", near_x)
    side_a = lax.ppermute(side_a, "gy", near_y)
    if ride:
        strip_b = append(side_a, strip_b)
    else:
        table = lax.all_gather(table, "gy").reshape(coarse_shape)
    matrices, along_z = z_products(phase.shape[2], strip_b)
    face_b, rest_b, strip_b = lax.optimization_barrier((face_b, rest_b, strip_b))
    strip_b = lax.ppermute(strip_b, "gy", far_y)
    rest_b = lax.ppermute(rest_b, "gy", far_y)
    face_b = lax.ppermute(face_b, "gx", far_x)
    coarse, corner_a, corner_b = corners(side_a, strip_b, table, coarse_y, coarse_shape)
    corner_a = lax.ppermute(corner_a, "gx", near_x)
    corner_b = lax.ppermute(corner_b, "gx", far_x)
    results = inner(phase, solute, side_a, strip_b, rest_b, coarse, matrices, along_z, coarse_y)
    middle, inner_latent, fans, kept = results[:2], results[2], results[3], results[4:]
    near = (*near_halo(face_a, corner_a), corner_a)
    *edges, mine, send = rims(
        phase.shape, face_b, corner_b, near, fans, matrices, along_z, inner_latent, kept, coarse_y
    )
    phase_out, solute_out = store(phase.shape, middle, edges, matrices, kept)
    if ride:
        mine, send = merge(mine, lax.ppermute(send, "gy", across))
        latent = owner(mine, lax.ppermute(send, "gy", near_y), coarse_x, coarse_y)
    else:
        low = lax.axis_index("gy") < count_y // 2
        total = jnp.concatenate([jnp.where(low, mine, send), jnp.where(low, send, mine)])
        latent = lax.psum_scatter(total, "gy", scatter_dimension=0, tiled=True)
        latent = jnp.swapaxes(latent.reshape(coarse_z, coarse_x, coarse_y), 0, 1)
    latent = jnp.swapaxes(latent, 1, 2)
    return phase_out, solute_out, latent


def solution(mesh):
    in_specs = (P("gx", "gy", None), P("gx", "gy", None), P("gx", None, "gy"))
    out_specs = (P("gx", "gy", None), P("gx", "gy", None), P("gx", None, "gy"))
    return jax.shard_map(body, mesh=mesh, in_specs=in_specs, out_specs=out_specs, check_vma=False)
```

```python
import functools

import jax
import jax.numpy as jnp
from jax import lax
from jax.experimental import pallas as pl
from jax.experimental.pallas import tpu as pltpu
from jax.sharding import PartitionSpec as P

time_step = 0.1
anisotropy = 0.3
coupling = 2.0
rejection = 0.5

F32 = jnp.float32
HALO = 4
STRIP = 4
ROWS = 8
LANES = 128
VMEM_LIMIT = 24 * 1024 * 1024


def vmem():
    return pl.BlockSpec(memory_space=pltpu.VMEM)


def anywhere():
    return pl.BlockSpec(memory_space=pl.ANY)


def hbm():
    return pl.BlockSpec(memory_space=pltpu.HBM)


def pairs(count, first):
    forward = [((first + k) % count, (first + k + 1) % count) for k in range(0, count, 2)]
    return forward + [(b, a) for a, b in forward]


def flips(me):
    odd = lax.rem(me, 2)
    return me, me + 1 - 2 * odd, lax.rem(me + 2, 4), 3 - me


def halves(value):
    coarse = value.astype(jnp.bfloat16)
    return coarse, (value - coarse.astype(F32)).astype(jnp.bfloat16)


def product(left, right, contract):
    dot = lambda a, b: lax.dot_general(a, b, ((contract[:1], contract[1:]), ((), ())), preferred_element_type=F32)
    if left.dtype == jnp.bfloat16:
        parts = [dot(left, part) for part in halves(right)]
    else:
        parts = [dot(part, right) for part in halves(left)]
    return parts[0] + parts[1]


def row_ids(shape):
    return lax.broadcasted_iota(jnp.int32, shape, len(shape) - 2)


def lane_ids(shape):
    return lax.broadcasted_iota(jnp.int32, shape, len(shape) - 1)


def start_all(copies, sems):
    copies = [pltpu.make_async_copy(source, target, sems.at[n]) for n, (source, target) in enumerate(copies)]
    for copy in copies:
        copy.start()
    return copies


def wait_all(copies):
    for copy in copies:
        copy.wait()


def fold(table):
    half = table.shape[0] // 2
    return jnp.concatenate([table[:half], table[half:]], axis=1)


def unfold(tile):
    return jnp.concatenate([tile[:, :LANES], tile[:, LANES:]], axis=0)


def pack_kernel(
    phase, solute, macro, phase_here, solute_here, face_a, face_b, side_a, strip_b, rest_b, table, local, sems
):
    size_x, size_y, size_z = phase.shape
    odd_x = lax.rem(lax.axis_index("gx"), 2)
    even_y = lax.rem(lax.axis_index("gy"), 2) == 0
    copies = [(macro, local)]
    for ref, here in ((phase, phase_here), (solute, solute_here)):
        for at in range(0, size_x, HALO):
            copies.append((ref.at[pl.ds(at, HALO)], here.at[pl.ds(at, HALO)]))
    copies = start_all(copies, sems)
    half = 1 + size_x // HALO
    for field, (here, batch) in enumerate(((phase_here, copies[:half]), (solute_here, copies[half:]))):
        wait_all(batch)
        face_a[field] = here[pl.ds((1 - odd_x) * (size_x - HALO), HALO)]
        face_b[field] = here[pl.ds(odd_x * (size_x - HALO), HALO)]
        if field == 0:
            wide = jnp.concatenate([local[k] for k in range(local.shape[0])], axis=1)
            table[...] = wide
    low = [here[:, pl.ds(0, ROWS), :] for here in (phase_here, solute_here)]
    high = [here[:, pl.ds(size_y - ROWS, ROWS), :] for here in (phase_here, solute_here)]
    top = row_ids((size_x, ROWS, size_z)) < HALO
    low_side = jnp.where(top, low[0], pltpu.roll(low[1], HALO, 1))
    high_side = jnp.where(top, pltpu.roll(high[1], HALO, 1), high[0])
    side_a[pl.ds(0, size_x)] = jnp.where(even_y, high_side, low_side)
    side_b = jnp.where(even_y, low_side, high_side)
    strip_b[pl.ds(0, STRIP)] = side_b[:STRIP]
    strip_b[pl.ds(STRIP, STRIP)] = side_b[size_x - STRIP :]
    rest_b[...] = side_b[STRIP : size_x - STRIP]
    if side_a.shape[0] > size_x:
        side_a[size_x] = fold(wide)
        strip_b[2 * STRIP] = fold(wide)


def pack(phase, solute, macro, ride):
    size_x, size_y, size_z = phase.shape
    coarse_x, coarse_z, coarse_y = macro.shape
    field = jax.ShapeDtypeStruct(phase.shape, F32)
    face = jax.ShapeDtypeStruct((2, HALO, size_y, size_z), F32)
    counts = (size_x, 2 * STRIP, size_x - 2 * STRIP)
    extra = (1, 2, 0) if ride else (0, 0, 0)
    sides = [jax.ShapeDtypeStruct((count + more, ROWS, size_z), F32) for count, more in zip(counts, extra)]
    table = jax.ShapeDtypeStruct((coarse_z, coarse_x * coarse_y), F32)
    return pl.pallas_call(
        pack_kernel,
        out_shape=(field, field, face, face, *sides, table),
        in_specs=[hbm()] * 3,
        out_specs=[vmem()] * 8,
        scratch_shapes=[pltpu.VMEM(macro.shape, F32), pltpu.SemaphoreType.DMA((1 + 2 * (size_x // HALO),))],
        compiler_params=pltpu.CompilerParams(vmem_limit_bytes=VMEM_LIMIT),
        cost_estimate=pl.CostEstimate(flops=10**5, bytes_accessed=2 * 10**6, transcendentals=0),
        name="pack",
    )(phase, solute, macro)


def append_kernel(arrived, side, out):
    out[side.shape[0] - 1] = arrived[arrived.shape[0] - 1]


def append(arrived, side):
    return pl.pallas_call(
        append_kernel,
        out_shape=jax.ShapeDtypeStruct(side.shape, F32),
        in_specs=[vmem(), vmem()],
        out_specs=vmem(),
        input_output_aliases={1: 0},
        compiler_params=pltpu.CompilerParams(vmem_limit_bytes=VMEM_LIMIT),
        cost_estimate=pl.CostEstimate(flops=0, bytes_accessed=10**5, transcendentals=0),
        name="append",
    )(arrived, side)


def near_rows(block, coarse_y):
    shape = (2 * ROWS, coarse_y)
    wanted = lax.rem(row_ids(shape) + lax.axis_index("gy") * ROWS + coarse_y - 1, coarse_y)
    pick = (lane_ids(shape) == wanted).astype(F32).astype(jnp.bfloat16)
    return product(pick, block, (1, 1))


def pack_edge(rows):
    pieces = rows[:ROWS], pltpu.roll(rows[:ROWS], 4, 0), rows[ROWS:], pltpu.roll(rows[ROWS:], 4, 0)
    return jnp.concatenate(pieces, axis=1)


def unpack_edge(tile):
    quarter = tile.shape[1] // 4
    pieces = [tile[:, at : at + quarter] for at in range(0, tile.shape[1], quarter)]
    top = row_ids(pieces[0].shape) < 4
    halves = [jnp.where(top, pieces[n], pltpu.roll(pieces[n + 1], 4, 0)) for n in (0, 2)]
    return jnp.concatenate(halves, axis=0)


def corner_kernel(coarse_y, gathered, side_a, strip_b, table, coarse, corner_a, corner_b):
    size_x = side_a.shape[0] - (0 if gathered else 1)
    me = lax.axis_index("gy")
    even_x = lax.rem(lax.axis_index("gx"), 2) == 0
    even_y = lax.rem(me, 2) == 0
    block = table[...]
    if not gathered:
        near, across, far = flips(me)[1:]
        depth = table.shape[0]
        tiles = (me, block), (near, unfold(side_a[size_x])), (far, unfold(strip_b[2 * STRIP])), (across, unfold(strip_b[2 * STRIP + 1]))
        for source, tile in tiles:
            coarse[pl.ds(pl.multiple_of(source * depth, depth), depth), :] = tile
        block = coarse[...]
    depth, width = block.shape
    flipped = [block[:, at : at + coarse_y] for at in range(width - coarse_y, -1, -coarse_y)]
    block = jnp.where(even_x, block, jnp.concatenate(flipped, axis=1))
    coarse[...] = block
    row = row_ids(side_a.shape[1:])
    edges = block[:, width - coarse_y :], block[:, :coarse_y]
    for corner, top_side, edge in ((corner_a, even_x, edges[0]), (corner_b, jnp.logical_not(even_x), edges[1])):

        def layer(d, high):
            first = side_a[jnp.where(top_side, size_x - d, d - 1)]
            second = strip_b[jnp.where(top_side, 2 * STRIP - d, d - 1)]
            return jnp.where(even_y, first, second) if high else jnp.where(even_y, second, first)

        spare = pack_edge(near_rows(edge, coarse_y))
        tile = jnp.where(row == 4, pltpu.roll(layer(3, False), 5, 0), layer(1, False))
        corner[0] = jnp.where(row < 2, spare, tile)
        tile = jnp.where(row == 3, pltpu.roll(layer(3, True), 3, 0), layer(1, True))
        corner[1] = jnp.where(row >= 6, pltpu.roll(spare, 4, 0), tile)
        corner[2] = jnp.where(row % 4 < 2, layer(2, True), layer(2, False))


def corners(side_a, strip_b, table, coarse_y, coarse_shape):
    size_z = side_a.shape[2]
    corner = jax.ShapeDtypeStruct((3, ROWS, size_z), F32)
    coarse = jax.ShapeDtypeStruct(coarse_shape, F32)
    return pl.pallas_call(
        functools.partial(corner_kernel, coarse_y, table.shape == coarse_shape),
        out_shape=(coarse, corner, corner),
        in_specs=[vmem()] * 3,
        out_specs=[vmem()] * 3,
        compiler_params=pltpu.CompilerParams(vmem_limit_bytes=VMEM_LIMIT),
        cost_estimate=pl.CostEstimate(flops=10**5, bytes_accessed=4 * 10**5, transcendentals=0),
        name="corners",
    )(side_a, strip_b, table)


def weights(ends, frac, tick):
    first, second = ends
    return jnp.where(tick == first, 1.0 - frac, 0.0) + jnp.where(tick == second, frac, 0.0)


def weights_z(depth, size_z):
    shape = (depth, size_z)
    fine = lane_ids(shape)
    lower = (2 * fine + 5) // 8 - 1
    frac = (2 * fine - 3 - 8 * lower).astype(F32) / 8.0
    ends = jnp.clip(lower, 0, depth - 1), jnp.clip(lower + 1, 0, depth - 1)
    return weights(ends, frac, row_ids(shape))


def interpolate(rows, along_z, size_y):
    deep = product(rows, along_z, (1, 0))
    shape = (size_y + 2 * HALO, 2 * ROWS)
    fine = row_ids(shape)
    fine = jnp.where(fine >= size_y + HALO, fine - shape[0], fine)
    lower = (2 * fine + 13) // 8 - 2
    frac = (2 * fine - 3 - 8 * lower).astype(F32) / 8.0
    along_y = weights((lower + 1, lower + 2), frac, lane_ids(shape)).astype(jnp.bfloat16)
    return [
        product(along_y, deep[at : at + 2 * ROWS], (1, 0))
        for at in range(0, rows.shape[0], 2 * ROWS)
    ]


def blend(x, fans):
    lower = (2 * x - 3) // 8
    frac = (2 * x - 3 - 8 * lower) / 8.0
    return (1.0 - frac) * fans[lower] + frac * fans[lower + 1]


def turn(value, by, axis):
    return pltpu.roll(value, by % value.shape[axis], axis)


def z_matrices(size_z):
    shape = (size_z, size_z)
    source, target = row_ids(shape), lane_ids(shape)
    hit = lambda at: (source == at).astype(F32)
    end = size_z - 1
    gradient = hit(jnp.minimum(target + 1, end)) - hit(jnp.maximum(target - 1, 0))
    difference = hit(target + 1) - hit(target - 1)
    laplace = hit(jnp.minimum(target + 2, end)) + hit(jnp.maximum(target - 2, 0)) - 6.0 * hit(target)
    return tuple(m.astype(jnp.bfloat16) for m in (gradient, difference, laplace))


def matrix_kernel(size_z, tile, out, along_z):
    for n, matrix in enumerate(z_matrices(size_z)):
        out[n] = matrix
    along_z[...] = weights_z(*along_z.shape).astype(jnp.bfloat16)


def z_products(size_z, tile):
    square = jax.ShapeDtypeStruct((3, size_z, size_z), jnp.bfloat16)
    return pl.pallas_call(
        functools.partial(matrix_kernel, size_z),
        out_shape=(square, jax.ShapeDtypeStruct((size_z // 4, size_z), jnp.bfloat16)),
        in_specs=[anywhere()],
        out_specs=[vmem()] * 2,
        compiler_params=pltpu.CompilerParams(vmem_limit_bytes=VMEM_LIMIT),
        cost_estimate=pl.CostEstimate(flops=10**6, bytes_accessed=4 * 10**5, transcendentals=0),
        name="products",
    )(tile)


def along(slabs, matrix):
    return product(slabs.reshape(-1, slabs.shape[-1]), matrix, (1, 0)).reshape(slabs.shape)


def z_difference(value, clamp):
    first, second = value[:, :LANES], value[:, LANES:]
    lane = lane_ids(first.shape)
    head, tail = lane == 0, lane == LANES - 1
    ends = (first, second) if clamp else (0.0, 0.0)
    ahead = turn(first, -1, 1), turn(second, -1, 1)
    behind = turn(first, 1, 1), turn(second, 1, 1)
    low = jnp.where(tail, ahead[1], ahead[0]) - jnp.where(head, ends[0], behind[0])
    high = jnp.where(tail, ends[1], ahead[1]) - jnp.where(head, behind[0], behind[1])
    return jnp.concatenate([low, high], axis=1)


def flux(before, here, after, along_z):
    along_x = after - before
    along_y = turn(here, -1, 0) - turn(here, 1, 0)
    sq_x = along_x * along_x
    sq_y = along_y * along_y
    both = sq_x + sq_y
    inverse = 1.0 / (both + 4.0)
    factor = 1.0 + anisotropy * (both * both - 8.0 * (sq_x * sq_y)) * (inverse * inverse)
    stiff = (0.25 * time_step) * (factor * factor)
    return stiff * along_x, stiff * along_y, stiff * along_z


def spread(flux_y):
    return turn(flux_y, -1, 0) - turn(flux_y, 1, 0)


def phase_change(here, conc, theta, divergence):
    square = 1.0 - here * here
    drive = square * (here - (coupling * square) * (theta + conc))
    return divergence + time_step * drive


def solute_step(conc, beyond_x, beyond_y, along_z, change):
    return conc + (0.25 * time_step) * (beyond_x + beyond_y + along_z) + rejection * change


def next_row(conc):
    return turn(conc, -2, 0) + turn(conc, 2, 0)


def restrict(changes, lanes, size_y, size_z, coarse_width):
    shape = (size_z, size_z // 4)
    pool_z = (row_ids(shape) // 4 == lane_ids(shape)).astype(F32).astype(jnp.bfloat16)
    shape = (size_y, coarse_width)
    cell, lane = row_ids(shape) // 4, lane_ids(shape)
    pool_y = [jnp.where(cell + at == lane, 0.5 / 64.0, 0.0).astype(jnp.bfloat16) for at in lanes]
    pooled = product(jnp.concatenate(changes, axis=0), pool_z, (1, 0))
    return product(pooled, jnp.concatenate(pool_y, axis=0), (0, 0))


def coarse_lane(u, size_x, size_y, coarse_y):
    last = size_x // 4 - 1
    x = u + lax.rem(lax.axis_index("gx"), 2) * (last - 2 * u)
    return x * coarse_y + lax.axis_index("gy") * (size_y // 4)


KEPT = ("p0", "c0", "dz0", "cz0", "gx0", "dv0", "p1", "c1", "dz1", "cz1", "gx1", "dv1", "th")


def spans(size_x):
    widths = dict(p0=0, c0=0, dz0=0, cz0=0, gx0=1, dv0=1, p1=2, c1=2, dz1=2, cz1=2, gx1=3, dv1=3, th=2)
    return {name: (widths[name], size_x - widths[name]) for name in KEPT}


def halo_rows(tile, top):
    zero = jnp.zeros_like(tile[0])
    low = tile[0], tile[2], pltpu.roll(tile[0], 3, 0), zero
    high = tile[1], tile[2], pltpu.roll(tile[1], 5, 0), zero
    return [
        (jnp.where(top, h, l), pltpu.roll(jnp.where(top, l, h), HALO, 0)) for l, h in zip(low, high)
    ]


def inner_kernel(
    coarse_y, phase, solute, side_a, strip_b, rest_b, coarse, matrices, along_z, phase_new, solute_new, latent, ends, *rest
):
    kept = dict(zip(KEPT, rest[: len(KEPT)]))
    (fz,) = rest[len(KEPT) :]
    size_x, size_y, size_z = phase.shape
    span = spans(size_x)
    odd_x = lax.rem(lax.axis_index("gx"), 2)
    even_y = lax.rem(lax.axis_index("gy"), 2) == 0
    at = lambda name, u: kept[name].at[u - span[name][0]]
    get = lambda name, u: kept[name][u - span[name][0]]
    place = lambda u: u + odd_x * (size_x - 1 - 2 * u)
    top = row_ids((ROWS, size_z)) < HALO
    for u in range(size_x):
        first = side_a[place(u)]
        if STRIP <= u < size_x - STRIP:
            second = rest_b[place(u) - STRIP]
        else:
            at_strip = u if u < STRIP else u - size_x + 2 * STRIP
            second = strip_b[at_strip + odd_x * (2 * STRIP - 1 - 2 * at_strip)]
        low, high = jnp.where(even_y, second, first), jnp.where(even_y, first, second)
        at("p0", u)[pl.ds(0, size_y), :] = phase[place(u)]
        at("c0", u)[pl.ds(0, size_y), :] = solute[place(u)]
        at("p0", u)[pl.ds(size_y, ROWS), :] = jnp.where(top, high, low)
        at("c0", u)[pl.ds(size_y, ROWS), :] = pltpu.roll(jnp.where(top, low, high), HALO, 0)
    block = coarse[...]
    block = [near_rows(block[:, at : at + coarse_y], coarse_y) for at in range(0, block.shape[1], coarse_y)]
    fans = dict(enumerate(interpolate(jnp.concatenate(block, axis=0), along_z[...], size_y)))
    ends[0], ends[1] = fans[0], fans[len(fans) - 1]
    for u in range(*span["th"]):
        at("th", u)[...] = blend(u, fans)

    for step in "01":
        p, c, dz, cz, gx, dv = (name + step for name in ("p", "c", "dz", "cz", "gx", "dv"))
        for u in range(*span[dz]):
            at(dz, u)[...] = z_difference(get(p, u), True)
        kept[cz][...] = along(kept[c][...], matrices[2])
        begin, end = span[gx]
        for u in range(begin, end):
            flux_x, flux_y, flux_z = flux(get(p, u - 1), get(p, u), get(p, u + 1), get(dz, u))
            at(gx, u)[...] = flux_x
            at(dv, u)[...] = spread(flux_y) + z_difference(flux_z, False)
        take = (lambda v: v) if step == "0" else (lambda v: v[:size_y])
        for u in range(begin + 1, end - 1):
            here, conc = take(get(p, u)), get(c, u)
            divergence = take(get(gx, u + 1)) - take(get(gx, u - 1)) + take(get(dv, u))
            change = phase_change(here, take(conc), take(get("th", u)), divergence)
            beyond = take(get(c, u + 2)) + take(get(c, u - 2))
            new_conc = solute_step(take(conc), beyond, take(next_row(conc)), take(get(cz, u)), change)
            if step == "0":
                at("p1", u)[...] = here + change
                at("c1", u)[...] = new_conc
            else:
                phase_new[place(u) - HALO] = here + change
                solute_new[place(u) - HALO] = new_conc
    changes, lanes = [], []
    for k in range(1, size_x // 4 - 1):
        change = jnp.zeros((size_y, size_z), F32)
        for u in range(4 * k, 4 * k + 4):
            change = change + (phase_new[place(u) - HALO] - get("p0", u)[:size_y])
        changes.append(change)
        lanes.append(coarse_lane(k, size_x, size_y, coarse_y))
    latent[...] = restrict(changes, lanes, size_y, size_z, latent.shape[1])


def inner(phase, solute, side_a, strip_b, rest_b, coarse, matrices, along_z, coarse_y):
    size_x, size_y, size_z = phase.shape
    rows = size_y + 2 * HALO
    part = jax.ShapeDtypeStruct((size_x - 2 * HALO, size_y, size_z), F32)
    kept = [jax.ShapeDtypeStruct((end - begin, rows, size_z), F32) for begin, end in spans(size_x).values()]
    latent = jax.ShapeDtypeStruct((size_z // 4, coarse.shape[1]), F32)
    return pl.pallas_call(
        functools.partial(inner_kernel, coarse_y),
        out_shape=(part, part, latent, jax.ShapeDtypeStruct((2, rows, size_z), F32), *kept),
        in_specs=[vmem()] * 8,
        out_specs=[vmem()] * (4 + len(kept)),
        scratch_shapes=[pltpu.VMEM((size_x - 2, rows, size_z), F32)],
        compiler_params=pltpu.CompilerParams(vmem_limit_bytes=VMEM_LIMIT),
        cost_estimate=pl.CostEstimate(flops=5 * 10**8, bytes_accessed=5 * 10**6, transcendentals=0),
        name="inner",
    )(phase, solute, side_a, strip_b, rest_b, coarse, matrices, along_z)


def rim_halo(near, face, corner, phase_halo, solute_halo):
    _, _, size_y, size_z = face.shape
    odd_x = lax.rem(lax.axis_index("gx"), 2)
    flip = odd_x if near else 1 - odd_x
    top = row_ids((ROWS, size_z)) < HALO
    for d, (p_rows, c_rows) in enumerate(halo_rows(corner, top)):
        layer = d + flip * (HALO - 1 - 2 * d)
        for n, (field, rows) in enumerate(((phase_halo, p_rows), (solute_halo, c_rows))):
            field[HALO - 1 - d, pl.ds(0, size_y), :] = face[n, layer]
            field[HALO - 1 - d, pl.ds(size_y, ROWS), :] = rows


def edge_fan(corner, along_z, size_y):
    edge = jnp.where(row_ids(corner.shape[1:]) < 2, corner[0], pltpu.roll(corner[1], 4, 0))
    return interpolate(unpack_edge(edge), along_z[...], size_y)[0]


def rim_spot(near):
    odd_x = lax.rem(lax.axis_index("gx"), 2)
    flip = odd_x if near else 1 - odd_x
    return lambda v: v + (1 - flip) * (HALO - 1 - 2 * v)


def rim_march(near, size_x, halo, fans, matrices, kept, scratch, p1, c1, phase_new, result):
    hp0, hc0, fan = halo
    gx, dv, dz, cz, th = scratch
    _, size_y, size_z = phase_new.shape
    span = spans(size_x)
    spot = rim_spot(near)

    def get(name, v):
        begin, end = span[name]
        if v >= begin:
            found = kept[name][(size_x - 1 - v if near else v) - begin]
            return -found if near and name.startswith("gx") else found
        own, first = dict(
            p0=(hp0, -4), c0=(hc0, -4), dz0=(dz, -3), cz0=(cz, -2), gx0=(gx, -3), dv0=(dv, -2),
            p1=(p1, -2), c1=(c1, -2), dz1=(dz, -1), gx1=(gx, -1), dv1=(dv, 0), th=(th, -2),
        )[name]
        return own[v - first]

    moved = []
    ends = {-1: fan, 0: fans[1 if near else 0]}
    for v in range(-2, 2):
        th[v + 2] = blend(v, ends)
    for step, begin in (("0", -3), ("1", -1)):
        p, c, gx_, dv_, dz_, cz_ = (name + step for name in ("p", "c", "gx", "dv", "dz", "cz"))
        for n in range(3):
            dz[n] = z_difference((hp0 if step == "0" else p1)[n + 1], True)
        if step == "0":
            cz[...] = along(hc0[pl.ds(2, 2)], matrices[2])
        yield
        for v in range(begin, begin + 4):
            flux_x, flux_y, flux_z = flux(get(p, v - 1), get(p, v), get(p, v + 1), get(dz_, v))
            gx[v - begin] = flux_x
            if v > begin:
                dv[v - begin - 1] = spread(flux_y) + z_difference(flux_z, False)
        yield
        take = (lambda w: w) if step == "0" else (lambda w: w[:size_y])
        for v in range(begin + 1, begin + 5):
            here, conc = take(get(p, v)), get(c, v)
            divergence = take(get(gx_, v + 1)) - take(get(gx_, v - 1)) + take(get(dv_, v))
            change = phase_change(here, take(conc), take(get("th", v)), divergence)
            if step == "0":
                beyond = get(c, v + 2) + get(c, v - 2)
                p1[v + 2] = here + change
                c1[v + 2] = solute_step(conc, beyond, next_row(conc), get(cz_, v), change)
            else:
                phase_new[spot(v)] = here + change
                moved.append(here + change - get("p0", v)[:size_y])
        yield
    result.append((moved[0] + moved[1]) + (moved[2] + moved[3]))


def near_kernel(face, corner, phase_halo, solute_halo):
    rim_halo(True, face, corner, phase_halo, solute_halo)


def near_halo(face, corner):
    _, _, size_y, size_z = face.shape
    slabs = jax.ShapeDtypeStruct((HALO, size_y + 2 * HALO, size_z), F32)
    return pl.pallas_call(
        near_kernel,
        out_shape=(slabs, slabs),
        in_specs=[vmem()] * 2,
        out_specs=[vmem()] * 2,
        compiler_params=pltpu.CompilerParams(vmem_limit_bytes=VMEM_LIMIT),
        cost_estimate=pl.CostEstimate(flops=15 * 10**8, bytes_accessed=15 * 10**6, transcendentals=0),
        name="near",
    )(face, corner)


def rim_kernel(
    coarse_y, size_x, face, corner, near_phase, near_solute, near_corner, fans, matrices, along_z, inner_latent, *rest
):
    kept = dict(zip(KEPT, rest[: len(KEPT)]))
    outs, (far_phase, far_solute, total, *scratch) = rest[len(KEPT) : len(KEPT) + 8], rest[len(KEPT) + 8 :]
    near_new, far_new, keep, send = outs[:3], outs[3:6], outs[6], outs[7]
    _, _, size_y, size_z = face.shape
    width = total.shape[1]
    rim_halo(False, face, corner, far_phase, far_solute)
    changes = []
    half = len(scratch) // 2
    near = near_phase, near_solute, edge_fan(near_corner, along_z, size_y)
    far = far_phase, far_solute, edge_fan(corner, along_z, size_y)
    sides = [
        rim_march(True, size_x, near, fans, matrices, kept, scratch[:half], *near_new, changes),
        rim_march(False, size_x, far, fans, matrices, kept, scratch[half:], *far_new, changes),
    ]
    while sides:
        sides = [side for side in sides if next(side, sides) is not sides]
    lanes = [coarse_lane(u, size_x, size_y, coarse_y) for u in (size_x // 4 - 1, 0)]
    total[...] = restrict(changes, lanes, size_y, size_z, width) + inner_latent[...]
    halve(total, lax.div(2 * lax.axis_index("gy"), lax.axis_size("gy")), keep, send)


def halve(total, side, keep, send):
    half = keep.shape[0]
    keep[...] = total[pl.ds(pl.multiple_of(side * half, half), half), :]
    send[...] = total[pl.ds(pl.multiple_of((1 - side) * half, half), half), :]


def rims(shape, face, corner, near, fans, matrices, along_z, inner_latent, kept, coarse_y):
    size_x, size_y, size_z = shape
    rows = size_y + 2 * HALO
    part = jax.ShapeDtypeStruct((HALO, size_y, size_z), F32)
    width = inner_latent.shape[1]
    half = jax.ShapeDtypeStruct((size_z // 8, width), F32)
    state = jax.ShapeDtypeStruct((HALO, rows, size_z), F32)
    slabs = lambda count: pltpu.VMEM((count, rows, size_z), F32)
    return pl.pallas_call(
        functools.partial(rim_kernel, coarse_y, size_x),
        out_shape=(state, state, part, state, state, part, half, half),
        in_specs=[vmem()] * (9 + len(kept)),
        out_specs=[vmem()] * 8,
        scratch_shapes=[
            slabs(HALO), slabs(HALO), pltpu.VMEM((size_z // 4, width), F32),
            *[slabs(count) for count in 2 * (4, 3, 3, 2, 4)],
        ],
        compiler_params=pltpu.CompilerParams(vmem_limit_bytes=VMEM_LIMIT),
        cost_estimate=pl.CostEstimate(flops=10**7, bytes_accessed=3 * 10**6, transcendentals=0),
        name="rims",
    )(face, corner, *near, fans, matrices, along_z, inner_latent, *kept)


def rim_solute(near, size_x, p1, c1, phase_new, matrices, kept, out):
    _, size_y, size_z = phase_new.shape
    span = spans(size_x)
    spot = rim_spot(near)
    own = {"p1": p1[...], "c1": c1[...], "cz1": along(c1[pl.ds(2, 2)], matrices[2])}

    def get(name, v):
        begin, _ = span[name]
        if v >= begin:
            return kept[name][(size_x - 1 - v if near else v) - begin]
        return own[name][v if name == "cz1" else v + 2]

    for v in range(HALO):
        conc = get("c1", v)
        change = phase_new[spot(v)] - get("p1", v)[:size_y]
        beyond = get("c1", v + 2)[:size_y] + get("c1", v - 2)[:size_y]
        out[spot(v)] = solute_step(
            conc[:size_y], beyond, next_row(conc)[:size_y], get("cz1", v)[:size_y], change
        )


def store_kernel(
    middle_phase, middle_solute, near_p1, near_c1, near_phase, far_p1, far_c1, far_phase, matrices, p1, c1, cz1,
    phase_out, solute_out, near_solute, far_solute, sems,
):
    size_x = phase_out.shape[0]
    odd_x = lax.rem(lax.axis_index("gx"), 2)
    near = (1 - odd_x) * (size_x - HALO)
    far = size_x - HALO - near
    put = lambda part, out, at: (part, out.at[pl.ds(at, part.shape[0])])
    copies = start_all(
        [
            put(middle_phase, phase_out, HALO), put(middle_solute, solute_out, HALO), put(near_phase, phase_out, near),
            put(far_phase, phase_out, far),
        ],
        sems,
    )
    kept = dict(p1=p1, c1=c1, cz1=cz1)
    rim_solute(True, size_x, near_p1, near_c1, near_phase, matrices, kept, near_solute)
    rim_solute(False, size_x, far_p1, far_c1, far_phase, matrices, kept, far_solute)
    copies += start_all(
        [put(near_solute, solute_out, near), put(far_solute, solute_out, far)], sems.at[pl.ds(4, 2)]
    )
    wait_all(copies)


def store(shape, middle, edges, matrices, kept):
    kept = dict(zip(KEPT, kept))
    out = jax.ShapeDtypeStruct(shape, F32)
    part = pltpu.VMEM((HALO, *shape[1:]), F32)
    return pl.pallas_call(
        store_kernel,
        out_shape=(out, out),
        in_specs=[vmem()] * 12,
        out_specs=[hbm()] * 2,
        scratch_shapes=[part, part, pltpu.SemaphoreType.DMA((6,))],
        compiler_params=pltpu.CompilerParams(vmem_limit_bytes=VMEM_LIMIT),
        cost_estimate=pl.CostEstimate(flops=0, bytes_accessed=4 * 10**6, transcendentals=0),
        name="store",
    )(*middle, *edges, matrices, kept["p1"], kept["c1"], kept["cz1"])


def merge_kernel(mine, arrived, keep, send, total):
    total[...] = mine[...] + arrived[...]
    halve(total, lax.rem(lax.axis_index("gy"), 2), keep, send)


def merge(mine, arrived):
    half = jax.ShapeDtypeStruct((mine.shape[0] // 2, mine.shape[1]), F32)
    return pl.pallas_call(
        merge_kernel,
        out_shape=(half, half),
        in_specs=[vmem()] * 2,
        out_specs=[vmem()] * 2,
        scratch_shapes=[pltpu.VMEM(mine.shape, F32)],
        compiler_params=pltpu.CompilerParams(vmem_limit_bytes=VMEM_LIMIT),
        cost_estimate=pl.CostEstimate(flops=10**4, bytes_accessed=10**5, transcendentals=0),
        name="merge",
    )(mine, arrived)


def owner_kernel(mine, arrived, out):
    total = mine[...] + arrived[...]
    coarse_x, _, coarse_y = out.shape
    for k in range(coarse_x):
        out[k] = total[:, k * coarse_y : (k + 1) * coarse_y]


def owner(mine, arrived, coarse_x, coarse_y):
    coarse_z = mine.shape[0]
    return pl.pallas_call(
        owner_kernel,
        out_shape=jax.ShapeDtypeStruct((coarse_x, coarse_z, coarse_y), F32),
        in_specs=[vmem()] * 2,
        out_specs=vmem(),
        compiler_params=pltpu.CompilerParams(vmem_limit_bytes=VMEM_LIMIT),
        cost_estimate=pl.CostEstimate(flops=10**4, bytes_accessed=10**5, transcendentals=0),
        name="owner",
    )(mine, arrived)


def body(phase, solute, macro_temp):
    count_x, count_y = lax.axis_size("gx"), lax.axis_size("gy")
    coarse_x, coarse_y, coarse_z = macro_temp.shape
    near_x, far_x = pairs(count_x, 0), pairs(count_x, 1)
    near_y, far_y = pairs(count_y, 0), pairs(count_y, 1)
    across = [(k, count_y - 1 - k) for k in range(count_y)]
    ride = count_y == 4
    macro = jnp.swapaxes(macro_temp, 1, 2)
    still = [pltpu.with_memory_space_constraint(v, pltpu.HBM) for v in (phase, solute, macro)]
    phase, solute, face_a, face_b, side_a, strip_b, rest_b, table = pack(*still, ride)
    coarse_shape = (coarse_z * count_y, coarse_x * coarse_y)
    face_a = lax.ppermute(face_a, "gx", near_x)
    side_a = lax.ppermute(side_a, "gy", near_y)
    if ride:
        strip_b = append(side_a, strip_b)
    else:
        table = lax.all_gather(table, "gy").reshape(coarse_shape)
    matrices, along_z = z_products(phase.shape[2], strip_b)
    face_b, rest_b, strip_b = lax.optimization_barrier((face_b, rest_b, strip_b))
    strip_b = lax.ppermute(strip_b, "gy", far_y)
    rest_b = lax.ppermute(rest_b, "gy", far_y)
    face_b = lax.ppermute(face_b, "gx", far_x)
    coarse, corner_a, corner_b = corners(side_a, strip_b, table, coarse_y, coarse_shape)
    corner_a = lax.ppermute(corner_a, "gx", near_x)
    corner_b = lax.ppermute(corner_b, "gx", far_x)
    results = inner(phase, solute, side_a, strip_b, rest_b, coarse, matrices, along_z, coarse_y)
    middle, inner_latent, fans, kept = results[:2], results[2], results[3], results[4:]
    near = (*near_halo(face_a, corner_a), corner_a)
    *edges, mine, send = rims(
        phase.shape, face_b, corner_b, near, fans, matrices, along_z, inner_latent, kept, coarse_y
    )
    phase_out, solute_out = store(phase.shape, middle, edges, matrices, kept)
    if ride:
        mine, send = merge(mine, lax.ppermute(send, "gy", across))
        latent = owner(mine, lax.ppermute(send, "gy", near_y), coarse_x, coarse_y)
    else:
        low = lax.axis_index("gy") < count_y // 2
        total = jnp.concatenate([jnp.where(low, mine, send), jnp.where(low, send, mine)])
        latent = lax.psum_scatter(total, "gy", scatter_dimension=0, tiled=True)
        latent = jnp.swapaxes(latent.reshape(coarse_z, coarse_x, coarse_y), 0, 1)
    latent = jnp.swapaxes(latent, 1, 2)
    return phase_out, solute_out, latent


def solution(mesh):
    in_specs = (P("gx", "gy", None), P("gx", "gy", None), P("gx", None, "gy"))
    out_specs = (P("gx", "gy", None), P("gx", "gy", None), P("gx", None, "gy"))
    return jax.shard_map(body, mesh=mesh, in_specs=in_specs, out_specs=out_specs, check_vma=False)
```

```python
import functools

import jax
import jax.numpy as jnp
from jax import lax
from jax.experimental import pallas as pl
from jax.experimental.pallas import tpu as pltpu
from jax.sharding import PartitionSpec as P

time_step = 0.1
anisotropy = 0.3
coupling = 2.0
rejection = 0.5

F32 = jnp.float32
HALO = 4
STRIP = 4
ROWS = 8
LANES = 128
VMEM_LIMIT = 24 * 1024 * 1024


def vmem():
    return pl.BlockSpec(memory_space=pltpu.VMEM)


def anywhere():
    return pl.BlockSpec(memory_space=pl.ANY)


def hbm():
    return pl.BlockSpec(memory_space=pltpu.HBM)


def pairs(count, first):
    forward = [((first + k) % count, (first + k + 1) % count) for k in range(0, count, 2)]
    return forward + [(b, a) for a, b in forward]


def flips(me):
    odd = lax.rem(me, 2)
    return me, me + 1 - 2 * odd, lax.rem(me + 2, 4), 3 - me


def halves(value):
    coarse = value.astype(jnp.bfloat16)
    return coarse, (value - coarse.astype(F32)).astype(jnp.bfloat16)


def product(left, right, contract):
    dot = lambda a, b: lax.dot_general(a, b, ((contract[:1], contract[1:]), ((), ())), preferred_element_type=F32)
    if left.dtype == jnp.bfloat16:
        parts = [dot(left, part) for part in halves(right)]
    else:
        parts = [dot(part, right) for part in halves(left)]
    return parts[0] + parts[1]


def row_ids(shape):
    return lax.broadcasted_iota(jnp.int32, shape, len(shape) - 2)


def lane_ids(shape):
    return lax.broadcasted_iota(jnp.int32, shape, len(shape) - 1)


def start_all(copies, sems):
    copies = [pltpu.make_async_copy(source, target, sems.at[n]) for n, (source, target) in enumerate(copies)]
    for copy in copies:
        copy.start()
    return copies


def wait_all(copies):
    for copy in copies:
        copy.wait()


def fold(table):
    half = table.shape[0] // 2
    return jnp.concatenate([table[:half], table[half:]], axis=1)


def unfold(tile):
    return jnp.concatenate([tile[:, :LANES], tile[:, LANES:]], axis=0)


def pack_kernel(
    phase, solute, macro, phase_here, solute_here, face_a, face_b, side_a, strip_b, rest_b, table, local, sems
):
    size_x, size_y, size_z = phase.shape
    odd_x = lax.rem(lax.axis_index("gx"), 2)
    even_y = lax.rem(lax.axis_index("gy"), 2) == 0
    copies = [(macro, local)]
    for ref, here in ((phase, phase_here), (solute, solute_here)):
        for at in range(0, size_x, HALO):
            copies.append((ref.at[pl.ds(at, HALO)], here.at[pl.ds(at, HALO)]))
    copies = start_all(copies, sems)
    half = 1 + size_x // HALO
    for field, (here, batch) in enumerate(((phase_here, copies[:half]), (solute_here, copies[half:]))):
        wait_all(batch)
        face_a[field] = here[pl.ds((1 - odd_x) * (size_x - HALO), HALO)]
        face_b[field] = here[pl.ds(odd_x * (size_x - HALO), HALO)]
        if field == 0:
            wide = jnp.concatenate([local[k] for k in range(local.shape[0])], axis=1)
            table[...] = wide
    low = [here[:, pl.ds(0, ROWS), :] for here in (phase_here, solute_here)]
    high = [here[:, pl.ds(size_y - ROWS, ROWS), :] for here in (phase_here, solute_here)]
    top = row_ids((size_x, ROWS, size_z)) < HALO
    low_side = jnp.where(top, low[0], pltpu.roll(low[1], HALO, 1))
    high_side = jnp.where(top, pltpu.roll(high[1], HALO, 1), high[0])
    side_a[pl.ds(0, size_x)] = jnp.where(even_y, high_side, low_side)
    side_b = jnp.where(even_y, low_side, high_side)
    strip_b[pl.ds(0, STRIP)] = side_b[:STRIP]
    strip_b[pl.ds(STRIP, STRIP)] = side_b[size_x - STRIP :]
    rest_b[...] = side_b[STRIP : size_x - STRIP]
    if side_a.shape[0] > size_x:
        side_a[size_x] = fold(wide)
        strip_b[2 * STRIP] = fold(wide)


def pack(phase, solute, macro, ride):
    size_x, size_y, size_z = phase.shape
    coarse_x, coarse_z, coarse_y = macro.shape
    field = jax.ShapeDtypeStruct(phase.shape, F32)
    face = jax.ShapeDtypeStruct((2, HALO, size_y, size_z), F32)
    counts = (size_x, 2 * STRIP, size_x - 2 * STRIP)
    extra = (1, 2, 0) if ride else (0, 0, 0)
    sides = [jax.ShapeDtypeStruct((count + more, ROWS, size_z), F32) for count, more in zip(counts, extra)]
    table = jax.ShapeDtypeStruct((coarse_z, coarse_x * coarse_y), F32)
    return pl.pallas_call(
        pack_kernel,
        out_shape=(field, field, face, face, *sides, table),
        in_specs=[hbm()] * 3,
        out_specs=[vmem()] * 8,
        scratch_shapes=[pltpu.VMEM(macro.shape, F32), pltpu.SemaphoreType.DMA((1 + 2 * (size_x // HALO),))],
        compiler_params=pltpu.CompilerParams(vmem_limit_bytes=VMEM_LIMIT),
        cost_estimate=pl.CostEstimate(flops=10**5, bytes_accessed=2 * 10**6, transcendentals=0),
        name="pack",
    )(phase, solute, macro)


def append_kernel(arrived, side, out):
    out[side.shape[0] - 1] = arrived[arrived.shape[0] - 1]


def append(arrived, side):
    return pl.pallas_call(
        append_kernel,
        out_shape=jax.ShapeDtypeStruct(side.shape, F32),
        in_specs=[vmem(), vmem()],
        out_specs=vmem(),
        input_output_aliases={1: 0},
        compiler_params=pltpu.CompilerParams(vmem_limit_bytes=VMEM_LIMIT),
        cost_estimate=pl.CostEstimate(flops=0, bytes_accessed=10**5, transcendentals=0),
        name="append",
    )(arrived, side)


def near_rows(block, coarse_y):
    shape = (2 * ROWS, coarse_y)
    wanted = lax.rem(row_ids(shape) + lax.axis_index("gy") * ROWS + coarse_y - 1, coarse_y)
    pick = (lane_ids(shape) == wanted).astype(F32).astype(jnp.bfloat16)
    return product(pick, block, (1, 1))


def pack_edge(rows):
    pieces = rows[:ROWS], pltpu.roll(rows[:ROWS], 4, 0), rows[ROWS:], pltpu.roll(rows[ROWS:], 4, 0)
    return jnp.concatenate(pieces, axis=1)


def unpack_edge(tile):
    quarter = tile.shape[1] // 4
    pieces = [tile[:, at : at + quarter] for at in range(0, tile.shape[1], quarter)]
    top = row_ids(pieces[0].shape) < 4
    halves = [jnp.where(top, pieces[n], pltpu.roll(pieces[n + 1], 4, 0)) for n in (0, 2)]
    return jnp.concatenate(halves, axis=0)


def corner_kernel(coarse_y, gathered, side_a, strip_b, table, coarse, corner_a, corner_b):
    size_x = side_a.shape[0] - (0 if gathered else 1)
    me = lax.axis_index("gy")
    even_x = lax.rem(lax.axis_index("gx"), 2) == 0
    even_y = lax.rem(me, 2) == 0
    block = table[...]
    if not gathered:
        near, across, far = flips(me)[1:]
        depth = table.shape[0]
        tiles = (me, block), (near, unfold(side_a[size_x])), (far, unfold(strip_b[2 * STRIP])), (across, unfold(strip_b[2 * STRIP + 1]))
        for source, tile in tiles:
            coarse[pl.ds(pl.multiple_of(source * depth, depth), depth), :] = tile
        block = coarse[...]
    depth, width = block.shape
    flipped = [block[:, at : at + coarse_y] for at in range(width - coarse_y, -1, -coarse_y)]
    block = jnp.where(even_x, block, jnp.concatenate(flipped, axis=1))
    coarse[...] = block
    row = row_ids(side_a.shape[1:])
    edges = block[:, width - coarse_y :], block[:, :coarse_y]
    for corner, top_side, edge in ((corner_a, even_x, edges[0]), (corner_b, jnp.logical_not(even_x), edges[1])):

        def layer(d, high):
            first = side_a[jnp.where(top_side, size_x - d, d - 1)]
            second = strip_b[jnp.where(top_side, 2 * STRIP - d, d - 1)]
            return jnp.where(even_y, first, second) if high else jnp.where(even_y, second, first)

        spare = pack_edge(near_rows(edge, coarse_y))
        tile = jnp.where(row == 4, pltpu.roll(layer(3, False), 5, 0), layer(1, False))
        corner[0] = jnp.where(row < 2, spare, tile)
        tile = jnp.where(row == 3, pltpu.roll(layer(3, True), 3, 0), layer(1, True))
        corner[1] = jnp.where(row >= 6, pltpu.roll(spare, 4, 0), tile)
        corner[2] = jnp.where(row % 4 < 2, layer(2, True), layer(2, False))


def corners(side_a, strip_b, table, coarse_y, coarse_shape):
    size_z = side_a.shape[2]
    corner = jax.ShapeDtypeStruct((3, ROWS, size_z), F32)
    coarse = jax.ShapeDtypeStruct(coarse_shape, F32)
    return pl.pallas_call(
        functools.partial(corner_kernel, coarse_y, table.shape == coarse_shape),
        out_shape=(coarse, corner, corner),
        in_specs=[vmem()] * 3,
        out_specs=[vmem()] * 3,
        compiler_params=pltpu.CompilerParams(vmem_limit_bytes=VMEM_LIMIT),
        cost_estimate=pl.CostEstimate(flops=10**5, bytes_accessed=4 * 10**5, transcendentals=0),
        name="corners",
    )(side_a, strip_b, table)


def weights(ends, frac, tick):
    first, second = ends
    return jnp.where(tick == first, 1.0 - frac, 0.0) + jnp.where(tick == second, frac, 0.0)


def weights_z(depth, size_z):
    shape = (depth, size_z)
    fine = lane_ids(shape)
    lower = (2 * fine + 5) // 8 - 1
    frac = (2 * fine - 3 - 8 * lower).astype(F32) / 8.0
    ends = jnp.clip(lower, 0, depth - 1), jnp.clip(lower + 1, 0, depth - 1)
    return weights(ends, frac, row_ids(shape))


def interpolate(rows, along_z, size_y):
    deep = product(rows, along_z, (1, 0))
    shape = (size_y + 2 * HALO, 2 * ROWS)
    fine = row_ids(shape)
    fine = jnp.where(fine >= size_y + HALO, fine - shape[0], fine)
    lower = (2 * fine + 13) // 8 - 2
    frac = (2 * fine - 3 - 8 * lower).astype(F32) / 8.0
    along_y = weights((lower + 1, lower + 2), frac, lane_ids(shape)).astype(jnp.bfloat16)
    return [
        product(along_y, deep[at : at + 2 * ROWS], (1, 0))
        for at in range(0, rows.shape[0], 2 * ROWS)
    ]


def blend(x, fans):
    lower = (2 * x - 3) // 8
    frac = (2 * x - 3 - 8 * lower) / 8.0
    return (1.0 - frac) * fans[lower] + frac * fans[lower + 1]


def turn(value, by, axis):
    return pltpu.roll(value, by % value.shape[axis], axis)


def z_matrices(size_z):
    shape = (size_z, size_z)
    source, target = row_ids(shape), lane_ids(shape)
    hit = lambda at: (source == at).astype(F32)
    end = size_z - 1
    gradient = hit(jnp.minimum(target + 1, end)) - hit(jnp.maximum(target - 1, 0))
    difference = hit(target + 1) - hit(target - 1)
    laplace = hit(jnp.minimum(target + 2, end)) + hit(jnp.maximum(target - 2, 0)) - 6.0 * hit(target)
    return tuple(m.astype(jnp.bfloat16) for m in (gradient, difference, laplace))


def matrix_kernel(size_z, tile, out, along_z):
    for n, matrix in enumerate(z_matrices(size_z)):
        out[n] = matrix
    along_z[...] = weights_z(*along_z.shape).astype(jnp.bfloat16)


def z_products(size_z, tile):
    square = jax.ShapeDtypeStruct((3, size_z, size_z), jnp.bfloat16)
    return pl.pallas_call(
        functools.partial(matrix_kernel, size_z),
        out_shape=(square, jax.ShapeDtypeStruct((size_z // 4, size_z), jnp.bfloat16)),
        in_specs=[anywhere()],
        out_specs=[vmem()] * 2,
        compiler_params=pltpu.CompilerParams(vmem_limit_bytes=VMEM_LIMIT),
        cost_estimate=pl.CostEstimate(flops=10**6, bytes_accessed=4 * 10**5, transcendentals=0),
        name="products",
    )(tile)


def along(slabs, matrix):
    return product(slabs.reshape(-1, slabs.shape[-1]), matrix, (1, 0)).reshape(slabs.shape)


def z_difference(value, clamp):
    first, second = value[:, :LANES], value[:, LANES:]
    lane = lane_ids(first.shape)
    head, tail = lane == 0, lane == LANES - 1
    ends = (first, second) if clamp else (0.0, 0.0)
    ahead = turn(first, -1, 1), turn(second, -1, 1)
    behind = turn(first, 1, 1), turn(second, 1, 1)
    low = jnp.where(tail, ahead[1], ahead[0]) - jnp.where(head, ends[0], behind[0])
    high = jnp.where(tail, ends[1], ahead[1]) - jnp.where(head, behind[0], behind[1])
    return jnp.concatenate([low, high], axis=1)


def flux(before, here, after, along_z):
    along_x = after - before
    along_y = turn(here, -1, 0) - turn(here, 1, 0)
    sq_x = along_x * along_x
    sq_y = along_y * along_y
    both = sq_x + sq_y
    inverse = 1.0 / (both + 4.0)
    factor = 1.0 + anisotropy * (both * both - 8.0 * (sq_x * sq_y)) * (inverse * inverse)
    stiff = (0.25 * time_step) * (factor * factor)
    return stiff * along_x, stiff * along_y, stiff * along_z


def spread(flux_y):
    return turn(flux_y, -1, 0) - turn(flux_y, 1, 0)


def phase_change(here, conc, theta, divergence):
    square = 1.0 - here * here
    drive = square * (here - (coupling * square) * (theta + conc))
    return divergence + time_step * drive


def solute_step(conc, beyond_x, beyond_y, along_z, change):
    return conc + (0.25 * time_step) * (beyond_x + beyond_y + along_z) + rejection * change


def next_row(conc):
    return turn(conc, -2, 0) + turn(conc, 2, 0)


def restrict(changes, lanes, size_y, size_z, coarse_width):
    shape = (size_z, size_z // 4)
    pool_z = (row_ids(shape) // 4 == lane_ids(shape)).astype(F32).astype(jnp.bfloat16)
    shape = (size_y, coarse_width)
    cell, lane = row_ids(shape) // 4, lane_ids(shape)
    pool_y = [jnp.where(cell + at == lane, 0.5 / 64.0, 0.0).astype(jnp.bfloat16) for at in lanes]
    parts = jnp.concatenate(halves(jnp.concatenate(changes, axis=0)), axis=1)
    pooled = jnp.dot(parts, jnp.concatenate([pool_z, pool_z], axis=0), preferred_element_type=F32)
    parts = jnp.concatenate(halves(pooled), axis=0)
    return lax.dot_general(
        parts, jnp.concatenate(pool_y + pool_y, axis=0), (((0,), (0,)), ((), ())), preferred_element_type=F32
    )


def coarse_lane(u, size_x, size_y, coarse_y):
    last = size_x // 4 - 1
    x = u + lax.rem(lax.axis_index("gx"), 2) * (last - 2 * u)
    return x * coarse_y + lax.axis_index("gy") * (size_y // 4)


KEPT = ("p0", "c0", "dz0", "cz0", "gx0", "dv0", "p1", "c1", "dz1", "cz1", "gx1", "dv1", "th")


def spans(size_x):
    widths = dict(p0=0, c0=0, dz0=0, cz0=0, gx0=1, dv0=1, p1=2, c1=2, dz1=2, cz1=2, gx1=3, dv1=3, th=2)
    return {name: (widths[name], size_x - widths[name]) for name in KEPT}


def halo_rows(tile, top):
    zero = jnp.zeros_like(tile[0])
    low = tile[0], tile[2], pltpu.roll(tile[0], 3, 0), zero
    high = tile[1], tile[2], pltpu.roll(tile[1], 5, 0), zero
    return [
        (jnp.where(top, h, l), pltpu.roll(jnp.where(top, l, h), HALO, 0)) for l, h in zip(low, high)
    ]


def inner_kernel(
    coarse_y, phase, solute, side_a, strip_b, rest_b, coarse, matrices, along_z, phase_new, solute_new, latent, ends, *rest
):
    kept = dict(zip(KEPT, rest[: len(KEPT)]))
    (fz,) = rest[len(KEPT) :]
    size_x, size_y, size_z = phase.shape
    span = spans(size_x)
    odd_x = lax.rem(lax.axis_index("gx"), 2)
    even_y = lax.rem(lax.axis_index("gy"), 2) == 0
    at = lambda name, u: kept[name].at[u - span[name][0]]
    get = lambda name, u: kept[name][u - span[name][0]]
    place = lambda u: u + odd_x * (size_x - 1 - 2 * u)
    top = row_ids((ROWS, size_z)) < HALO
    for u in range(size_x):
        first = side_a[place(u)]
        if STRIP <= u < size_x - STRIP:
            second = rest_b[place(u) - STRIP]
        else:
            at_strip = u if u < STRIP else u - size_x + 2 * STRIP
            second = strip_b[at_strip + odd_x * (2 * STRIP - 1 - 2 * at_strip)]
        low, high = jnp.where(even_y, second, first), jnp.where(even_y, first, second)
        at("p0", u)[pl.ds(0, size_y), :] = phase[place(u)]
        at("c0", u)[pl.ds(0, size_y), :] = solute[place(u)]
        at("p0", u)[pl.ds(size_y, ROWS), :] = jnp.where(top, high, low)
        at("c0", u)[pl.ds(size_y, ROWS), :] = pltpu.roll(jnp.where(top, low, high), HALO, 0)
    block = coarse[...]
    block = [near_rows(block[:, at : at + coarse_y], coarse_y) for at in range(0, block.shape[1], coarse_y)]
    fans = dict(enumerate(interpolate(jnp.concatenate(block, axis=0), along_z[...], size_y)))
    ends[0], ends[1] = fans[0], fans[len(fans) - 1]
    for u in range(*span["th"]):
        at("th", u)[...] = blend(u, fans)

    for step in "01":
        p, c, dz, cz, gx, dv = (name + step for name in ("p", "c", "dz", "cz", "gx", "dv"))
        for u in range(*span[dz]):
            at(dz, u)[...] = z_difference(get(p, u), True)
        kept[cz][...] = along(kept[c][...], matrices[2])
        begin, end = span[gx]
        for u in range(begin, end):
            flux_x, flux_y, flux_z = flux(get(p, u - 1), get(p, u), get(p, u + 1), get(dz, u))
            at(gx, u)[...] = flux_x
            at(dv, u)[...] = spread(flux_y) + z_difference(flux_z, False)
        take = (lambda v: v) if step == "0" else (lambda v: v[:size_y])
        for u in range(begin + 1, end - 1):
            here, conc = take(get(p, u)), get(c, u)
            divergence = take(get(gx, u + 1)) - take(get(gx, u - 1)) + take(get(dv, u))
            change = phase_change(here, take(conc), take(get("th", u)), divergence)
            beyond = take(get(c, u + 2)) + take(get(c, u - 2))
            new_conc = solute_step(take(conc), beyond, take(next_row(conc)), take(get(cz, u)), change)
            if step == "0":
                at("p1", u)[...] = here + change
                at("c1", u)[...] = new_conc
            else:
                phase_new[place(u) - HALO] = here + change
                solute_new[place(u) - HALO] = new_conc
    changes, lanes = [], []
    for k in range(1, size_x // 4 - 1):
        change = jnp.zeros((size_y, size_z), F32)
        for u in range(4 * k, 4 * k + 4):
            change = change + (phase_new[place(u) - HALO] - get("p0", u)[:size_y])
        changes.append(change)
        lanes.append(coarse_lane(k, size_x, size_y, coarse_y))
    latent[...] = restrict(changes, lanes, size_y, size_z, latent.shape[1])


def inner(phase, solute, side_a, strip_b, rest_b, coarse, matrices, along_z, coarse_y):
    size_x, size_y, size_z = phase.shape
    rows = size_y + 2 * HALO
    part = jax.ShapeDtypeStruct((size_x - 2 * HALO, size_y, size_z), F32)
    kept = [jax.ShapeDtypeStruct((end - begin, rows, size_z), F32) for begin, end in spans(size_x).values()]
    latent = jax.ShapeDtypeStruct((size_z // 4, coarse.shape[1]), F32)
    return pl.pallas_call(
        functools.partial(inner_kernel, coarse_y),
        out_shape=(part, part, latent, jax.ShapeDtypeStruct((2, rows, size_z), F32), *kept),
        in_specs=[vmem()] * 8,
        out_specs=[vmem()] * (4 + len(kept)),
        scratch_shapes=[pltpu.VMEM((size_x - 2, rows, size_z), F32)],
        compiler_params=pltpu.CompilerParams(vmem_limit_bytes=VMEM_LIMIT),
        cost_estimate=pl.CostEstimate(flops=5 * 10**8, bytes_accessed=5 * 10**6, transcendentals=0),
        name="inner",
    )(phase, solute, side_a, strip_b, rest_b, coarse, matrices, along_z)


def rim_halo(near, face, corner, phase_halo, solute_halo):
    _, _, size_y, size_z = face.shape
    odd_x = lax.rem(lax.axis_index("gx"), 2)
    flip = odd_x if near else 1 - odd_x
    top = row_ids((ROWS, size_z)) < HALO
    for d, (p_rows, c_rows) in enumerate(halo_rows(corner, top)):
        layer = d + flip * (HALO - 1 - 2 * d)
        for n, (field, rows) in enumerate(((phase_halo, p_rows), (solute_halo, c_rows))):
            field[HALO - 1 - d, pl.ds(0, size_y), :] = face[n, layer]
            field[HALO - 1 - d, pl.ds(size_y, ROWS), :] = rows


def edge_fan(corner, along_z, size_y):
    edge = jnp.where(row_ids(corner.shape[1:]) < 2, corner[0], pltpu.roll(corner[1], 4, 0))
    return interpolate(unpack_edge(edge), along_z[...], size_y)[0]


def rim_spot(near):
    odd_x = lax.rem(lax.axis_index("gx"), 2)
    flip = odd_x if near else 1 - odd_x
    return lambda v: v + (1 - flip) * (HALO - 1 - 2 * v)


def rim_march(near, size_x, halo, fans, matrices, kept, scratch, p1, c1, phase_new, result):
    hp0, hc0, fan = halo
    gx, dv, dz, cz, th = scratch
    _, size_y, size_z = phase_new.shape
    span = spans(size_x)
    spot = rim_spot(near)

    def get(name, v):
        begin, end = span[name]
        if v >= begin:
            found = kept[name][(size_x - 1 - v if near else v) - begin]
            return -found if near and name.startswith("gx") else found
        own, first = dict(
            p0=(hp0, -4), c0=(hc0, -4), dz0=(dz, -3), cz0=(cz, -2), gx0=(gx, -3), dv0=(dv, -2),
            p1=(p1, -2), c1=(c1, -2), dz1=(dz, -1), gx1=(gx, -1), dv1=(dv, 0), th=(th, -2),
        )[name]
        return own[v - first]

    moved = []
    ends = {-1: fan, 0: fans[1 if near else 0]}
    for v in range(-2, 2):
        th[v + 2] = blend(v, ends)
    for step, begin in (("0", -3), ("1", -1)):
        p, c, gx_, dv_, dz_, cz_ = (name + step for name in ("p", "c", "gx", "dv", "dz", "cz"))
        for n in range(3):
            dz[n] = z_difference((hp0 if step == "0" else p1)[n + 1], True)
        if step == "0":
            cz[...] = along(hc0[pl.ds(2, 2)], matrices[2])
        yield
        for v in range(begin, begin + 4):
            flux_x, flux_y, flux_z = flux(get(p, v - 1), get(p, v), get(p, v + 1), get(dz_, v))
            gx[v - begin] = flux_x
            if v > begin:
                dv[v - begin - 1] = spread(flux_y) + z_difference(flux_z, False)
        yield
        take = (lambda w: w) if step == "0" else (lambda w: w[:size_y])
        for v in range(begin + 1, begin + 5):
            here, conc = take(get(p, v)), get(c, v)
            divergence = take(get(gx_, v + 1)) - take(get(gx_, v - 1)) + take(get(dv_, v))
            change = phase_change(here, take(conc), take(get("th", v)), divergence)
            if step == "0":
                beyond = get(c, v + 2) + get(c, v - 2)
                p1[v + 2] = here + change
                c1[v + 2] = solute_step(conc, beyond, next_row(conc), get(cz_, v), change)
            else:
                phase_new[spot(v)] = here + change
                moved.append(here + change - get("p0", v)[:size_y])
        yield
    result.append((moved[0] + moved[1]) + (moved[2] + moved[3]))


def near_kernel(face, corner, phase_halo, solute_halo):
    rim_halo(True, face, corner, phase_halo, solute_halo)


def near_halo(face, corner):
    _, _, size_y, size_z = face.shape
    slabs = jax.ShapeDtypeStruct((HALO, size_y + 2 * HALO, size_z), F32)
    return pl.pallas_call(
        near_kernel,
        out_shape=(slabs, slabs),
        in_specs=[vmem()] * 2,
        out_specs=[vmem()] * 2,
        compiler_params=pltpu.CompilerParams(vmem_limit_bytes=VMEM_LIMIT),
        cost_estimate=pl.CostEstimate(flops=15 * 10**8, bytes_accessed=15 * 10**6, transcendentals=0),
        name="near",
    )(face, corner)


def rim_kernel(
    coarse_y, size_x, face, corner, near_phase, near_solute, near_corner, fans, matrices, along_z, inner_latent, *rest
):
    kept = dict(zip(KEPT, rest[: len(KEPT)]))
    outs, (far_phase, far_solute, total, *scratch) = rest[len(KEPT) : len(KEPT) + 8], rest[len(KEPT) + 8 :]
    near_new, far_new, keep, send = outs[:3], outs[3:6], outs[6], outs[7]
    _, _, size_y, size_z = face.shape
    width = total.shape[1]
    rim_halo(False, face, corner, far_phase, far_solute)
    changes = []
    half = len(scratch) // 2
    near = near_phase, near_solute, edge_fan(near_corner, along_z, size_y)
    far = far_phase, far_solute, edge_fan(corner, along_z, size_y)
    sides = [
        rim_march(True, size_x, near, fans, matrices, kept, scratch[:half], *near_new, changes),
        rim_march(False, size_x, far, fans, matrices, kept, scratch[half:], *far_new, changes),
    ]
    while sides:
        sides = [side for side in sides if next(side, sides) is not sides]
    lanes = [coarse_lane(u, size_x, size_y, coarse_y) for u in (size_x // 4 - 1, 0)]
    total[...] = restrict(changes, lanes, size_y, size_z, width) + inner_latent[...]
    halve(total, lax.div(2 * lax.axis_index("gy"), lax.axis_size("gy")), keep, send)


def halve(total, side, keep, send):
    half = keep.shape[0]
    keep[...] = total[pl.ds(pl.multiple_of(side * half, half), half), :]
    send[...] = total[pl.ds(pl.multiple_of((1 - side) * half, half), half), :]


def rims(shape, face, corner, near, fans, matrices, along_z, inner_latent, kept, coarse_y):
    size_x, size_y, size_z = shape
    rows = size_y + 2 * HALO
    part = jax.ShapeDtypeStruct((HALO, size_y, size_z), F32)
    width = inner_latent.shape[1]
    half = jax.ShapeDtypeStruct((size_z // 8, width), F32)
    state = jax.ShapeDtypeStruct((HALO, rows, size_z), F32)
    slabs = lambda count: pltpu.VMEM((count, rows, size_z), F32)
    return pl.pallas_call(
        functools.partial(rim_kernel, coarse_y, size_x),
        out_shape=(state, state, part, state, state, part, half, half),
        in_specs=[vmem()] * (9 + len(kept)),
        out_specs=[vmem()] * 8,
        scratch_shapes=[
            slabs(HALO), slabs(HALO), pltpu.VMEM((size_z // 4, width), F32),
            *[slabs(count) for count in 2 * (4, 3, 3, 2, 4)],
        ],
        compiler_params=pltpu.CompilerParams(vmem_limit_bytes=VMEM_LIMIT),
        cost_estimate=pl.CostEstimate(flops=10**7, bytes_accessed=3 * 10**6, transcendentals=0),
        name="rims",
    )(face, corner, *near, fans, matrices, along_z, inner_latent, *kept)


def rim_solute(near, size_x, p1, c1, phase_new, matrices, kept, out):
    _, size_y, size_z = phase_new.shape
    span = spans(size_x)
    spot = rim_spot(near)
    own = {"p1": p1[...], "c1": c1[...], "cz1": along(c1[pl.ds(2, 2)], matrices[2])}

    def get(name, v):
        begin, _ = span[name]
        if v >= begin:
            return kept[name][(size_x - 1 - v if near else v) - begin]
        return own[name][v if name == "cz1" else v + 2]

    for v in range(HALO):
        conc = get("c1", v)
        change = phase_new[spot(v)] - get("p1", v)[:size_y]
        beyond = get("c1", v + 2)[:size_y] + get("c1", v - 2)[:size_y]
        out[spot(v)] = solute_step(
            conc[:size_y], beyond, next_row(conc)[:size_y], get("cz1", v)[:size_y], change
        )


def store_kernel(
    middle_phase, middle_solute, near_p1, near_c1, near_phase, far_p1, far_c1, far_phase, matrices, p1, c1, cz1,
    phase_out, solute_out, near_solute, far_solute, sems,
):
    size_x = phase_out.shape[0]
    odd_x = lax.rem(lax.axis_index("gx"), 2)
    near = (1 - odd_x) * (size_x - HALO)
    far = size_x - HALO - near
    put = lambda part, out, at: (part, out.at[pl.ds(at, part.shape[0])])
    copies = start_all(
        [
            put(middle_phase, phase_out, HALO), put(middle_solute, solute_out, HALO), put(near_phase, phase_out, near),
            put(far_phase, phase_out, far),
        ],
        sems,
    )
    kept = dict(p1=p1, c1=c1, cz1=cz1)
    rim_solute(True, size_x, near_p1, near_c1, near_phase, matrices, kept, near_solute)
    rim_solute(False, size_x, far_p1, far_c1, far_phase, matrices, kept, far_solute)
    copies += start_all(
        [put(near_solute, solute_out, near), put(far_solute, solute_out, far)], sems.at[pl.ds(4, 2)]
    )
    wait_all(copies)


def store(shape, middle, edges, matrices, kept):
    kept = dict(zip(KEPT, kept))
    out = jax.ShapeDtypeStruct(shape, F32)
    part = pltpu.VMEM((HALO, *shape[1:]), F32)
    return pl.pallas_call(
        store_kernel,
        out_shape=(out, out),
        in_specs=[vmem()] * 12,
        out_specs=[hbm()] * 2,
        scratch_shapes=[part, part, pltpu.SemaphoreType.DMA((6,))],
        compiler_params=pltpu.CompilerParams(vmem_limit_bytes=VMEM_LIMIT),
        cost_estimate=pl.CostEstimate(flops=0, bytes_accessed=4 * 10**6, transcendentals=0),
        name="store",
    )(*middle, *edges, matrices, kept["p1"], kept["c1"], kept["cz1"])


def merge_kernel(mine, arrived, keep, send, total):
    total[...] = mine[...] + arrived[...]
    halve(total, lax.rem(lax.axis_index("gy"), 2), keep, send)


def merge(mine, arrived):
    half = jax.ShapeDtypeStruct((mine.shape[0] // 2, mine.shape[1]), F32)
    return pl.pallas_call(
        merge_kernel,
        out_shape=(half, half),
        in_specs=[vmem()] * 2,
        out_specs=[vmem()] * 2,
        scratch_shapes=[pltpu.VMEM(mine.shape, F32)],
        compiler_params=pltpu.CompilerParams(vmem_limit_bytes=VMEM_LIMIT),
        cost_estimate=pl.CostEstimate(flops=10**4, bytes_accessed=10**5, transcendentals=0),
        name="merge",
    )(mine, arrived)


def owner_kernel(mine, arrived, out):
    total = mine[...] + arrived[...]
    coarse_x, _, coarse_y = out.shape
    for k in range(coarse_x):
        out[k] = total[:, k * coarse_y : (k + 1) * coarse_y]


def owner(mine, arrived, coarse_x, coarse_y):
    coarse_z = mine.shape[0]
    return pl.pallas_call(
        owner_kernel,
        out_shape=jax.ShapeDtypeStruct((coarse_x, coarse_z, coarse_y), F32),
        in_specs=[vmem()] * 2,
        out_specs=vmem(),
        compiler_params=pltpu.CompilerParams(vmem_limit_bytes=VMEM_LIMIT),
        cost_estimate=pl.CostEstimate(flops=10**4, bytes_accessed=10**5, transcendentals=0),
        name="owner",
    )(mine, arrived)


def body(phase, solute, macro_temp):
    count_x, count_y = lax.axis_size("gx"), lax.axis_size("gy")
    coarse_x, coarse_y, coarse_z = macro_temp.shape
    near_x, far_x = pairs(count_x, 0), pairs(count_x, 1)
    near_y, far_y = pairs(count_y, 0), pairs(count_y, 1)
    across = [(k, count_y - 1 - k) for k in range(count_y)]
    ride = count_y == 4
    macro = jnp.swapaxes(macro_temp, 1, 2)
    still = [pltpu.with_memory_space_constraint(v, pltpu.HBM) for v in (phase, solute, macro)]
    phase, solute, face_a, face_b, side_a, strip_b, rest_b, table = pack(*still, ride)
    coarse_shape = (coarse_z * count_y, coarse_x * coarse_y)
    face_a = lax.ppermute(face_a, "gx", near_x)
    side_a = lax.ppermute(side_a, "gy", near_y)
    if ride:
        strip_b = append(side_a, strip_b)
    else:
        table = lax.all_gather(table, "gy").reshape(coarse_shape)
    matrices, along_z = z_products(phase.shape[2], strip_b)
    face_b, rest_b, strip_b = lax.optimization_barrier((face_b, rest_b, strip_b))
    strip_b = lax.ppermute(strip_b, "gy", far_y)
    rest_b = lax.ppermute(rest_b, "gy", far_y)
    face_b = lax.ppermute(face_b, "gx", far_x)
    coarse, corner_a, corner_b = corners(side_a, strip_b, table, coarse_y, coarse_shape)
    corner_a = lax.ppermute(corner_a, "gx", near_x)
    corner_b = lax.ppermute(corner_b, "gx", far_x)
    results = inner(phase, solute, side_a, strip_b, rest_b, coarse, matrices, along_z, coarse_y)
    middle, inner_latent, fans, kept = results[:2], results[2], results[3], results[4:]
    near = (*near_halo(face_a, corner_a), corner_a)
    *edges, mine, send = rims(
        phase.shape, face_b, corner_b, near, fans, matrices, along_z, inner_latent, kept, coarse_y
    )
    phase_out, solute_out = store(phase.shape, middle, edges, matrices, kept)
    if ride:
        mine, send = merge(mine, lax.ppermute(send, "gy", across))
        latent = owner(mine, lax.ppermute(send, "gy", near_y), coarse_x, coarse_y)
    else:
        low = lax.axis_index("gy") < count_y // 2
        total = jnp.concatenate([jnp.where(low, mine, send), jnp.where(low, send, mine)])
        latent = lax.psum_scatter(total, "gy", scatter_dimension=0, tiled=True)
        latent = jnp.swapaxes(latent.reshape(coarse_z, coarse_x, coarse_y), 0, 1)
    latent = jnp.swapaxes(latent, 1, 2)
    return phase_out, solute_out, latent


def solution(mesh):
    in_specs = (P("gx", "gy", None), P("gx", "gy", None), P("gx", None, "gy"))
    out_specs = (P("gx", "gy", None), P("gx", "gy", None), P("gx", None, "gy"))
    return jax.shard_map(body, mesh=mesh, in_specs=in_specs, out_specs=out_specs, check_vma=False)
```
